32 devices in a mesh: cells: 16 (over z, y, x), members: 2 (over core).
Axes of the slice: x: 2, y: 2, z: 4, core: 2. Of those that a mesh axis runs over, the one named last changes fastest.
Arguments:
- ensemble: float32 [64, 4, 16384], P('members', None, 'cells')
- speed: float32 [16384], P('cells'), may hold values from 0.1 to 0.85
- direction: int32 [16384], P('cells'), may hold values 0 or 1
- couple: float32 [4, 4], replicated, may hold values from -0.25 to 0.25
- obs_place: int32 [4096], P('cells'), may hold values from 0 to 1023
- obs_field: int32 [4096], P('cells'), may hold values from 0 to 3
- obs_value: float32 [4096], P('cells'), may hold values from -8 to 8
- obs_sigma: float32 [4096], P('cells'), may hold values from 0.5 to 5
- send_count: int32 [16, 16], P('cells'), may hold values from 0 to 32, as said below
Outputs:
- analysis: float32 [64, 4, 16384], P('members', None, 'cells')
- innovation: float32 [4096], P('cells')
The draws below stay inside these ranges and needn't reach their ends.
Inputs may be any that keep to these rules, and one draw needn't show every extreme that they name: Each row of send_count sums to 256; no entry exceeds 32; in every row four blocks get exactly 32, and one block gets exactly 32 from every row.
All inputs are finite; a program needn't handle non-finite values. No bound on the sum of `direction` on one device may be relied on, other than what follows from the above.
Results may differ from the reference program's by a relative error of at most 0.0001.
Values sent between devices are 32-bit elements; how exact they have to be, the bound alone decides.
No kernel may reach another device: no remote copies, remote signals or barrier semaphores. Data moves between devices by JAX's collectives and lax.ppermute only.
A program may use at most 64 MiB of HBM per device.

```python
import math
import jax
import jax.numpy as jnp
from jax import lax

F = 4
K = 64
STEPS = 4
CELLS_DEV = 1024
OBS_DEV = 256
CAP = 32
OWNERS = 16
NC = 16384
NOBS = 4096


def draw_ensemble(key, part):
    key_noise, key_rough, key_center = jax.random.split(key, 3)
    position = jnp.arange(NC, dtype=jnp.float32) / NC
    rising = jnp.exp(jnp.log(3.0) * position)
    center = jax.random.normal(key_center, (1, F, NC), jnp.float32)
    roughness = jnp.exp(jax.random.uniform(key_rough, (1, F, NC), jnp.float32, -0.7, 0.7))
    noise_draw = jnp.clip(jax.random.normal(key_noise, (K, F, NC), jnp.float32), -4.0, 4.0)
    return center + rising * roughness * noise_draw


def draw_send_count(key, part):
    base_key = jax.random.fold_in(key, 11)
    key_hot, key_pick, key_spread = jax.random.split(base_key, 3)
    hottest = jax.random.permutation(key_hot, OWNERS)[:8]
    pick_keys = jax.random.split(key_pick, OWNERS)
    picked = jax.vmap(lambda single_key: jax.random.permutation(single_key, 7)[:3] + 1)(pick_keys)
    chosen = jnp.concatenate([jnp.broadcast_to(hottest[:1], (OWNERS, 1)), hottest[picked]], axis=1)
    owner_ids = jnp.arange(OWNERS, dtype=jnp.int32)
    is_hot = jnp.any(owner_ids[None, :, None] == chosen[:, None, :], axis=2).astype(jnp.int32)
    ordering = jnp.argsort(is_hot * OWNERS + owner_ids[None, :], axis=1)
    spare_rows = OBS_DEV - 4 * CAP
    other_owners = OWNERS - 4
    spread_keys = jax.random.split(key_spread, OWNERS)

    def spread_row(single_key):
        slot_owner = jax.random.permutation(single_key, other_owners * CAP)[:spare_rows] // CAP
        return jnp.sum((slot_owner[:, None] == jnp.arange(other_owners, dtype=jnp.int32)[None, :]).astype(jnp.int32), axis=0)
    loads = jax.vmap(spread_row)(spread_keys).astype(jnp.int32)
    in_order = jnp.concatenate([loads, jnp.full((OWNERS, 4), CAP, jnp.int32)], axis=1)
    row_ids = jnp.broadcast_to(owner_ids[:, None], (OWNERS, OWNERS))
    return jnp.zeros((OWNERS, OWNERS), jnp.int32).at[row_ids, ordering].set(in_order)


def with_ends(entries, key, smallest, high):
    extent = entries.shape
    spot = [jax.random.randint(jax.random.fold_in(key, axis), (), 0, extent[axis]) for axis in range(len(extent))]
    entries = entries.at[tuple(spot)].set(smallest)
    longest = extent.index(max(extent))
    spot[longest] = (spot[longest] + 1) % extent[longest]
    return entries.at[tuple(spot)].set(high)


def block_scale(rng, dims, cuts, low, top_value):
    def one(axis_at, blocks):
        steps = jax.random.uniform(jax.random.fold_in(jax.random.fold_in(rng, 6), axis_at), (blocks,), jnp.float32, low / len(cuts), top_value / len(cuts))
        return jnp.repeat(jnp.exp(steps), dims[axis_at] // blocks).reshape((-1,) + (1,) * (len(dims) - axis_at - 1))

    loudness = one(*cuts[0])
    for cut in cuts[1:]:
        loudness = loudness * one(*cut)
    return loudness


def noise(key, extent, deviation, limit, pieces=(), kind=jnp.bfloat16):
    array = deviation * jax.random.normal(key, extent, jnp.float32)
    if pieces:
        array = array * block_scale(key, extent, pieces, -0.22, 0.18)
    return jnp.clip(array, -limit, limit).astype(kind)


def setup_inputs(seed: int = 0) -> dict:
    streams_of = jax.random.split(jax.random.key(seed), 10)
    ensemble = draw_ensemble(jax.random.fold_in(streams_of[9], 71), 0)
    speed = jnp.clip(jnp.exp(math.log(0.85) - 2.1400662 * jax.random.uniform(streams_of[1], (NC,), jnp.float32) ** block_scale(streams_of[1], (NC,), ((0, 16),), -0.2, 0.2)), 0.1, 0.85)
    direction = with_ends((jax.random.randint(streams_of[2], (NC,), 0, 2) < 1).astype(jnp.int32), jax.random.fold_in(streams_of[2], 1), 0, 1)
    couple = jnp.clip(jax.random.uniform(streams_of[3], (F, F), jnp.float32, -0.25, 0.25), -0.25, 0.25)
    obs_place = with_ends(jax.random.randint(streams_of[4], (NOBS,), 0, CELLS_DEV), jax.random.fold_in(streams_of[4], 1), 0, CELLS_DEV - 1).astype(jnp.int32)
    obs_field = with_ends(jax.random.randint(streams_of[5], (NOBS,), 0, F), jax.random.fold_in(streams_of[5], 1), 0, F - 1).astype(jnp.int32)
    obs_value = noise(streams_of[6], (NOBS,), 2.0, 8.0, ((0, 16),), jnp.float32)
    obs_sigma = jnp.clip(jnp.exp(math.log(5.0) - 2.3025851 * jax.random.uniform(streams_of[7], (NOBS,), jnp.float32) ** block_scale(streams_of[7], (NOBS,), ((0, 16),), -0.2, 0.2)), 0.5, 5.0)
    send_count = draw_send_count(jax.random.fold_in(streams_of[9], 71), 0)
    return dict(ensemble=ensemble, speed=speed, direction=direction, couple=couple, obs_place=obs_place, obs_field=obs_field, obs_value=obs_value, obs_sigma=obs_sigma, send_count=send_count)


DIFFUSION = 0.05

def advance(states, speed, toward_left, toward_right, couple):
    padded = jnp.pad(states, ((0, 0), (0, 0), (1, 1)))
    left_cells = padded[:, :, :-2]
    right_cells = padded[:, :, 2:]
    advanced = states + toward_left * left_cells + toward_right * right_cells - speed * states + DIFFUSION * (left_cells - 2.0 * states + right_cells)
    return advanced + jnp.einsum('fg,kgc->kfc', couple, advanced, precision=lax.Precision.HIGHEST)

def mixing_matrix(upper_factor, carried, members):
    mean_weights = jax.scipy.linalg.solve_triangular(upper_factor, carried, lower=False)
    identity = jnp.eye(members, dtype=jnp.float32)
    spread = math.sqrt(members - 1.0) * jax.scipy.linalg.solve_triangular(upper_factor, identity, lower=False)
    centering = identity - 1.0 / members
    shifted = jnp.dot(centering, mean_weights, precision=lax.Precision.HIGHEST)
    inner = jnp.dot(jnp.dot(centering, spread, precision=lax.Precision.HIGHEST), centering, precision=lax.Precision.HIGHEST)
    return 1.0 / members + shifted[:, None] + inner

def reference(ensemble, speed, direction, couple, obs_place, obs_field, obs_value, obs_sigma, send_count):
    flag_values = direction.astype(jnp.float32)
    toward_left = speed * flag_values
    toward_right = speed - toward_left
    states = ensemble
    for step_index in range(STEPS):
        states = advance(states, speed, toward_left, toward_right, couple)
    owner_ends = jnp.cumsum(send_count, axis=1)
    slot_ids = jnp.arange(OBS_DEV, dtype=jnp.int32)
    owner_of = lax.optimization_barrier(jnp.sum((owner_ends[:, :, None] <= slot_ids[None, None, :]).astype(jnp.int32), axis=1))
    global_cell = owner_of.reshape(-1) * CELLS_DEV + obs_place
    flat_states = states.reshape(K, F * NC)
    picked = jnp.take(flat_states, obs_field * NC + global_cell, axis=1)
    center = lax.optimization_barrier(jnp.mean(picked, axis=0))
    scaled_anomaly = (picked - center) / obs_sigma
    innovation = (obs_value - center) / obs_sigma
    gram = jnp.dot(scaled_anomaly, scaled_anomaly.T, precision=lax.Precision.HIGHEST) + (K - 1.0) * jnp.eye(K, dtype=jnp.float32)
    cross = jnp.dot(scaled_anomaly, innovation, precision=lax.Precision.HIGHEST)
    lower_factor = jnp.linalg.cholesky(gram)
    carried = jax.scipy.linalg.solve_triangular(lower_factor, cross, lower=True)
    mixing = mixing_matrix(lower_factor.T, carried, K)
    analysis = jnp.einsum('kj,kfc->jfc', mixing, states, precision=lax.Precision.HIGHEST)
    return (analysis, innovation)
```

```python
import functools
import math

import jax
import jax.numpy as jnp
from jax import lax
from jax.experimental import pallas as pl
from jax.experimental.pallas import tpu as pltpu
from jax.sharding import PartitionSpec as P

STEPS = 4
DIFFUSION = 0.05
LANES = 128
BOTH = ("cells", "members")
EXACT = lax.Precision.HIGHEST
VMEM_BYTES = 48 * 1024 * 1024


def core_pairs(owners, place):
    pairs = []
    for block in range(owners):
        for core in range(2):
            to_block, to_core = place(block, core)
            pairs.append((block * 2 + core, to_block * 2 + to_core))
    return pairs


def stage_units(owners):
    units = []
    unit = 1
    while unit < owners:
        radix = 4 if unit * 4 <= owners else 2
        units.append((unit, radix))
        unit *= radix
    return units


def swap_cores(x, owners):
    return lax.ppermute(x, BOTH, core_pairs(owners, lambda block, core: (block, 1 - core)))


def exchange(x, owners, unit, radix):
    if radix == 2:
        return (lax.ppermute(x, BOTH, core_pairs(owners, lambda block, core: (block ^ unit, core))),)
    first = lax.ppermute(
        x, BOTH, core_pairs(owners, lambda block, core: (block ^ (unit * (1 + core)), core))
    )
    third = lax.ppermute(x, BOTH, core_pairs(owners, lambda block, core: (block ^ (unit * 3), core)))
    return first, swap_cores(first, owners), third


def stage_slot(units, block, target, core):
    distance = jnp.bitwise_xor(block, target)
    side = core
    place = jnp.zeros_like(target)
    for unit, radix in reversed(units):
        digit = lax.rem(lax.div(distance, jnp.int32(unit)), jnp.int32(radix))
        if radix == 4:
            middle = (digit == 1) | (digit == 2)
            own_side = digit == 1 + side
            slot = jnp.where(middle, jnp.where(own_side, 1, 2), digit)
            side = jnp.where(middle & ~own_side, 1 - side, side)
        else:
            slot = digit
        place = place + slot * unit
    return place


def pack_kernel(
    send_ref, mine_head, mine_tail, other_head, other_tail, speed_ref, flag_ref, place_ref, field_ref,
    value_ref, sigma_ref, which_ref, out_ref, *, cells, fields, rows,
):
    own_core = which_ref[1]
    members = mine_head.shape[0]
    for own, head, tail in ((True, mine_head, mine_tail), (False, other_head, other_tail)):
        head_rows = jnp.concatenate([head[:, f, :] for f in range(fields)], axis=0)
        tail_rows = jnp.concatenate([tail[:, f, :] for f in range(fields)], axis=0)
        first = jnp.transpose(head_rows)[:STEPS, :]
        last = jnp.transpose(tail_rows)[LANES - STEPS :, :]
        strip = jnp.concatenate([first, last], axis=0)
        core = own_core if own else 1 - own_core
        out_ref[pl.ds(pl.multiple_of(core * 8, 8), 8), :] = strip
    slots = (
        lax.broadcasted_iota(jnp.int32, (rows, LANES), 0) * LANES
        + lax.broadcasted_iota(jnp.int32, (rows, LANES), 1)
    )
    owner = jnp.zeros((rows, LANES), jnp.int32)
    end = jnp.int32(0)
    for d in range(send_ref.shape[1]):
        end = end + send_ref[0, d]
        owner = owner + jnp.where(slots >= end, 1, 0)
    ids = (owner * fields + field_ref[...]) * cells + place_ref[...]
    weight = 1.0 / (sigma_ref[...] * sigma_ref[...])
    base = 16
    out_ref[base : base + rows, :] = ids.astype(jnp.float32)
    out_ref[base + rows : base + 2 * rows, :] = weight
    out_ref[base + 2 * rows : base + 3 * rows, :] = weight * value_ref[...]
    tiles = speed_ref.shape[0]
    lane = lax.broadcasted_iota(jnp.int32, (1, LANES), 1)
    toward_left = speed_ref[...] * flag_ref[...].astype(jnp.float32)
    toward_right = speed_ref[...] - toward_left
    low = lane < LANES // 2
    base = base + 3 * rows
    out_ref[base : base + 1, :] = jnp.where(low, toward_left[:1], toward_left[tiles - 1 :])
    out_ref[base + 1 : base + 2, :] = jnp.where(low, toward_right[:1], toward_right[tiles - 1 :])


def pieces_of(x):
    high = x.astype(jnp.bfloat16).astype(jnp.float32)
    rest = x - high
    middle = rest.astype(jnp.bfloat16).astype(jnp.float32)
    return high, middle, rest - middle


def forecast_kernel(
    which_ref, couple_ref, mine_ref, other_ref, speed_ref, flag_ref, *refs, owners, parts, block_rows, obs_rows,
):
    gathered = refs[:parts]
    state_ref, sums_ref, halo_ref, work_ref, all_ref, mean_ref, onehot_ref, spread_ref, weighted_ref, plain_ref, found_ref = refs[parts:]
    block, core = which_ref[0], which_ref[1]
    left_slot = which_ref[2 + jnp.maximum(block - 1, 0)]
    right_slot = which_ref[2 + jnp.minimum(block + 1, owners - 1)]
    members, fields, cells = mine_ref.shape
    tiles = cells // LANES
    total = 2 * members
    places = fields * tiles
    part_rows = gathered[0].shape[0]
    for p in range(parts):
        all_ref[p * part_rows : (p + 1) * part_rows, :] = gathered[p][...]
    left_at = pl.multiple_of(left_slot * block_rows, 8)
    right_at = pl.multiple_of(right_slot * block_rows, 8)
    has_left = (block > 0).astype(jnp.float32)
    has_right = (block < owners - 1).astype(jnp.float32)
    sub = lax.broadcasted_iota(jnp.int32, (8, LANES), 0)
    lane = lax.broadcasted_iota(jnp.int32, (1, LANES), 1)

    strip_rows = fields * members
    for half in range(2):
        left = all_ref[pl.ds(left_at + 8 * half, 8), :]
        right = all_ref[pl.ds(right_at + 8 * half, 8), :]
        top = jnp.where(sub < STEPS, right * has_right, 0.0)
        bottom = jnp.where(sub >= 8 - STEPS, left * has_left, 0.0)
        tile = jnp.concatenate(
            [top, jnp.zeros((LANES - 16, LANES), jnp.float32), bottom], axis=0
        )
        halo_ref[half * strip_rows : (half + 1) * strip_rows, :] = jnp.transpose(tile)
    coef_at = block_rows - 8
    left_coef = all_ref[pl.ds(left_at + coef_at, 8), :]
    right_coef = all_ref[pl.ds(right_at + coef_at, 8), :]
    low = lane < LANES // 2
    inside = jnp.where(low, has_right, has_left)
    row = 16 + 3 * obs_rows - coef_at
    halo_left = jnp.where(low, right_coef[row : row + 1], left_coef[row : row + 1])
    halo_right = jnp.where(low, right_coef[row + 1 : row + 2], left_coef[row + 1 : row + 2])
    speed = speed_ref[...]
    toward_left = speed * flag_ref[...].astype(jnp.float32)
    toward_right = speed - toward_left
    from_left = [toward_left[t : t + 1] + DIFFUSION for t in range(tiles)]
    from_right = [toward_right[t : t + 1] + DIFFUSION for t in range(tiles)]
    stay = [1.0 - 2.0 * DIFFUSION - speed[t : t + 1] for t in range(tiles)]
    from_left.append((halo_left + DIFFUSION) * inside)
    from_right.append((halo_right + DIFFUSION) * inside)
    stay.append((1.0 - 2.0 * DIFFUSION - halo_left - halo_right) * inside)

    def wide(parts_of):
        return jnp.broadcast_to(jnp.concatenate(parts_of, axis=1), (8, LANES * (tiles + 1)))

    from_left, from_right, stay = wide(from_left), wide(from_right), wide(stay)
    width = LANES * (tiles + 1)

    mix = [[couple_ref[f, g] + (1.0 if f == g else 0.0) for g in range(fields)] for f in range(fields)]
    for _ in range(2):
        mix = [
            [sum(mix[f][h] * mix[h][g] for h in range(fields)) for g in range(fields)]
            for f in range(fields)
        ]

    mean_ref[...] = jnp.zeros_like(mean_ref)
    for half_of, source in ((core, mine_ref), (1 - core, other_ref)):

        def group(i, _, half_of=half_of, source=source):
            at = pl.multiple_of(i * 8, 8)
            for f in range(fields):
                halo_at = pl.multiple_of(half_of * strip_rows + f * members + at, 8)
                x = jnp.concatenate(
                    [source[pl.ds(at, 8), f, :], halo_ref[pl.ds(halo_at, 8), :]], axis=1
                )
                for _ in range(STEPS):
                    x = (
                        from_left * pltpu.roll(x, 1, 1)
                        + stay * x
                        + from_right * pltpu.roll(x, width - 1, 1)
                    )
                work_ref[f * 8 : (f + 1) * 8, :] = x[:, :cells]
            into = pl.multiple_of(half_of * members + at, 8)
            for t in range(tiles):
                lanes = slice(t * LANES, (t + 1) * LANES)
                moved = [work_ref[f * 8 : (f + 1) * 8, lanes] for f in range(fields)]
                for f in range(fields):
                    value = sum(mix[f][g] * moved[g] for g in range(fields))
                    state_ref[pl.ds(f * total + into, 8), lanes] = value
                    at_mean = (f * tiles + t) * 8
                    mean_ref[at_mean : at_mean + 8, :] += value
            return 0

        lax.fori_loop(0, members // 8, group, 0)

    mean = jnp.concatenate(
        [jnp.sum(mean_ref[p * 8 : (p + 1) * 8, :], axis=0, keepdims=True) for p in range(places)],
        axis=0,
    ) * (1.0 / total)

    place_ids = lax.broadcasted_iota(jnp.int32, (places, LANES), 0)
    lane_ids = lax.broadcasted_iota(jnp.int32, (LANES, LANES), 0)
    start = block * (fields * cells)

    def spread(i, _):
        at = i * block_rows + 16
        rows = all_ref[pl.ds(pl.multiple_of(at, 8), 8), :]
        for r in range(obs_rows):
            local = rows[r : r + 1].astype(jnp.int32) - start
            hit = place_ids == lax.shift_right_arithmetic(local, 7)
            onehot = (lane_ids == jnp.bitwise_and(local, LANES - 1)).astype(jnp.float32)
            lanes = pl.ds(pl.multiple_of((i * obs_rows + r) * LANES, LANES), LANES)
            onehot_ref[:, lanes] = onehot.astype(jnp.bfloat16)
            weight = rows[obs_rows + r : obs_rows + r + 1]
            pull = rows[2 * obs_rows + r : 2 * obs_rows + r + 1]
            stack = [jnp.where(hit, piece, 0.0) for piece in pieces_of(weight) + pieces_of(pull)]
            spread_ref[:, lanes] = jnp.concatenate(stack, axis=0).astype(jnp.bfloat16)
        return 0

    lax.fori_loop(0, owners, spread, 0)
    placed = lax.dot_general(
        spread_ref[...], onehot_ref[...], (((1,), (1,)), ((), ())), preferred_element_type=jnp.float32
    )
    placed = [placed[p * places : (p + 1) * places] for p in range(6)]
    weight = placed[0] + placed[1] + placed[2]
    pull = placed[3] + placed[4] + placed[5] - weight * mean

    for f in range(fields):
        for t in range(tiles):
            at = f * tiles + t
            lanes = slice(t * LANES, (t + 1) * LANES)
            into = slice(at * LANES, (at + 1) * LANES)
            anomaly = state_ref[f * total : (f + 1) * total, lanes] - mean[at : at + 1]
            plain_ref[:, into] = anomaly
            weighted_ref[:total, into] = anomaly * weight[at : at + 1]
            weighted_ref[total : total + 8, into] = jnp.where(sub == 0, pull[at : at + 1], 0.0)
    gram = lax.dot_general(
        weighted_ref[...], plain_ref[...], (((1,), (1,)), ((), ())),
        precision=EXACT, preferred_element_type=jnp.float32,
    )
    gram = jnp.concatenate([gram, jnp.zeros((total + 8, LANES - total), jnp.float32)], axis=1)
    sums_ref[:members, :] = gram[:members] + pltpu.roll(gram[members:total], total, 1)
    sums_ref[members : members + 8, :] = gram[total:]

    found = lax.dot_general(
        jnp.concatenate(pieces_of(mean), axis=0).astype(jnp.bfloat16), onehot_ref[...],
        (((1,), (0,)), ((), ())), preferred_element_type=jnp.float32,
    )
    found_ref[...] = found[:places] + found[places : 2 * places] + found[2 * places :]
    for i in range(owners):
        slot = which_ref[2 + i]
        rows = all_ref[pl.ds(pl.multiple_of(slot * block_rows + 16, 8), 8), :]
        for r in range(obs_rows):
            local = rows[r : r + 1].astype(jnp.int32) - start
            hit = place_ids == lax.shift_right_arithmetic(local, 7)
            lanes = pl.ds(pl.multiple_of((slot * obs_rows + r) * LANES, LANES), LANES)
            into = members + 8 + i * obs_rows + r
            sums_ref[into : into + 1, :] = jnp.sum(
                jnp.where(hit, found_ref[:, lanes], 0.0), axis=0, keepdims=True
            )


def spread_row(row):
    return jnp.broadcast_to(row, (8, LANES))


def eliminate(rows):
    count = len(rows)
    rows = list(rows)
    sub = lax.broadcasted_iota(jnp.int32, (8, LANES), 0)
    for b in range(count):
        columns = [
            [jnp.broadcast_to(rows[i][:, 8 * b + k : 8 * b + k + 1], (8, LANES)) for k in range(8)]
            for i in range(b, count)
        ]
        for j in range(8):
            scale = lax.rsqrt(spread_row(columns[0][j][j : j + 1, :]))
            upper = spread_row(rows[b][j : j + 1, :]) * scale
            lower = columns[0][j] * scale
            factors = [spread_row(lower[k : k + 1, :]) for k in range(8)]
            for i in range(b, count):
                here = lower if i == b else columns[i - b][j] * scale
                if i == b:
                    rows[b] = jnp.where(sub == j, upper, rows[b] - jnp.where(sub > j, here, 0.0) * upper)
                else:
                    rows[i] = rows[i] - here * upper
                for k in range(j + 1, 8):
                    columns[i - b][k] = columns[i - b][k] - here * factors[k]
    return rows


def analysis_kernel(which_ref, state_ref, value_ref, sigma_ref, *refs, parts, obs_rows):
    pieces = refs[:parts]
    analysis_ref, innovation_ref, mixing_ref, center_ref = refs[parts:]
    block, core = which_ref[0], which_ref[1]
    members, fields, cells = analysis_ref.shape
    total = 2 * members
    if parts == 4:
        sums = (pieces[0][...] + pieces[3][...]) + (pieces[1][...] + pieces[2][...])
    else:
        sums = pieces[0][...] + pieces[1][...]
    center_ref[...] = sums[members + 8 :]
    lane = lax.broadcasted_iota(jnp.int32, (8, LANES), 1)
    sub = lax.broadcasted_iota(jnp.int32, (8, LANES), 0)
    shifted = pltpu.roll(sums[:members], LANES - total, 1)
    rows = []
    for b in range(total // 8):
        at = 8 * b
        source = sums[at : at + 8] if at < members else shifted[at - members : at - members + 8]
        own = jnp.where(lane == sub + at, total - 1.0, 0.0)
        unit = jnp.where(lane == sub + at + total, 1.0, 0.0)
        rows.append(jnp.where(lane < total, source + own, unit))
    rows = eliminate(rows)
    cross = sums[members : members + 1]
    inverse = [jnp.where(lane < total, pltpu.roll(r, LANES - total, 1), 0.0) for r in rows]
    carried = [jnp.sum(r * cross, axis=1, keepdims=True) for r in inverse]
    weights = sum(jnp.sum(r * c, axis=0, keepdims=True) for r, c in zip(inverse, carried))
    row_means = [jnp.sum(r, axis=1, keepdims=True) * (1.0 / total) for r in inverse]
    column_mean = sum(jnp.sum(r, axis=0, keepdims=True) for r in inverse) * (1.0 / total)
    grand = jnp.sum(column_mean, axis=1, keepdims=True) * (1.0 / total)
    weights = weights - jnp.sum(weights, axis=1, keepdims=True) * (1.0 / total)
    root = math.sqrt(total - 1.0)
    add = weights + 1.0 / total - root * (column_mean - grand)
    for b in range(total // 8):
        mixing_ref[8 * b : 8 * b + 8, :] = root * (inverse[b] - row_means[b]) + add
    own_rows = mixing_ref[pl.ds(pl.multiple_of(core * members, 8), members), :][:, :total]
    for f in range(fields):
        analysis_ref[:, f, :] = jnp.dot(
            own_rows, state_ref[f * total : (f + 1) * total, :],
            precision=EXACT, preferred_element_type=jnp.float32,
        )
    for r in range(obs_rows):
        center = center_ref[pl.ds(block * obs_rows + r, 1), :]
        innovation_ref[r : r + 1, :] = (value_ref[r : r + 1, :] - center) / sigma_ref[r : r + 1, :]


def shards(
    ensemble, speed, direction, couple, obs_place, obs_field, obs_value, obs_sigma, send_count
):
    members, fields, cells = ensemble.shape
    owners = lax.axis_size("cells")
    total = members * lax.axis_size("members")
    obs = obs_place.shape[0]
    obs_rows = obs // LANES
    tiles = cells // LANES
    places = fields * tiles
    units = stage_units(owners)
    block = lax.axis_index("cells").astype(jnp.int32)
    core = lax.axis_index("members").astype(jnp.int32)
    slots = stage_slot(units, block, jnp.arange(owners, dtype=jnp.int32), core)
    which = jnp.concatenate([jnp.stack([block, core]), slots])
    speed = speed.reshape(tiles, LANES)
    direction = direction.reshape(tiles, LANES)
    obs_place, obs_field, obs_value, obs_sigma = (
        x.reshape(obs_rows, LANES) for x in (obs_place, obs_field, obs_value, obs_sigma)
    )
    whole = pl.BlockSpec(memory_space=pltpu.VMEM)
    scalars = pl.BlockSpec(memory_space=pltpu.SMEM)
    params = pltpu.CompilerParams(vmem_limit_bytes=VMEM_BYTES)

    other = swap_cores(ensemble, owners)

    block_rows = -(-(16 + 3 * obs_rows + 2) // 8) * 8
    head = pl.BlockSpec((members, fields, LANES), lambda i: (0, 0, 0))
    tail = pl.BlockSpec((members, fields, LANES), lambda i: (0, 0, tiles - 1))
    flat = lambda x: pl.BlockSpec(x.shape, lambda i: (0, 0))
    packed = pl.pallas_call(
        functools.partial(pack_kernel, cells=cells, fields=fields, rows=obs_rows),
        out_shape=jax.ShapeDtypeStruct((block_rows, LANES), jnp.float32),
        grid=(1,),
        in_specs=[scalars, head, tail, head, tail]
        + [flat(x) for x in (speed, direction, obs_place, obs_field, obs_value, obs_sigma)]
        + [scalars],
        out_specs=pl.BlockSpec((block_rows, LANES), lambda i: (0, 0)),
        compiler_params=params,
        name="pack",
    )(
        send_count, ensemble, ensemble, other, other, speed, direction, obs_place, obs_field,
        obs_value, obs_sigma, which,
    )

    pieces = (packed,)
    for unit, radix in units:
        packed = jnp.concatenate(pieces, axis=0) if len(pieces) > 1 else pieces[0]
        pieces = (packed,) + exchange(packed, owners, unit, radix)

    sums_rows = members + 8 + owners * obs_rows
    all_obs = owners * obs
    states, sums = pl.pallas_call(
        functools.partial(
            forecast_kernel, owners=owners, parts=len(pieces), block_rows=block_rows, obs_rows=obs_rows
        ),
        out_shape=(
            jax.ShapeDtypeStruct((fields * total, cells), jnp.float32),
            jax.ShapeDtypeStruct((sums_rows, LANES), jnp.float32),
        ),
        in_specs=[scalars, scalars] + [whole] * (4 + len(pieces)),
        out_specs=(whole, whole),
        scratch_shapes=[
            pltpu.VMEM((2 * fields * members, LANES), jnp.float32),
            pltpu.VMEM((fields * 8, cells), jnp.float32),
            pltpu.VMEM((owners * block_rows, LANES), jnp.float32),
            pltpu.VMEM((places * 8, LANES), jnp.float32),
            pltpu.VMEM((LANES, all_obs), jnp.bfloat16),
            pltpu.VMEM((6 * places, all_obs), jnp.bfloat16),
            pltpu.VMEM((total + 8, fields * cells), jnp.float32),
            pltpu.VMEM((total, fields * cells), jnp.float32),
            pltpu.VMEM((places, all_obs), jnp.float32),
        ],
        compiler_params=params,
        name="forecast",
    )(which, couple, ensemble, other, speed, direction, *pieces)

    pieces = (sums,)
    for unit, radix in units:
        if len(pieces) == 4:
            sums = (pieces[0] + pieces[3]) + (pieces[1] + pieces[2])
        elif len(pieces) == 2:
            sums = pieces[0] + pieces[1]
        pieces = (sums,) + exchange(sums, owners, unit, radix)

    analysis, innovation = pl.pallas_call(
        functools.partial(analysis_kernel, parts=len(pieces), obs_rows=obs_rows),
        out_shape=(
            jax.ShapeDtypeStruct((members, fields, cells), jnp.float32),
            jax.ShapeDtypeStruct((obs_rows, LANES), jnp.float32),
        ),
        in_specs=[scalars] + [whole] * (3 + len(pieces)),
        out_specs=(whole, whole),
        scratch_shapes=[
            pltpu.VMEM((total, LANES), jnp.float32),
            pltpu.VMEM((owners * obs_rows, LANES), jnp.float32),
        ],
        compiler_params=params,
        name="analysis",
    )(which, states, obs_value, obs_sigma, *pieces)
    return (analysis, innovation.reshape(obs))


def solution(mesh):
    return jax.shard_map(
        shards,
        mesh=mesh,
        in_specs=(
            P("members", None, "cells"),
            P("cells"),
            P("cells"),
            P(),
            P("cells"),
            P("cells"),
            P("cells"),
            P("cells"),
            P("cells", None),
        ),
        out_specs=(P("members", None, "cells"), P("cells")),
        check_vma=False,
    )
```

```python
import functools
import math

import jax
import jax.numpy as jnp
from jax import lax
from jax.experimental import pallas as pl
from jax.experimental.pallas import tpu as pltpu
from jax.sharding import PartitionSpec as P

STEPS = 4
DIFFUSION = 0.05
LANES = 128
CAP = 32
GROUPS = LANES // CAP
BOTH = ("cells", "members")
EXACT = lax.Precision.HIGHEST
VMEM_BYTES = 48 * 1024 * 1024


def core_pairs(owners, place):
    pairs = []
    for block in range(owners):
        for core in range(2):
            to_block, to_core = place(block, core)
            pairs.append((block * 2 + core, to_block * 2 + to_core))
    return pairs


def stage_units(owners):
    units = []
    unit = 1
    while unit < owners:
        units.append(unit)
        unit *= 4
    if unit != owners or len(units) < 2:
        raise ValueError("blocks not 4**n")
    return units


def swap_cores(x, owners):
    return lax.ppermute(x, BOTH, core_pairs(owners, lambda block, core: (block, 1 - core)))


def exchange(to_middle, to_third, owners, unit):
    first = lax.ppermute(
        to_middle, BOTH, core_pairs(owners, lambda block, core: (block ^ (unit * (1 + core)), core))
    )
    third = lax.ppermute(
        to_third, BOTH, core_pairs(owners, lambda block, core: (block ^ (unit * 3), core))
    )
    return first, swap_cores(first, owners), third


def digit_of(block, unit):
    return jnp.bitwise_and(lax.div(block, jnp.int32(unit)), 3)


def table_row(number, count):
    return (number % 4) * (count // 4) + number // 4


def pack_kernel(
    send_in, ensemble_ref, speed_in, flag_in, place_in, field_in, value_in, sigma_in,
    strip_ref, table_ref, send_ref, head, tail, speed_ref, flag_ref, place_ref, field_ref, value_ref,
    sigma_ref, sems, *, rows,
):
    fields, cells = ensemble_ref.shape[1:]
    small = (
        (send_in, send_ref), (speed_in, speed_ref), (flag_in, flag_ref), (place_in, place_ref),
        (field_in, field_ref), (value_in, value_ref), (sigma_in, sigma_ref),
    )
    large = (
        (ensemble_ref.at[:, :, pl.ds(0, LANES)], head),
        (ensemble_ref.at[:, :, pl.ds(cells - LANES, LANES)], tail),
    )
    copies = [
        pltpu.make_async_copy(source, target, sems.at[i])
        for i, (source, target) in enumerate(large + small)
    ]
    for copy in copies:
        copy.start()
    for copy in copies[2:]:
        copy.wait()
    tiles = speed_ref.shape[0]
    lane = lax.broadcasted_iota(jnp.int32, (1, LANES), 1)
    low = lane < LANES // 2
    toward_left = speed_ref[...] * flag_ref[...].astype(jnp.float32)
    toward_right = speed_ref[...] - toward_left
    edge_left = jnp.where(low, toward_left[:1], toward_left[tiles - 1 :])
    edge_right = jnp.where(low, toward_right[:1], toward_right[tiles - 1 :])
    ids = (field_ref[...] * cells + place_ref[...]).astype(jnp.float32)
    weight = 1.0 / (sigma_ref[...] * sigma_ref[...])
    pull = weight * value_ref[...]
    wide = rows * LANES

    def row_of(x):
        return jnp.concatenate([x[r : r + 1] for r in range(rows)], axis=1)

    listed = jnp.concatenate(
        [row_of(ids), row_of(weight), row_of(pull), jnp.zeros((5, wide), jnp.float32)], axis=0
    )
    sub = lax.broadcasted_iota(jnp.int32, (8, LANES), 0)
    lane8 = lax.broadcasted_iota(jnp.int32, (8, LANES), 1)
    empty = jnp.where(sub == 0, -1.0, 0.0)
    empty = jnp.where(sub == 3, edge_left, jnp.where(sub == 4, edge_right, empty))
    owners = send_ref.shape[1]
    count = owners // GROUPS
    for r in range(count):
        table_ref[8 * table_row(r, count) : 8 * table_row(r, count) + 8, :] = empty
    start = jnp.int32(0)
    for owner in range(owners):
        held = send_ref[0, owner]
        group, r = owner // count, owner % count
        moved = pltpu.roll(listed, lax.rem(group * CAP - start + 2 * wide, jnp.int32(wide)), 1)[:, :LANES]
        here = (lane8 >= group * CAP) & (lane8 < group * CAP + held) & (sub < 3)
        row = 8 * table_row(r, count)
        table_ref[row : row + 8, :] = jnp.where(here, moved, table_ref[row : row + 8, :])
        start = start + held
    for copy in copies[:2]:
        copy.wait()
    head_rows = jnp.concatenate([head[:, f, :] for f in range(fields)], axis=0)
    tail_rows = jnp.concatenate([tail[:, f, :] for f in range(fields)], axis=0)
    strip_ref[:STEPS, :] = jnp.transpose(head_rows)[:STEPS, :]
    strip_ref[STEPS:, :] = jnp.transpose(tail_rows)[LANES - STEPS :, :]


def incoming(digit, core, first, swapped, third):
    sub = lax.broadcasted_iota(jnp.int32, (8, LANES), 0)
    low = lax.broadcasted_iota(jnp.int32, (8, LANES), 1) < LANES // 2
    odd = jnp.bitwise_and(digit, 1) == 1
    result = []
    for part, other_part in ((0, 1), (1, 0), (2, 2)):
        near = jnp.where(
            core == 0, first[8 * part : 8 * part + 8, :], swapped[8 * other_part : 8 * other_part + 8, :]
        )
        far = third[8 * part : 8 * part + 8, :]
        from_right = jnp.where(odd, far, near)
        from_left = jnp.where(odd, near, far)
        result.append(jnp.where(sub < STEPS if part < 2 else low, from_right, from_left))
    return result


def regroup_kernel(
    which_ref, kept, first, swapped, third, _, to_middle, to_third, stay, *, unit, into_lanes,
):
    block, core = which_ref[0], which_ref[1]
    digit = digit_of(block, unit)
    after = digit_of(block, unit * 4)
    own, other, coefs = incoming(digit, core, first, swapped, third)
    sub = lax.broadcasted_iota(jnp.int32, (8, LANES), 0)
    lane_group = lax.broadcasted_iota(jnp.int32, (8, LANES), 1) // CAP
    held = (third.shape[0] - 16) // 8
    for target, partner in ((to_middle, 1 + core), (to_third, 3), (stay, 0)):
        wanted = jnp.bitwise_xor(after, partner)
        base = 0
        if target is not stay:
            target[0:8, :] = own
            target[8:16, :] = other
            base = 16

        def received(k, at):
            if k == 0:
                return kept[pl.ds(at, 8), :]
            if k == 3:
                return third[pl.ds(16 + at, 8), :]
            a, b = first[pl.ds(16 + at, 8), :], swapped[pl.ds(16 + at, 8), :]
            return jnp.where(core == k - 1, a, b)

        if into_lanes:
            for j in range(held):
                merged = coefs
                for k in range(4):
                    moved = pltpu.roll(
                        received(k, 8 * j), jnp.bitwise_and(k - wanted, 3) * CAP, 1
                    )
                    merged = jnp.where((lane_group == k) & (sub < 3), moved, merged)
                target[base + 8 * j : base + 8 * j + 8, :] = merged
        else:
            rest = held // 4
            for k in range(4):
                for r in range(rest):
                    at = pl.multiple_of((wanted * rest + r) * 8, 8)
                    row = base + 8 * (r * 4 + k)
                    target[row : row + 8, :] = jnp.where(sub < 3, received(k, at), coefs)


def power_of_coupling(couple_ref, fields):
    mix = [[couple_ref[f, g] + (1.0 if f == g else 0.0) for g in range(fields)] for f in range(fields)]
    for _ in range(2):
        mix = [
            [sum(mix[f][h] * mix[h][g] for h in range(fields)) for g in range(fields)]
            for f in range(fields)
        ]
    return mix


def transport(x, from_left, stay, from_right):
    for _ in range(STEPS):
        x = from_left * pltpu.roll(x, 1, 1) + stay * x + from_right * pltpu.roll(x, x.shape[1] - 1, 1)
    return x


def forecast_kernel(
    couple_ref, source, speed_ref, flag_ref, state, edge, sums_ref, work_ref, coef_ref,
):
    members, fields, cells = source.shape
    tiles = cells // LANES
    speed = speed_ref[...]
    toward_left = speed * flag_ref[...].astype(jnp.float32)
    toward_right = speed - toward_left

    def row_of(x):
        return jnp.concatenate([x[t : t + 1] for t in range(tiles)], axis=1)

    def shifted(x, by):
        return pltpu.roll(x, -by % cells, 1) if by else x

    step = {-1: row_of(toward_left + DIFFUSION), 0: row_of(1.0 - 2.0 * DIFFUSION - speed), 1: row_of(toward_right + DIFFUSION)}
    reach = dict(step)
    for _ in range(STEPS - 1):
        longer = {}
        for e in step:
            for d in reach:
                term = step[e] * shifted(reach[d], e)
                longer[d + e] = longer[d + e] + term if d + e in longer else term
        reach = longer
    for d in range(-STEPS, STEPS + 1):
        at = 8 * (d + STEPS)
        coef_ref[at : at + 8, :] = jnp.broadcast_to(reach[d], (8, cells))
    mix = power_of_coupling(couple_ref, fields)
    low = lax.broadcasted_iota(jnp.int32, (8, LANES), 1) < LANES // 2
    sums_ref[...] = jnp.zeros_like(sums_ref)

    def group(i, _):
        at = pl.multiple_of(i * 8, 8)
        for f in range(fields):
            x = source[pl.ds(at, 8), f, :]
            edge[pl.ds(f * members + at, 8), :] = jnp.where(
                low,
                pltpu.roll(x[:, :LANES], STEPS, 1),
                pltpu.roll(x[:, cells - LANES :], LANES // 2 + 3 * STEPS, 1),
            )
            total = None
            for d in range(-STEPS, STEPS + 1):
                term = coef_ref[8 * (d + STEPS) : 8 * (d + STEPS) + 8, :] * shifted(x, d)
                total = term if total is None else total + term
            work_ref[f * 8 : f * 8 + 8, :] = total
        for t in range(tiles):
            lanes = slice(t * LANES, (t + 1) * LANES)
            moved = [work_ref[f * 8 : (f + 1) * 8, lanes] for f in range(fields)]
            for f in range(fields):
                value = sum(mix[f][g] * moved[g] for g in range(fields))
                state[pl.ds(f * members + at, 8), lanes] = value
                place = (f * tiles + t) * 8
                sums_ref[place : place + 8, :] += value
        return 0

    lax.fori_loop(0, members // 8, group, 0)


def pieces_of(x):
    high = x.astype(jnp.bfloat16).astype(jnp.float32)
    rest = x - high
    middle = rest.astype(jnp.bfloat16).astype(jnp.float32)
    return high, middle, rest - middle


def sums_kernel(
    which_ref, couple_ref, speed_ref, flag_ref, own_state, own_edge, own_sums, other_state, other_edge, other_sums,
    kept, first, swapped, third, *refs, owners, units, fields,
):
    carried = refs[: len(units) - 1]
    (
        stay_ref, middle_ref, third_ref, edge_ref, halo_ref, onehot_ref, spread_ref, split_ref,
    ) = refs[len(units) - 1 :]
    states, raw_edges = (own_state, other_state), (own_edge, other_edge)
    block, core = which_ref[0], which_ref[1]
    members = states[0].shape[0] // fields
    cells = states[0].shape[1]
    tiles = cells // LANES
    total = 2 * members
    places = fields * tiles
    has_left = (block > 0).astype(jnp.float32)
    has_right = (block < owners - 1).astype(jnp.float32)
    sub = lax.broadcasted_iota(jnp.int32, (8, LANES), 0)
    lane = lax.broadcasted_iota(jnp.int32, (1, LANES), 1)
    lane8 = lax.broadcasted_iota(jnp.int32, (8, LANES), 1)
    half_lanes = LANES // 2
    low = lane < half_lanes

    strips = incoming(digit_of(block, units[-1]), core, first, swapped, third)
    for unit, earlier in reversed(list(zip(units, carried))):
        digit = digit_of(block, unit)
        rows = [earlier[8 * p : 8 * p + 8, :] for p in range(3)]
        picked = []
        for p in range(3):
            from_right = jnp.where(digit != 3, rows[p], strips[p])
            from_left = jnp.where(digit != 0, rows[p], strips[p])
            picked.append(jnp.where(sub < STEPS if p < 2 else lane8 < half_lanes, from_right, from_left))
        strips = picked

    right_first = half_lanes + 3 * STEPS
    strip_rows = fields * members
    for half in range(2):
        strip = strips[half]
        left = jnp.where(sub < STEPS, pltpu.roll(strip, STEPS, 0) * has_left, 0.0)
        at = right_first % 8
        right = jnp.where(
            (sub >= at) & (sub < at + STEPS), (pltpu.roll(strip, at, 0) if at else strip) * has_right, 0.0
        )
        gap = jnp.zeros((right_first - at - 8, LANES), jnp.float32)
        rest = jnp.zeros((LANES - (right_first - at) - 8, LANES), jnp.float32)
        halo_ref[half * strip_rows : (half + 1) * strip_rows, :] = jnp.transpose(
            jnp.concatenate([left, gap, right, rest], axis=0)
        )
    speed = speed_ref[...]
    toward_left = speed * flag_ref[...].astype(jnp.float32)
    toward_right = speed - toward_left
    is_left = lane < STEPS
    is_right = (lane >= right_first) & (lane < right_first + STEPS)
    inside = jnp.where(is_left, has_left, jnp.where(is_right, has_right, 1.0))
    from_outside = (lane8 < STEPS) | ((lane8 >= right_first) & (lane8 < right_first + STEPS))

    def edge_row(rows, row):
        own = jnp.where(
            low, pltpu.roll(rows[:1], STEPS, 1), pltpu.roll(rows[tiles - 1 :], half_lanes + 3 * STEPS, 1)
        )
        left = pltpu.roll(strips[2][row : row + 1], STEPS, 1)
        right = pltpu.roll(strips[2][row : row + 1], right_first, 1)
        return jnp.where(is_left, left, jnp.where(is_right, right, own))

    edge_left = edge_row(toward_left, 3)
    edge_right = edge_row(toward_right, 4)
    from_left = jnp.broadcast_to((edge_left + DIFFUSION) * inside, (8, LANES))
    from_right = jnp.broadcast_to((edge_right + DIFFUSION) * inside, (8, LANES))
    stay = jnp.broadcast_to((1.0 - 2.0 * DIFFUSION - edge_left - edge_right) * inside, (8, LANES))
    mix = power_of_coupling(couple_ref, fields)
    first_sums = [jnp.zeros((8, LANES), jnp.float32) for _ in range(fields)]
    last_sums = [jnp.zeros((8, LANES), jnp.float32) for _ in range(fields)]
    for half in range(2):
        state, edge = states[half], raw_edges[half]
        for i in range(members // 8):
            moved = []
            for f in range(fields):
                at = f * members + 8 * i
                x = edge[at : at + 8, :]
                x = jnp.where(from_outside, halo_ref[half * strip_rows + at : half * strip_rows + at + 8, :], x)
                moved.append(transport(x, from_left, stay, from_right))
            for f in range(fields):
                at = f * members + 8 * i
                value = sum(mix[f][g] * moved[g] for g in range(fields))
                first_tile = jnp.where(lane8 < STEPS, pltpu.roll(value, LANES - STEPS, 1), state[at : at + 8, :LANES])
                last_tile = jnp.where(
                    lane8 >= LANES - STEPS,
                    pltpu.roll(value, LANES - right_first, 1),
                    state[at : at + 8, cells - LANES :],
                )
                edge_ref[half * strip_rows + at : half * strip_rows + at + 8, :LANES] = first_tile
                edge_ref[half * strip_rows + at : half * strip_rows + at + 8, LANES:] = last_tile
                first_sums[f] = first_sums[f] + first_tile
                last_sums[f] = last_sums[f] + last_tile
    means = []
    for f in range(fields):
        for t in range(tiles):
            at = (f * tiles + t) * 8
            if t == 0:
                partial = first_sums[f]
            elif t == tiles - 1:
                partial = last_sums[f]
            else:
                partial = own_sums[at : at + 8, :] + other_sums[at : at + 8, :]
            means.append(jnp.sum(partial, axis=0, keepdims=True))
    mean = jnp.concatenate(means, axis=0) * (1.0 / total)

    place_ids = lax.broadcasted_iota(jnp.int32, (places, LANES), 0)
    lane_ids = lax.broadcasted_iota(jnp.int32, (LANES, LANES), 0)
    held = kept.shape[0] // 8
    sources = [(kept, 8 * j) for j in range(held)]
    for source in (first, swapped, third):
        sources += [(source, 16 + 8 * j) for j in range(held)]
    hits = []
    for n, (source, at) in enumerate(sources):
        local = source[at : at + 1, :].astype(jnp.int32)
        hit = place_ids == lax.shift_right_arithmetic(local, 7)
        hits.append(hit)
        onehot = (lane_ids == jnp.bitwise_and(local, LANES - 1)).astype(jnp.float32)
        lanes = slice(n * LANES, (n + 1) * LANES)
        onehot_ref[:, lanes] = onehot.astype(jnp.bfloat16)
        weight, pull = source[at + 1 : at + 2, :], source[at + 2 : at + 3, :]
        stack = [jnp.where(hit, piece, 0.0) for piece in pieces_of(weight) + pieces_of(pull)]
        spread_ref[:, lanes] = jnp.concatenate(stack, axis=0).astype(jnp.bfloat16)
    placed = lax.dot_general(
        spread_ref[...], onehot_ref[...], (((1,), (1,)), ((), ())), preferred_element_type=jnp.float32
    )
    placed = [placed[p * places : (p + 1) * places] for p in range(6)]
    weight = placed[0] + placed[1] + placed[2]
    pull = placed[3] + placed[4] + placed[5] - weight * mean

    root = jnp.sqrt(weight)
    pull = jnp.where(weight > 0.0, pull * lax.rsqrt(jnp.where(weight > 0.0, weight, 1.0)), 0.0)
    sub16 = lax.broadcasted_iota(jnp.int32, (16, LANES), 0)
    depth = total + 16

    def put(row, lanes, value):
        for p, piece in enumerate(pieces_of(value)):
            split_ref[pl.ds(row + p * depth, value.shape[0]), lanes] = piece.astype(jnp.bfloat16)

    for f in range(fields):
        for t in range(tiles):
            at = f * tiles + t
            lanes = slice(t * LANES, (t + 1) * LANES)
            into = slice(at * LANES, (at + 1) * LANES)
            for half in range(2):
                if t in (0, tiles - 1):
                    column = slice(0, LANES) if t == 0 else slice(LANES, 2 * LANES)
                    value = edge_ref[half * strip_rows + f * members : half * strip_rows + (f + 1) * members, column]
                else:
                    value = states[half][f * members : (f + 1) * members, lanes]
                anomaly = (value - mean[at : at + 1]) * root[at : at + 1]
                side = core if half == 0 else 1 - core
                put(pl.multiple_of(side * members, 16), into, anomaly)
            put(total, into, jnp.where(sub16 == 0, pull[at : at + 1], 0.0))
    products = lax.dot_general(
        split_ref[...], split_ref[...], (((1,), (1,)), ((), ())), preferred_element_type=jnp.float32
    )
    gram = sum(
        products[p * depth : p * depth + total + 8, q * depth : q * depth + total]
        for p, q in ((2, 0), (1, 1), (0, 2), (1, 0), (0, 1), (0, 0))
    )
    gram = jnp.concatenate([gram, jnp.zeros((total + 8, LANES - total), jnp.float32)], axis=1)
    folded = gram[:members] + pltpu.roll(gram[members:total], total, 1)
    blank = jnp.zeros((stay_ref.shape[0] - members - 1, LANES), jnp.float32)
    for out in (stay_ref, middle_ref, third_ref):
        out[:members, :] = folded
        out[members : members + 1, :] = gram[total : total + 1]
        out[members + 1 :, :] = blank

    found = lax.dot_general(
        jnp.concatenate(pieces_of(mean), axis=0).astype(jnp.bfloat16), onehot_ref[...],
        (((1,), (0,)), ((), ())), preferred_element_type=jnp.float32,
    )
    found = found[:places] + found[places : 2 * places] + found[2 * places :]
    for out, source, partner in ((stay_ref, 0, 0), (middle_ref, 1, 1 + core), (third_ref, 3, 3)):
        for j in range(held):
            n = source * held + j
            center = jnp.sum(
                jnp.where(hits[n], found[:, n * LANES : (n + 1) * LANES], 0.0), axis=0, keepdims=True
            )
            out[pl.ds(members + 1 + partner * held + j, 1), :] = center


def spread_row(row):
    return jnp.broadcast_to(row, (8, LANES))


def eliminate(rows):
    count = len(rows)
    rows = list(rows)
    sub = lax.broadcasted_iota(jnp.int32, (8, LANES), 0)
    for b in range(count):
        columns = [
            [jnp.broadcast_to(rows[i][:, 8 * b + k : 8 * b + k + 1], (8, LANES)) for k in range(8)]
            for i in range(b, count)
        ]
        for j in range(8):
            scale = lax.rsqrt(spread_row(columns[0][j][j : j + 1, :]))
            upper = spread_row(rows[b][j : j + 1, :]) * scale
            lower = columns[0][j] * scale
            factors = [spread_row(lower[k : k + 1, :]) for k in range(8)]
            for i in range(b, count):
                here = lower if i == b else columns[i - b][j] * scale
                if i == b:
                    rows[b] = jnp.where(sub == j, upper, rows[b] - jnp.where(sub > j, here, 0.0) * upper)
                else:
                    rows[i] = rows[i] - here * upper
                for k in range(j + 1, 8):
                    columns[i - b][k] = columns[i - b][k] - here * factors[k]
    return rows


def analysis_kernel(
    which_ref, send_ref, own_ref, other_ref, edge_ref, value_ref, sigma_ref, kept, first, swapped, third,
    analysis_ref, innovation_ref, mixing_ref, center_ref, *, units, obs_rows,
):
    block, core = which_ref[0], which_ref[1]
    members, fields, cells = analysis_ref.shape
    total = 2 * members
    head = members + 1
    sums = (kept[:head, :] + third[:head, :]) + (first[:head, :] + swapped[:head, :])
    returned = kept.shape[0] - head
    center_ref[:returned, :] = kept[head:, :]
    center_ref[returned : 2 * returned, :] = jnp.where(core == 0, first[head:, :], swapped[head:, :])
    center_ref[2 * returned : 3 * returned, :] = jnp.where(core == 0, swapped[head:, :], first[head:, :])
    center_ref[3 * returned :, :] = third[head:, :]
    lane = lax.broadcasted_iota(jnp.int32, (8, LANES), 1)
    sub = lax.broadcasted_iota(jnp.int32, (8, LANES), 0)
    shifted = pltpu.roll(sums[:members], LANES - total, 1)
    rows = []
    for b in range(total // 8):
        at = 8 * b
        source = sums[at : at + 8] if at < members else shifted[at - members : at - members + 8]
        own = jnp.where(lane == sub + at, total - 1.0, 0.0)
        unit = jnp.where(lane == sub + at + total, 1.0, 0.0)
        rows.append(jnp.where(lane < total, source + own, unit))
    rows = eliminate(rows)
    cross = sums[members : members + 1]
    inverse = [jnp.where(lane < total, pltpu.roll(r, LANES - total, 1), 0.0) for r in rows]
    carried = [jnp.sum(r * cross, axis=1, keepdims=True) for r in inverse]
    weights = sum(jnp.sum(r * c, axis=0, keepdims=True) for r, c in zip(inverse, carried))
    row_means = [jnp.sum(r, axis=1, keepdims=True) * (1.0 / total) for r in inverse]
    column_mean = sum(jnp.sum(r, axis=0, keepdims=True) for r in inverse) * (1.0 / total)
    grand = jnp.sum(column_mean, axis=1, keepdims=True) * (1.0 / total)
    weights = weights - jnp.sum(weights, axis=1, keepdims=True) * (1.0 / total)
    root = math.sqrt(total - 1.0)
    add = weights + 1.0 / total - root * (column_mean - grand)
    for b in range(total // 8):
        mixing_ref[8 * b : 8 * b + 8, :] = root * (inverse[b] - row_means[b]) + add
    own_rows = mixing_ref[pl.ds(pl.multiple_of(core * members, 8), members), :]
    rolled = pltpu.roll(own_rows, LANES - members, 1)
    to_own = jnp.where(core == 0, own_rows, rolled)[:, :members]
    to_other = jnp.where(core == 0, rolled, own_rows)[:, :members]
    mixing = jnp.concatenate([to_own, to_other], axis=1)
    strip_rows = fields * members
    for f in range(fields):
        rows = slice(f * members, (f + 1) * members)
        other_rows = slice(strip_rows + f * members, strip_rows + (f + 1) * members)
        states = jnp.concatenate(
            [
                jnp.concatenate([edge_ref[rows, :LANES], edge_ref[other_rows, :LANES]], axis=0),
                jnp.concatenate(
                    [own_ref[rows, LANES : cells - LANES], other_ref[rows, LANES : cells - LANES]], axis=0
                ),
                jnp.concatenate([edge_ref[rows, LANES:], edge_ref[other_rows, LANES:]], axis=0),
            ],
            axis=1,
        )
        analysis_ref[:, f, :] = jnp.dot(
            mixing, states, precision=EXACT, preferred_element_type=jnp.float32
        )
    owners = send_ref.shape[1]
    held = owners // 16
    wide = obs_rows * LANES
    slot = lax.broadcasted_iota(jnp.int32, (1, wide), 1)
    centers = jnp.zeros((1, wide), jnp.float32)
    start = jnp.int32(0)
    for owner in range(owners):
        way = [jnp.bitwise_xor(digit_of(block, unit), (owner // unit) % 4) for unit in units]
        row = way[-1] * held
        if len(units) > 2:
            row = row + sum(step * 4**s for s, step in enumerate(way[:-2]))
        size = 4 * held
        for step in reversed(way[1:-1]):
            row = row + step * size
            size = size * 4
        row = row + way[0] * returned
        line = center_ref[pl.ds(row, 1), :]
        line = jnp.concatenate([line] + [jnp.zeros((1, LANES), jnp.float32)] * (obs_rows - 1), axis=1)
        moved = pltpu.roll(line, lax.rem(start - way[-2] * CAP + 2 * wide, jnp.int32(wide)), 1)
        end = start + send_ref[0, owner]
        centers = jnp.where((slot >= start) & (slot < end), moved, centers)
        start = end
    for r in range(obs_rows):
        center = centers[:, r * LANES : (r + 1) * LANES]
        innovation_ref[r : r + 1, :] = (value_ref[r : r + 1, :] - center) / sigma_ref[r : r + 1, :]


def shards(
    ensemble, speed, direction, couple, obs_place, obs_field, obs_value, obs_sigma, send_count
):
    members, fields, cells = ensemble.shape
    owners = lax.axis_size("cells")
    total = members * lax.axis_size("members")
    obs = obs_place.shape[0]
    obs_rows = obs // LANES
    tiles = cells // LANES
    places = fields * tiles
    units = stage_units(owners)
    block = lax.axis_index("cells").astype(jnp.int32)
    core = lax.axis_index("members").astype(jnp.int32)
    which = jnp.stack([block, core])
    speed = speed.reshape(tiles, LANES)
    direction = direction.reshape(tiles, LANES)
    obs_place, obs_field, obs_value, obs_sigma = (
        x.reshape(obs_rows, LANES) for x in (obs_place, obs_field, obs_value, obs_sigma)
    )
    whole = pl.BlockSpec(memory_space=pltpu.VMEM)
    scalars = pl.BlockSpec(memory_space=pltpu.SMEM)
    params = pltpu.CompilerParams(vmem_limit_bytes=VMEM_BYTES)
    real = jnp.float32

    table_rows = 8 * (owners // GROUPS)
    strips, table = pl.pallas_call(
        functools.partial(pack_kernel, rows=obs_rows),
        out_shape=(jax.ShapeDtypeStruct((8, LANES), real), jax.ShapeDtypeStruct((table_rows, LANES), real)),
        in_specs=[pl.BlockSpec(memory_space=pltpu.HBM)] * 8,
        out_specs=(whole, whole),
        scratch_shapes=[
            pltpu.SMEM(send_count.shape, jnp.int32),
            pltpu.VMEM((members, fields, LANES), real),
            pltpu.VMEM((members, fields, LANES), real),
            pltpu.VMEM((tiles, LANES), real),
            pltpu.VMEM((tiles, LANES), jnp.int32),
            pltpu.VMEM((obs_rows, LANES), jnp.int32),
            pltpu.VMEM((obs_rows, LANES), jnp.int32),
            pltpu.VMEM((obs_rows, LANES), real),
            pltpu.VMEM((obs_rows, LANES), real),
            pltpu.SemaphoreType.DMA((9,)),
        ],
        name="pack",
    )(send_count, ensemble, speed, direction, obs_place, obs_field, obs_value, obs_sigma)

    def forecast(half):
        return pl.pallas_call(
            forecast_kernel,
            out_shape=(
                jax.ShapeDtypeStruct((strip_rows, cells), real),
                jax.ShapeDtypeStruct((strip_rows, LANES), real),
                jax.ShapeDtypeStruct((places * 8, LANES), real),
            ),
            in_specs=[scalars] + [whole] * 3,
            out_specs=(whole,) * 3,
            scratch_shapes=[
                pltpu.VMEM((fields * 8, cells), real),
                pltpu.VMEM((8 * (2 * STEPS + 1), cells), real),
            ],
            compiler_params=params,
            cost_estimate=pl.CostEstimate(
                flops=80 * strip_rows * cells, bytes_accessed=8 * strip_rows * cells, transcendentals=0
            ),
            name="forecast",
        )(couple, half, speed, direction)

    strip_rows = fields * members
    other_strips = swap_cores(strips, owners)
    other = swap_cores(ensemble, owners)
    own_forecast = forecast(ensemble)
    part = table_rows // 4
    digit = digit_of(block, 1)

    def part_of(partner):
        return lax.dynamic_slice_in_dim(table, jnp.bitwise_xor(digit, partner) * part, part, 0)

    kept = part_of(0)
    to_middle = jnp.concatenate([strips, other_strips, part_of(1 + core)], axis=0)
    to_third = jnp.concatenate([strips, other_strips, part_of(3)], axis=0)
    carried = []
    for n, unit in enumerate(units):
        arrived = exchange(to_middle, to_third, owners, unit)
        if n + 1 < len(units):
            payload = jax.ShapeDtypeStruct(to_third.shape, real)
            to_middle, to_third, kept = pl.pallas_call(
                functools.partial(regroup_kernel, unit=unit, into_lanes=n + 2 == len(units)),
                out_shape=(payload, payload, jax.ShapeDtypeStruct(kept.shape, real)),
                in_specs=[scalars] + [whole] * 4 + [pl.BlockSpec(memory_space=pl.ANY)],
                out_specs=(whole,) * 3,
                compiler_params=params,
                name="regroup",
            )(which, kept, *arrived, own_forecast[2])
            carried.append(to_third)
    other_forecast = forecast(other)

    held = kept.shape[0] // 8
    sums_rows = -(-(members + 1 + 4 * held) // 8) * 8
    all_slots = 4 * held * LANES
    sums = jax.ShapeDtypeStruct((sums_rows, LANES), real)
    stay, to_middle, to_third, edges = pl.pallas_call(
        functools.partial(sums_kernel, owners=owners, units=units, fields=fields),
        out_shape=(sums, sums, sums, jax.ShapeDtypeStruct((2 * strip_rows, 2 * LANES), real)),
        in_specs=[scalars, scalars] + [whole] * (12 + len(carried)),
        out_specs=(whole,) * 4,
        scratch_shapes=[
            pltpu.VMEM((2 * strip_rows, LANES), real),
            pltpu.VMEM((LANES, all_slots), jnp.bfloat16),
            pltpu.VMEM((6 * places, all_slots), jnp.bfloat16),
            pltpu.VMEM((3 * (total + 16), fields * cells), jnp.bfloat16),
        ],
        compiler_params=params,
        name="sums",
    )(
        which, couple, speed, direction, *own_forecast, *other_forecast, kept, *arrived, *carried,
    )

    head = members + 1
    used = head + 4 * held
    for n, unit in enumerate(reversed(units)):
        first, swapped, third = exchange(to_middle, to_third, owners, unit)
        if n + 1 < len(units):
            added = (stay + third) + (first + swapped)
            if n > 0:
                near = jnp.where(core == 0, first, swapped)
                middle = jnp.where(core == 0, swapped, first)
                added = jnp.concatenate(
                    [added[:head]] + [x[head:used] for x in (stay, near, middle, third)], axis=0
                )
                used = added.shape[0]
            stay = to_middle = to_third = added

    analysis, innovation = pl.pallas_call(
        functools.partial(analysis_kernel, units=units, obs_rows=obs_rows),
        out_shape=(
            jax.ShapeDtypeStruct((members, fields, cells), real),
            jax.ShapeDtypeStruct((obs_rows, LANES), real),
        ),
        in_specs=[scalars, scalars] + [whole] * 9,
        out_specs=(whole, whole),
        scratch_shapes=[
            pltpu.VMEM((total, LANES), real),
            pltpu.VMEM((4 * (stay.shape[0] - head), LANES), real),
        ],
        compiler_params=params,
        name="analysis",
    )(
        which, send_count, own_forecast[0], other_forecast[0], edges, obs_value, obs_sigma,
        stay, first, swapped, third,
    )
    return (analysis, innovation.reshape(obs))


def solution(mesh):
    return jax.shard_map(
        shards,
        mesh=mesh,
        in_specs=(
            P("members", None, "cells"),
            P("cells"),
            P("cells"),
            P(),
            P("cells"),
            P("cells"),
            P("cells"),
            P("cells"),
            P("cells", None),
        ),
        out_specs=(P("members", None, "cells"), P("cells")),
        check_vma=False,
    )
```

```python
import functools
import math

import jax
import jax.numpy as jnp
from jax import lax
from jax.experimental import pallas as pl
from jax.experimental.pallas import tpu as pltpu
from jax.sharding import PartitionSpec as P

STEPS = 4
DIFFUSION = 0.05
LANES = 128
CAP = 32
GROUPS = LANES // CAP
BOTH = ("cells", "members")
EXACT = lax.Precision.HIGHEST
VMEM_BYTES = 48 * 1024 * 1024


def core_pairs(owners, place):
    pairs = []
    for block in range(owners):
        for core in range(2):
            to_block, to_core = place(block, core)
            pairs.append((block * 2 + core, to_block * 2 + to_core))
    return pairs


def stage_units(owners):
    units = []
    unit = 1
    while unit < owners:
        units.append(unit)
        unit *= 4
    if unit != owners or len(units) < 2:
        raise ValueError("blocks not 4**n")
    return units


def swap_cores(x, owners):
    return lax.ppermute(x, BOTH, core_pairs(owners, lambda block, core: (block, 1 - core)))


def exchange(to_odd, to_even, owners, unit):
    odd = lax.ppermute(
        to_odd, BOTH, core_pairs(owners, lambda block, core: (block ^ (unit * (1 + 2 * core)), core))
    )
    even = lax.ppermute(
        to_even, BOTH, core_pairs(owners, lambda block, core: (block ^ (unit * 2), core))
    )
    return odd, swap_cores(odd, owners), even


def digit_of(block, unit):
    return jnp.bitwise_and(lax.shift_right_logical(block, jnp.int32(unit.bit_length() - 1)), 3)


def within(shift, wide):
    shift = jnp.where(shift < 0, shift + wide, shift)
    return jnp.where(shift >= wide, shift - wide, shift)


def table_row(number, count):
    return (number % 4) * (count // 4) + number // 4


def strips_of(head, tail):
    fields, cells = tail.shape[1:]
    lane = lax.broadcasted_iota(jnp.int32, (1, LANES), 1)
    ends = [jnp.where(lane < STEPS, head[:, f, :LANES], tail[:, f, cells - LANES :]) for f in range(fields)]
    ends = jnp.transpose(jnp.concatenate(ends, axis=0))
    return jnp.concatenate([ends[:STEPS, :], ends[LANES - STEPS :, :]], axis=0)


def pack_kernel(
    which_ref, send_ref, speed_ref, flag_ref, place_ref, field_ref, value_ref, sigma_ref,
    kept_ref, odd_ref, even_ref, small_ref, table_ref, *, rows, cells, fields,
):
    tiles = cells // LANES
    speed, value, sigma = speed_ref[...], value_ref[...], sigma_ref[...]
    flag, place, field = (ref[...].astype(jnp.float32) for ref in (flag_ref, place_ref, field_ref))
    at = 0
    for part in (speed, flag, value, sigma):
        small_ref[at : at + part.shape[0], :] = part
        at += part.shape[0]
    lane = lax.broadcasted_iota(jnp.int32, (1, LANES), 1)
    low = lane < LANES // 2
    toward_left = speed * flag
    toward_right = speed - toward_left
    edge_left = jnp.where(low, toward_left[:1], toward_left[tiles - 1 :])
    edge_right = jnp.where(low, toward_right[:1], toward_right[tiles - 1 :])
    ids = field * float(cells) + place
    weight = 1.0 / (sigma * sigma)
    pull = weight * value
    wide = rows * LANES

    def row_of(x):
        return jnp.concatenate([x[r : r + 1] for r in range(rows)], axis=1)

    listed = jnp.concatenate(
        [row_of(ids), row_of(weight), row_of(pull), jnp.zeros((5, wide), jnp.float32)], axis=0
    )
    sub = lax.broadcasted_iota(jnp.int32, (8, LANES), 0)
    lane8 = lax.broadcasted_iota(jnp.int32, (8, LANES), 1)
    empty = jnp.where(sub == 0, -1.0, 0.0)
    empty = jnp.where(sub == 3, edge_left, jnp.where(sub == 4, edge_right, empty))
    owners = send_ref.shape[1]
    count = owners // GROUPS
    table = [empty] * count
    start = jnp.int32(0)
    for owner in range(owners):
        held = send_ref[0, owner]
        group, r = owner // count, owner % count
        moved = pltpu.roll(listed, within(group * CAP - start, wide), 1)[:, :LANES]
        here = (lane8 >= group * CAP) & (lane8 < group * CAP + held) & (sub < 3)
        table[r] = jnp.where(here, moved, table[r])
        start = start + held
    for r in range(count):
        row = 8 * table_row(r, count)
        table_ref[row : row + 8, :] = table[r]
    part = kept_ref.shape[0]
    digit = digit_of(which_ref[0], 1)
    for out, partner in ((kept_ref, 0), (odd_ref, 1 + 2 * which_ref[1]), (even_ref, 2)):
        out[...] = table_ref[pl.ds(pl.multiple_of(jnp.bitwise_xor(digit, partner) * part, 8), part), :]


def strips_kernel(ensemble_ref, out_ref):
    out_ref[...] = strips_of(ensemble_ref, ensemble_ref)


def join_kernel(own_ref, other_ref, odd_part, even_part, odd_ref, even_ref):
    strips = jnp.concatenate([own_ref[...], strips_of(other_ref, other_ref)], axis=0)
    for part, out in ((odd_part, odd_ref), (even_part, even_ref)):
        out[:16, :] = strips
        out[16:, :] = part[...]


def incoming(digit, core, odd, swapped):
    sub = lax.broadcasted_iota(jnp.int32, (8, LANES), 0)
    low = lax.broadcasted_iota(jnp.int32, (8, LANES), 1) < LANES // 2
    direct = jnp.bitwise_xor(jnp.bitwise_and(digit, 1), core) == 0
    result = []
    for part, other_part in ((0, 1), (1, 0), (2, 2)):
        mine = odd[8 * part : 8 * part + 8, :]
        others = swapped[8 * other_part : 8 * other_part + 8, :]
        from_right = jnp.where(direct, mine, others)
        from_left = jnp.where(direct, others, mine)
        result.append(jnp.where(sub < STEPS if part < 2 else low, from_right, from_left))
    return result


def regroup_kernel(
    which_ref, kept, odd, swapped, even, _, to_odd, to_even, stay, *, unit, into_lanes,
):
    block, core = which_ref[0], which_ref[1]
    after = digit_of(block, unit * 4)
    own, other, coefs = incoming(digit_of(block, unit), core, odd, swapped)
    sub = lax.broadcasted_iota(jnp.int32, (8, LANES), 0)
    lane_group = lax.broadcasted_iota(jnp.int32, (8, LANES), 1) // CAP
    held = kept.shape[0] // 8

    def received(k, at):
        if k == 0:
            return kept[pl.ds(at, 8), :]
        if k == 2:
            return even[pl.ds(16 + at, 8), :]
        mine, others = odd[pl.ds(16 + at, 8), :], swapped[pl.ds(16 + at, 8), :]
        return jnp.where(core == k // 2, mine, others)

    for target in (to_odd, to_even):
        target[0:8, :] = own
        target[8:16, :] = other
    for target, base, partner in ((to_odd, 16, 1 + 2 * core), (to_even, 16, 2), (stay, 0, 0)):
        wanted = jnp.bitwise_xor(after, partner)
        if into_lanes:
            for j in range(held):
                merged = coefs
                for k in range(4):
                    moved = pltpu.roll(received(k, 8 * j), jnp.bitwise_and(k - wanted, 3) * CAP, 1)
                    merged = jnp.where((lane_group == k) & (sub < 3), moved, merged)
                target[base + 8 * j : base + 8 * j + 8, :] = merged
        else:
            rest = held // 4
            for k in range(4):
                for r in range(rest):
                    at = pl.multiple_of((wanted * rest + r) * 8, 8)
                    row = base + 8 * (r * 4 + k)
                    target[row : row + 8, :] = jnp.where(sub < 3, received(k, at), coefs)


def power_of_coupling(couple_ref, fields):
    mix = [[couple_ref[f, g] + (1.0 if f == g else 0.0) for g in range(fields)] for f in range(fields)]
    for _ in range(2):
        mix = [
            [sum(mix[f][h] * mix[h][g] for h in range(fields)) for g in range(fields)]
            for f in range(fields)
        ]
    return mix


def transport(x, from_left, stay, from_right):
    for _ in range(STEPS):
        x = from_left * pltpu.roll(x, 1, 1) + stay * x + from_right * pltpu.roll(x, x.shape[1] - 1, 1)
    return x


def forecast_kernel(
    couple_ref, source, small_ref, state, edge, sums_ref, work_ref, coef_ref,
):
    members, fields, cells = source.shape
    tiles = cells // LANES
    speed = small_ref[:tiles, :]
    toward_left = speed * small_ref[tiles : 2 * tiles, :]
    toward_right = speed - toward_left

    def row_of(x):
        return jnp.concatenate([x[t : t + 1] for t in range(tiles)], axis=1)

    def shifted(x, by):
        return pltpu.roll(x, -by % cells, 1) if by else x

    step = {-1: row_of(toward_left + DIFFUSION), 0: row_of(1.0 - 2.0 * DIFFUSION - speed), 1: row_of(toward_right + DIFFUSION)}
    reach = dict(step)
    for _ in range(STEPS - 1):
        longer = {}
        for e in step:
            for d in reach:
                term = step[e] * shifted(reach[d], e)
                longer[d + e] = longer[d + e] + term if d + e in longer else term
        reach = longer
    for d in range(-STEPS, STEPS + 1):
        at = 8 * (d + STEPS)
        coef_ref[at : at + 8, :] = jnp.broadcast_to(reach[d], (8, cells))
    mix = power_of_coupling(couple_ref, fields)
    low = lax.broadcasted_iota(jnp.int32, (8, LANES), 1) < LANES // 2
    sums_ref[...] = jnp.zeros_like(sums_ref)

    def group(i, _):
        at = pl.multiple_of(i * 8, 8)
        for f in range(fields):
            x = source[pl.ds(at, 8), f, :]
            edge[pl.ds(f * members + at, 8), :] = jnp.where(
                low,
                pltpu.roll(x[:, :LANES], STEPS, 1),
                pltpu.roll(x[:, cells - LANES :], LANES // 2 + 3 * STEPS, 1),
            )
            total = None
            for d in range(-STEPS, STEPS + 1):
                term = coef_ref[8 * (d + STEPS) : 8 * (d + STEPS) + 8, :] * shifted(x, d)
                total = term if total is None else total + term
            work_ref[f * 8 : f * 8 + 8, :] = total
        for t in range(tiles):
            lanes = slice(t * LANES, (t + 1) * LANES)
            moved = [work_ref[f * 8 : (f + 1) * 8, lanes] for f in range(fields)]
            for f in range(fields):
                value = sum(mix[f][g] * moved[g] for g in range(fields))
                state[pl.ds(f * members + at, 8), lanes] = value
                place = (f * tiles + t) * 8
                sums_ref[place : place + 8, :] += value
        return 0

    lax.fori_loop(0, members // 8, group, 0)


def halves_of(x):
    high = x.astype(jnp.bfloat16)
    return high, (x - high.astype(jnp.float32)).astype(jnp.bfloat16)


def pieces_of(x):
    high = x.astype(jnp.bfloat16).astype(jnp.float32)
    rest = x - high
    middle = rest.astype(jnp.bfloat16).astype(jnp.float32)
    return high, middle, rest - middle


def sums_kernel(
    which_ref, couple_ref, small_ref, own_state, own_edge, own_sums, other_state, other_edge, other_sums,
    kept, odd, swapped, even, *refs, owners, units, fields,
):
    carried = refs[: len(units) - 1]
    (
        stay_ref, odd_ref, even_ref, edge_ref, halo_ref, onehot_ref, spread_ref, split_ref,
    ) = refs[len(units) - 1 :]
    states, raw_edges = (own_state, other_state), (own_edge, other_edge)
    block, core = which_ref[0], which_ref[1]
    members = states[0].shape[0] // fields
    cells = states[0].shape[1]
    tiles = cells // LANES
    total = 2 * members
    places = fields * tiles
    has_left = (block > 0).astype(jnp.float32)
    has_right = (block < owners - 1).astype(jnp.float32)
    sub = lax.broadcasted_iota(jnp.int32, (8, LANES), 0)
    lane = lax.broadcasted_iota(jnp.int32, (1, LANES), 1)
    lane8 = lax.broadcasted_iota(jnp.int32, (8, LANES), 1)
    half_lanes = LANES // 2
    low = lane < half_lanes

    strips = incoming(digit_of(block, units[-1]), core, odd, swapped)
    for unit, earlier in reversed(list(zip(units, carried))):
        digit = digit_of(block, unit)
        rows = [earlier[8 * p : 8 * p + 8, :] for p in range(3)]
        picked = []
        for p in range(3):
            from_right = jnp.where(digit != 3, rows[p], strips[p])
            from_left = jnp.where(digit != 0, rows[p], strips[p])
            picked.append(jnp.where(sub < STEPS if p < 2 else lane8 < half_lanes, from_right, from_left))
        strips = picked

    right_first = half_lanes + 3 * STEPS
    strip_rows = fields * members
    for half in range(2):
        strip = strips[half]
        left = jnp.where(sub < STEPS, pltpu.roll(strip, STEPS, 0) * has_left, 0.0)
        at = right_first % 8
        right = jnp.where(
            (sub >= at) & (sub < at + STEPS), (pltpu.roll(strip, at, 0) if at else strip) * has_right, 0.0
        )
        gap = jnp.zeros((right_first - at - 8, LANES), jnp.float32)
        rest = jnp.zeros((LANES - (right_first - at) - 8, LANES), jnp.float32)
        halo_ref[half * strip_rows : (half + 1) * strip_rows, :] = jnp.transpose(
            jnp.concatenate([left, gap, right, rest], axis=0)
        )
    speed = small_ref[:tiles, :]
    toward_left = speed * small_ref[tiles : 2 * tiles, :]
    toward_right = speed - toward_left
    is_left = lane < STEPS
    is_right = (lane >= right_first) & (lane < right_first + STEPS)
    inside = jnp.where(is_left, has_left, jnp.where(is_right, has_right, 1.0))
    from_outside = (lane8 < STEPS) | ((lane8 >= right_first) & (lane8 < right_first + STEPS))

    def edge_row(rows, row):
        own = jnp.where(
            low, pltpu.roll(rows[:1], STEPS, 1), pltpu.roll(rows[tiles - 1 :], half_lanes + 3 * STEPS, 1)
        )
        left = pltpu.roll(strips[2][row : row + 1], STEPS, 1)
        right = pltpu.roll(strips[2][row : row + 1], right_first, 1)
        return jnp.where(is_left, left, jnp.where(is_right, right, own))

    edge_left = edge_row(toward_left, 3)
    edge_right = edge_row(toward_right, 4)
    from_left = jnp.broadcast_to((edge_left + DIFFUSION) * inside, (8, LANES))
    from_right = jnp.broadcast_to((edge_right + DIFFUSION) * inside, (8, LANES))
    stay = jnp.broadcast_to((1.0 - 2.0 * DIFFUSION - edge_left - edge_right) * inside, (8, LANES))
    mix = power_of_coupling(couple_ref, fields)
    first_sums = [jnp.zeros((8, LANES), jnp.float32) for _ in range(fields)]
    last_sums = [jnp.zeros((8, LANES), jnp.float32) for _ in range(fields)]
    for half in range(2):
        state, edge = states[half], raw_edges[half]
        for i in range(members // 8):
            moved = []
            for f in range(fields):
                at = f * members + 8 * i
                x = edge[at : at + 8, :]
                x = jnp.where(from_outside, halo_ref[half * strip_rows + at : half * strip_rows + at + 8, :], x)
                moved.append(transport(x, from_left, stay, from_right))
            for f in range(fields):
                at = f * members + 8 * i
                value = sum(mix[f][g] * moved[g] for g in range(fields))
                first_tile = jnp.where(lane8 < STEPS, pltpu.roll(value, LANES - STEPS, 1), state[at : at + 8, :LANES])
                last_tile = jnp.where(
                    lane8 >= LANES - STEPS,
                    pltpu.roll(value, LANES - right_first, 1),
                    state[at : at + 8, cells - LANES :],
                )
                edge_ref[half * strip_rows + at : half * strip_rows + at + 8, :LANES] = first_tile
                edge_ref[half * strip_rows + at : half * strip_rows + at + 8, LANES:] = last_tile
                first_sums[f] = first_sums[f] + first_tile
                last_sums[f] = last_sums[f] + last_tile
    means = []
    for f in range(fields):
        for t in range(tiles):
            at = (f * tiles + t) * 8
            if t == 0:
                partial = first_sums[f]
            elif t == tiles - 1:
                partial = last_sums[f]
            else:
                partial = own_sums[at : at + 8, :] + other_sums[at : at + 8, :]
            means.append(jnp.sum(partial, axis=0, keepdims=True))
    mean = jnp.concatenate(means, axis=0) * (1.0 / total)

    place_ids = lax.broadcasted_iota(jnp.int32, (places, LANES), 0)
    lane_ids = lax.broadcasted_iota(jnp.int32, (LANES, LANES), 0)
    held = kept.shape[0] // 8
    sources = [(kept, 8 * j) for j in range(held)]
    for source, base in ((odd, 16), (swapped, 16), (even, 16)):
        sources += [(source, base + 8 * j) for j in range(held)]
    hits = []
    for n, (source, at) in enumerate(sources):
        local = source[at : at + 1, :].astype(jnp.int32)
        hit = place_ids == lax.shift_right_arithmetic(local, 7)
        hits.append(hit)
        onehot = (lane_ids == jnp.bitwise_and(local, LANES - 1)).astype(jnp.float32)
        lanes = slice(n * LANES, (n + 1) * LANES)
        onehot_ref[:, lanes] = onehot.astype(jnp.bfloat16)
        weight, pull = source[at + 1 : at + 2, :], source[at + 2 : at + 3, :]
        stack = [jnp.where(hit, piece, 0.0) for piece in pieces_of(weight) + pieces_of(pull)]
        spread_ref[:, lanes] = jnp.concatenate(stack, axis=0).astype(jnp.bfloat16)
    placed = lax.dot_general(
        spread_ref[...], onehot_ref[...], (((1,), (1,)), ((), ())), preferred_element_type=jnp.float32
    )
    placed = [placed[p * places : (p + 1) * places] for p in range(6)]
    weight = placed[0] + placed[1] + placed[2]
    pull = placed[3] + placed[4] + placed[5] - weight * mean

    root = jnp.sqrt(weight)
    pull = jnp.where(weight > 0.0, pull * lax.rsqrt(jnp.where(weight > 0.0, weight, 1.0)), 0.0)
    sub16 = lax.broadcasted_iota(jnp.int32, (16, LANES), 0)
    depth = total + 16

    def put(row, lanes, value):
        for p, piece in enumerate(halves_of(value)):
            split_ref[pl.ds(row + p * depth, value.shape[0]), lanes] = piece

    for f in range(fields):
        for t in range(tiles):
            at = f * tiles + t
            lanes = slice(t * LANES, (t + 1) * LANES)
            into = slice(at * LANES, (at + 1) * LANES)
            for half in range(2):
                if t in (0, tiles - 1):
                    column = slice(0, LANES) if t == 0 else slice(LANES, 2 * LANES)
                    value = edge_ref[half * strip_rows + f * members : half * strip_rows + (f + 1) * members, column]
                else:
                    value = states[half][f * members : (f + 1) * members, lanes]
                anomaly = (value - mean[at : at + 1]) * root[at : at + 1]
                side = core if half == 0 else 1 - core
                put(pl.multiple_of(side * members, 16), into, anomaly)
            put(total, into, jnp.where(sub16 == 0, pull[at : at + 1], 0.0))
    products = lax.dot_general(
        split_ref[...], split_ref[...], (((1,), (1,)), ((), ())), preferred_element_type=jnp.float32
    )
    gram = sum(
        products[p * depth : p * depth + total + 8, q * depth : q * depth + total]
        for p, q in ((1, 1), (1, 0), (0, 1), (0, 0))
    )
    gram = jnp.concatenate([gram, jnp.zeros((total + 8, LANES - total), jnp.float32)], axis=1)
    folded = gram[:members] + pltpu.roll(gram[members:total], total, 1)
    blank = jnp.zeros((stay_ref.shape[0] - members - 1, LANES), jnp.float32)
    for out in (stay_ref, odd_ref, even_ref):
        out[:members, :] = folded
        out[members : members + 1, :] = gram[total : total + 1]
        out[members + 1 :, :] = blank

    found = lax.dot_general(
        jnp.concatenate(pieces_of(mean), axis=0).astype(jnp.bfloat16), onehot_ref[...],
        (((1,), (0,)), ((), ())), preferred_element_type=jnp.float32,
    )
    found = found[:places] + found[places : 2 * places] + found[2 * places :]
    for out, source, partner in ((stay_ref, 0, 0), (odd_ref, 1, 1 + 2 * core), (even_ref, 3, 2)):
        for j in range(held):
            n = source * held + j
            center = jnp.sum(
                jnp.where(hits[n], found[:, n * LANES : (n + 1) * LANES], 0.0), axis=0, keepdims=True
            )
            out[pl.ds(members + 1 + partner * held + j, 1), :] = center


def spread_row(row):
    return jnp.broadcast_to(row, (8, LANES))


def eliminate(rows):
    count = len(rows)
    rows = list(rows)
    sub = lax.broadcasted_iota(jnp.int32, (8, LANES), 0)
    for b in range(count):
        columns = [
            [jnp.broadcast_to(rows[i][:, 8 * b + k : 8 * b + k + 1], (8, LANES)) for k in range(8)]
            for i in range(b, count)
        ]
        for j in range(8):
            scale = lax.rsqrt(spread_row(columns[0][j][j : j + 1, :]))
            upper = spread_row(rows[b][j : j + 1, :]) * scale
            lower = columns[0][j] * scale
            factors = [spread_row(lower[k : k + 1, :]) for k in range(8)]
            for i in range(b, count):
                here = lower if i == b else columns[i - b][j] * scale
                if i == b:
                    rows[b] = jnp.where(sub == j, upper, rows[b] - jnp.where(sub > j, here, 0.0) * upper)
                else:
                    rows[i] = rows[i] - here * upper
                for k in range(j + 1, 8):
                    columns[i - b][k] = columns[i - b][k] - here * factors[k]
    return rows


def analysis_kernel(
    which_ref, send_ref, own_ref, other_ref, edge_ref, small_ref, kept, odd, swapped, even,
    analysis_ref, innovation_ref, mixing_ref, center_ref, pieces_ref, *, units, obs_rows,
):
    block, core = which_ref[0], which_ref[1]
    members, fields, cells = analysis_ref.shape
    total = 2 * members
    strip_rows = fields * members
    for f in range(fields):
        for half, state in enumerate((own_ref, other_ref)):
            rows = slice(f * members, (f + 1) * members)
            edges = slice(half * strip_rows + f * members, half * strip_rows + (f + 1) * members)
            for lanes, value in (
                (slice(0, LANES), edge_ref[edges, :LANES]),
                (slice(LANES, cells - LANES), state[rows, LANES : cells - LANES]),
                (slice(cells - LANES, cells), edge_ref[edges, LANES:]),
            ):
                for p, piece in enumerate(halves_of(value)):
                    at = (f * 2 + p) * total + half * members
                    pieces_ref[at : at + members, lanes] = piece
    head = members + 1
    sums = (kept[:head, :] + even[:head, :]) + (odd[:head, :] + swapped[:head, :])
    returned = kept.shape[0] - head
    center_ref[:returned, :] = kept[head:, :]
    center_ref[returned : 2 * returned, :] = jnp.where(core == 0, odd[head:, :], swapped[head:, :])
    center_ref[2 * returned : 3 * returned, :] = even[head:, :]
    center_ref[3 * returned :, :] = jnp.where(core == 0, swapped[head:, :], odd[head:, :])
    lane = lax.broadcasted_iota(jnp.int32, (8, LANES), 1)
    sub = lax.broadcasted_iota(jnp.int32, (8, LANES), 0)
    shifted = pltpu.roll(sums[:members], LANES - total, 1)
    rows = []
    for b in range(total // 8):
        at = 8 * b
        source = sums[at : at + 8] if at < members else shifted[at - members : at - members + 8]
        own = jnp.where(lane == sub + at, total - 1.0, 0.0)
        unit = jnp.where(lane == sub + at + total, 1.0, 0.0)
        rows.append(jnp.where(lane < total, source + own, unit))
    rows = eliminate(rows)
    cross = sums[members : members + 1]
    inverse = [jnp.where(lane < total, pltpu.roll(r, LANES - total, 1), 0.0) for r in rows]
    carried = [jnp.sum(r * cross, axis=1, keepdims=True) for r in inverse]
    row_sums = [jnp.sum(r, axis=1, keepdims=True) for r in inverse]
    row_means = [r * (1.0 / total) for r in row_sums]
    weights = jnp.sum(sum(r * c for r, c in zip(inverse, carried)), axis=0, keepdims=True)
    column_mean = jnp.sum(sum(inverse), axis=0, keepdims=True) * (1.0 / total)
    grand = jnp.sum(sum(row_means), axis=0, keepdims=True) * (1.0 / total)
    weights = weights - jnp.sum(sum(r * c for r, c in zip(row_means, carried)), axis=0, keepdims=True)
    root = math.sqrt(total - 1.0)
    add = weights + 1.0 / total - root * (column_mean - grand)
    for b in range(total // 8):
        mixing_ref[8 * b : 8 * b + 8, :] = root * (inverse[b] - row_means[b]) + add
    own_rows = mixing_ref[pl.ds(pl.multiple_of(core * members, 8), members), :]
    rolled = pltpu.roll(own_rows, LANES - members, 1)
    to_own = jnp.where(core == 0, own_rows, rolled)[:, :members]
    to_other = jnp.where(core == 0, rolled, own_rows)[:, :members]
    high, rest = halves_of(jnp.concatenate([to_own, to_other], axis=1))
    mixing = jnp.concatenate(
        [jnp.concatenate([high, high], axis=1), jnp.concatenate([rest, rest], axis=1)], axis=0
    )
    for f in range(fields):
        product = jnp.dot(
            mixing, pieces_ref[f * 2 * total : (f + 1) * 2 * total, :], preferred_element_type=jnp.float32
        )
        analysis_ref[:, f, :] = product[:members] + product[members:]

    owners = send_ref.shape[1]
    held = owners // 16
    wide = obs_rows * LANES
    slot = lax.broadcasted_iota(jnp.int32, (1, wide), 1)
    centers = jnp.zeros((1, wide), jnp.float32)
    start = jnp.int32(0)
    for owner in range(owners):
        way = [jnp.bitwise_xor(digit_of(block, unit), (owner // unit) % 4) for unit in units]
        row = way[-1] * held
        if len(units) > 2:
            row = row + sum(step * 4**s for s, step in enumerate(way[:-2]))
        size = 4 * held
        for step in reversed(way[1:-1]):
            row = row + step * size
            size = size * 4
        row = row + way[0] * returned
        line = center_ref[pl.ds(row, 1), :]
        line = jnp.concatenate([line] + [jnp.zeros((1, LANES), jnp.float32)] * (obs_rows - 1), axis=1)
        moved = pltpu.roll(line, within(start - way[-2] * CAP, wide), 1)
        end = start + send_ref[0, owner]
        centers = jnp.where((slot >= start) & (slot < end), moved, centers)
        start = end
    for r in range(obs_rows):
        center = centers[:, r * LANES : (r + 1) * LANES]
        at = small_ref.shape[0] - 2 * obs_rows + r
        value, sigma = small_ref[at : at + 1, :], small_ref[at + obs_rows : at + obs_rows + 1, :]
        innovation_ref[r : r + 1, :] = (value - center) / sigma


def shards(
    ensemble, speed, direction, couple, obs_place, obs_field, obs_value, obs_sigma, send_count
):
    members, fields, cells = ensemble.shape
    owners = lax.axis_size("cells")
    total = members * lax.axis_size("members")
    obs = obs_place.shape[0]
    obs_rows = obs // LANES
    tiles = cells // LANES
    places = fields * tiles
    units = stage_units(owners)
    block = lax.axis_index("cells").astype(jnp.int32)
    core = lax.axis_index("members").astype(jnp.int32)
    which = jnp.stack([block, core])
    small = (
        speed.reshape(tiles, LANES), direction.reshape(tiles, LANES),
        *(x.reshape(obs_rows, LANES) for x in (obs_place, obs_field, obs_value, obs_sigma)),
    )
    whole = pl.BlockSpec(memory_space=pltpu.VMEM)
    scalars = pl.BlockSpec(memory_space=pltpu.SMEM)
    params = pltpu.CompilerParams(vmem_limit_bytes=VMEM_BYTES)
    real = jnp.float32

    table_rows = 8 * (owners // GROUPS)
    part = table_rows // 4
    other = swap_cores(ensemble, owners)
    rows_of = lambda count: pl.BlockSpec((count, LANES), lambda i: (0, 0))
    small_rows = 2 * tiles + 2 * obs_rows
    strips = pl.pallas_call(
        strips_kernel,
        out_shape=jax.ShapeDtypeStruct((8, LANES), real),
        in_specs=[whole],
        out_specs=whole,
        compiler_params=params,
        name="strips",
    )(ensemble)
    kept, to_odd, to_even, small = pl.pallas_call(
        functools.partial(pack_kernel, rows=obs_rows, cells=cells, fields=fields),
        out_shape=(jax.ShapeDtypeStruct((part, LANES), real),) * 3
        + (jax.ShapeDtypeStruct((small_rows, LANES), real),),
        grid=(1,),
        in_specs=[scalars, scalars] + [rows_of(x.shape[0]) for x in small],
        out_specs=(whole,) * 4,
        scratch_shapes=[pltpu.VMEM((table_rows, LANES), real)],
        compiler_params=params,
        name="pack",
    )(which, send_count, *small)
    to_odd, to_even = pl.pallas_call(
        join_kernel,
        out_shape=(jax.ShapeDtypeStruct((16 + part, LANES), real),) * 2,
        in_specs=[whole] * 4,
        out_specs=(whole,) * 2,
        compiler_params=params,
        name="join",
    )(strips, other, to_odd, to_even)

    def forecast(half):
        return pl.pallas_call(
            forecast_kernel,
            out_shape=(
                jax.ShapeDtypeStruct((strip_rows, cells), real),
                jax.ShapeDtypeStruct((strip_rows, LANES), real),
                jax.ShapeDtypeStruct((places * 8, LANES), real),
            ),
            in_specs=[scalars] + [whole] * 2,
            out_specs=(whole,) * 3,
            scratch_shapes=[
                pltpu.VMEM((fields * 8, cells), real),
                pltpu.VMEM((8 * (2 * STEPS + 1), cells), real),
            ],
            compiler_params=params,
            cost_estimate=pl.CostEstimate(
                flops=80 * strip_rows * cells, bytes_accessed=8 * strip_rows * cells, transcendentals=0
            ),
            name="forecast",
        )(couple, half, small)

    strip_rows = fields * members
    own_forecast = forecast(ensemble)
    carried = []
    for n, unit in enumerate(units):
        arrived = exchange(to_odd, to_even, owners, unit)
        if n + 1 < len(units):
            to_odd, to_even, kept = pl.pallas_call(
                functools.partial(regroup_kernel, unit=unit, into_lanes=n + 2 == len(units)),
                out_shape=tuple(jax.ShapeDtypeStruct(x.shape, real) for x in (to_odd, to_even, kept)),
                in_specs=[scalars] + [whole] * 4 + [pl.BlockSpec(memory_space=pl.ANY)],
                out_specs=(whole,) * 3,
                compiler_params=params,
                name="regroup",
            )(which, kept, *arrived, own_forecast[2])
            carried.append(to_odd)
    other_forecast = forecast(other)

    held = kept.shape[0] // 8
    sums_rows = -(-(members + 1 + 4 * held) // 8) * 8
    all_slots = 4 * held * LANES
    sums = jax.ShapeDtypeStruct((sums_rows, LANES), real)
    stay, to_odd, to_even, edges = pl.pallas_call(
        functools.partial(sums_kernel, owners=owners, units=units, fields=fields),
        out_shape=(sums, sums, sums, jax.ShapeDtypeStruct((2 * strip_rows, 2 * LANES), real)),
        in_specs=[scalars, scalars] + [whole] * (11 + len(carried)),
        out_specs=(whole,) * 4,
        scratch_shapes=[
            pltpu.VMEM((2 * strip_rows, LANES), real),
            pltpu.VMEM((LANES, all_slots), jnp.bfloat16),
            pltpu.VMEM((6 * places, all_slots), jnp.bfloat16),
            pltpu.VMEM((2 * (total + 16), fields * cells), jnp.bfloat16),
        ],
        compiler_params=params,
        name="sums",
    )(
        which, couple, small, *own_forecast, *other_forecast, kept, *arrived, *carried,
    )

    head = members + 1
    used = head + 4 * held
    for n, unit in enumerate(reversed(units)):
        odd, swapped, even = exchange(to_odd, to_even, owners, unit)
        if n + 1 < len(units):
            added = (stay + even) + (odd + swapped)
            if n > 0:
                first = jnp.where(core == 0, odd, swapped)
                third = jnp.where(core == 0, swapped, odd)
                added = jnp.concatenate(
                    [added[:head]] + [x[head:used] for x in (stay, first, even, third)], axis=0
                )
                used = added.shape[0]
            stay = to_odd = to_even = added

    analysis, innovation = pl.pallas_call(
        functools.partial(analysis_kernel, units=units, obs_rows=obs_rows),
        out_shape=(
            jax.ShapeDtypeStruct((members, fields, cells), real),
            jax.ShapeDtypeStruct((obs_rows, LANES), real),
        ),
        in_specs=[scalars, scalars] + [whole] * 8,
        out_specs=(whole, whole),
        scratch_shapes=[
            pltpu.VMEM((total, LANES), real),
            pltpu.VMEM((4 * (stay.shape[0] - head), LANES), real),
            pltpu.VMEM((fields * 2 * total, cells), jnp.bfloat16),
        ],
        compiler_params=params,
        name="analysis",
    )(
        which, send_count, own_forecast[0], other_forecast[0], edges, small,
        stay, odd, swapped, even,
    )
    return (analysis, innovation.reshape(obs))


def solution(mesh):
    return jax.shard_map(
        shards,
        mesh=mesh,
        in_specs=(
            P("members", None, "cells"),
            P("cells"),
            P("cells"),
            P(),
            P("cells"),
            P("cells"),
            P("cells"),
            P("cells"),
            P("cells", None),
        ),
        out_specs=(P("members", None, "cells"), P("cells")),
        check_vma=False,
    )
```

```python
import functools
import math

import jax
import jax.numpy as jnp
from jax import lax
from jax.experimental import pallas as pl
from jax.experimental.pallas import tpu as pltpu
from jax.sharding import PartitionSpec as P

STEPS = 4
DIFFUSION = 0.05
LANES = 128
CAP = 32
GROUPS = LANES // CAP
BOTH = ("cells", "members")
EXACT = lax.Precision.HIGHEST
VMEM_BYTES = 48 * 1024 * 1024


def core_pairs(owners, place):
    pairs = []
    for block in range(owners):
        for core in range(2):
            to_block, to_core = place(block, core)
            pairs.append((block * 2 + core, to_block * 2 + to_core))
    return pairs


def stage_units(owners):
    units = []
    unit = 1
    while unit < owners:
        units.append(unit)
        unit *= 4
    if unit != owners or len(units) < 2:
        raise ValueError("blocks not 4**n")
    return units


def swap_cores(x, owners):
    return lax.ppermute(x, BOTH, core_pairs(owners, lambda block, core: (block, 1 - core)))


def exchange(to_odd, to_even, owners, unit):
    odd = lax.ppermute(
        to_odd, BOTH, core_pairs(owners, lambda block, core: (block ^ (unit * (1 + 2 * core)), core))
    )
    even = lax.ppermute(
        to_even, BOTH, core_pairs(owners, lambda block, core: (block ^ (unit * 2), core))
    )
    return odd, swap_cores(odd, owners), even


def digit_of(block, unit):
    return jnp.bitwise_and(lax.shift_right_logical(block, jnp.int32(unit.bit_length() - 1)), 3)


def here():
    return lax.axis_index("cells"), lax.axis_index("members")


def table_row(number, count):
    return (number % 4) * (count // 4) + number // 4


def strips_of(ref):
    fields, cells = ref.shape[1:]
    lane = lax.broadcasted_iota(jnp.int32, (1, LANES), 1)
    ends = [jnp.where(lane < STEPS, ref[:, f, :LANES], ref[:, f, cells - LANES :]) for f in range(fields)]
    ends = jnp.transpose(jnp.concatenate(ends, axis=0))
    return jnp.concatenate([ends[:STEPS, :], ends[LANES - STEPS :, :]], axis=0)


def pack_kernel(
    send_ref, speed_ref, flag_ref, place_ref, field_ref, value_ref, sigma_ref,
    kept_ref, odd_ref, even_ref, small_ref, table_ref, *, rows, cells, fields,
):
    block, core = here()
    tiles = cells // LANES
    speed, value, sigma = speed_ref[...], value_ref[...], sigma_ref[...]
    flag, place, field = (ref[...].astype(jnp.float32) for ref in (flag_ref, place_ref, field_ref))
    at = 0
    for part in (speed, flag, value, sigma):
        small_ref[at : at + part.shape[0], :] = part
        at += part.shape[0]
    lane = lax.broadcasted_iota(jnp.int32, (1, LANES), 1)
    low = lane < LANES // 2
    toward_left = speed * flag
    toward_right = speed - toward_left
    edge_left = jnp.where(low, toward_left[:1], toward_left[tiles - 1 :])
    edge_right = jnp.where(low, toward_right[:1], toward_right[tiles - 1 :])
    ids = field * float(cells) + place
    weight = 1.0 / (sigma * sigma)
    pull = weight * value
    sub = lax.broadcasted_iota(jnp.int32, (8, LANES), 0)
    empty = jnp.where(sub == 0, -1.0, 0.0)
    empty = jnp.where(sub == 3, edge_left, jnp.where(sub == 4, edge_right, empty))
    listed = [
        jnp.where(sub == 0, ids[r : r + 1], jnp.where(sub == 1, weight[r : r + 1], pull[r : r + 1]))
        for r in range(rows)
    ]
    owners = send_ref.shape[1]
    count = owners // GROUPS
    sends = jnp.broadcast_to(send_ref[...], (8, owners)).astype(jnp.bfloat16)
    sender = lax.broadcasted_iota(jnp.int32, (owners, LANES), 0)
    group = lax.broadcasted_iota(jnp.int32, (owners, LANES), 1) // CAP
    slot = lax.broadcasted_iota(jnp.int32, (8, LANES), 1) % CAP
    one = lambda mask: jnp.where(mask, 1.0, 0.0)
    which = jnp.concatenate(
        [one(sender < group * count + r) for r in range(count)] + [one(sender == group * count + r) for r in range(count)],
        axis=1,
    )
    found = jnp.dot(sends, which.astype(jnp.bfloat16), preferred_element_type=jnp.float32).astype(jnp.int32)
    for r in range(count):
        index = found[:, r * LANES : (r + 1) * LANES] + slot
        held = found[:, (count + r) * LANES : (count + r + 1) * LANES]
        block_of = empty
        inside = (slot < held) & (sub < 3)
        for w in range(rows):
            moved = jnp.take_along_axis(
                listed[w], jnp.bitwise_and(index, LANES - 1), axis=1, mode="promise_in_bounds"
            )
            block_of = jnp.where(inside & (lax.shift_right_logical(index, 7) == w), moved, block_of)
        row = 8 * table_row(r, count)
        table_ref[row : row + 8, :] = block_of
    part = kept_ref.shape[0]
    digit = digit_of(block, 1)
    for out, partner in ((kept_ref, 0), (odd_ref, 1 + 2 * core), (even_ref, 2)):
        out[...] = table_ref[pl.ds(pl.multiple_of(jnp.bitwise_xor(digit, partner) * part, 8), part), :]


def strips_kernel(ensemble_ref, out_ref):
    out_ref[...] = strips_of(ensemble_ref)


def join_kernel(own_ref, other_ref, odd_part, even_part, odd_ref, even_ref):
    strips = jnp.concatenate([own_ref[...], strips_of(other_ref)], axis=0)
    for part, out in ((odd_part, odd_ref), (even_part, even_ref)):
        out[:16, :] = strips
        out[16:, :] = part[...]


def incoming(digit, core, odd, swapped):
    sub = lax.broadcasted_iota(jnp.int32, (8, LANES), 0)
    low = lax.broadcasted_iota(jnp.int32, (8, LANES), 1) < LANES // 2
    direct = jnp.bitwise_xor(jnp.bitwise_and(digit, 1), core) == 0
    result = []
    for part, other_part in ((0, 1), (1, 0), (2, 2)):
        mine = odd[8 * part : 8 * part + 8, :]
        others = swapped[8 * other_part : 8 * other_part + 8, :]
        from_right = jnp.where(direct, mine, others)
        from_left = jnp.where(direct, others, mine)
        result.append(jnp.where(sub < STEPS if part < 2 else low, from_right, from_left))
    return result


def regroup_kernel(
    kept, odd, swapped, even, _, to_odd, to_even, stay, *, unit, into_lanes,
):
    block, core = here()
    after = digit_of(block, unit * 4)
    own, other, coefs = incoming(digit_of(block, unit), core, odd, swapped)
    sub = lax.broadcasted_iota(jnp.int32, (8, LANES), 0)
    lane_group = lax.broadcasted_iota(jnp.int32, (8, LANES), 1) // CAP
    held = kept.shape[0] // 8

    def received(k, at):
        if k == 0:
            return kept[pl.ds(at, 8), :]
        if k == 2:
            return even[pl.ds(16 + at, 8), :]
        mine, others = odd[pl.ds(16 + at, 8), :], swapped[pl.ds(16 + at, 8), :]
        return jnp.where(core == k // 2, mine, others)

    for target in (to_odd, to_even):
        target[0:8, :] = own
        target[8:16, :] = other
    for target, base, partner in ((to_odd, 16, 1 + 2 * core), (to_even, 16, 2), (stay, 0, 0)):
        wanted = jnp.bitwise_xor(after, partner)
        if into_lanes:
            for j in range(held):
                merged = coefs
                for k in range(4):
                    moved = pltpu.roll(received(k, 8 * j), jnp.bitwise_and(k - wanted, 3) * CAP, 1)
                    merged = jnp.where((lane_group == k) & (sub < 3), moved, merged)
                target[base + 8 * j : base + 8 * j + 8, :] = merged
        else:
            rest = held // 4
            for k in range(4):
                for r in range(rest):
                    at = pl.multiple_of((wanted * rest + r) * 8, 8)
                    row = base + 8 * (r * 4 + k)
                    target[row : row + 8, :] = jnp.where(sub < 3, received(k, at), coefs)


def fill_powers(couple_ref, powers_ref):
    fields = couple_ref.shape[0]
    mix = [
        [
            jnp.broadcast_to(couple_ref[f : f + 1, g : g + 1], (1, LANES)) + (1.0 if f == g else 0.0)
            for g in range(fields)
        ]
        for f in range(fields)
    ]
    for _ in range(2):
        mix = [
            [sum(mix[f][h] * mix[h][g] for h in range(fields)) for g in range(fields)]
            for f in range(fields)
        ]
    for f in range(fields):
        for g in range(fields):
            powers_ref[f * fields + g : f * fields + g + 1, :] = mix[f][g]


def powers_of(powers_ref, fields):
    return [[powers_ref[f * fields + g : f * fields + g + 1, :] for g in range(fields)] for f in range(fields)]


def transport(x, from_left, stay, from_right):
    for _ in range(STEPS):
        x = from_left * pltpu.roll(x, 1, 1) + stay * x + from_right * pltpu.roll(x, x.shape[1] - 1, 1)
    return x


def halves_of(x):
    high = x.astype(jnp.bfloat16)
    return high, (x - high.astype(jnp.float32)).astype(jnp.bfloat16)


def fill_band(small_ref, band_ref, cells):
    tiles = cells // LANES
    speed = small_ref[:tiles, :]
    toward_left = speed * small_ref[tiles : 2 * tiles, :]
    toward_right = speed - toward_left

    def row_of(x):
        return jnp.concatenate([x[t : t + 1] for t in range(tiles)], axis=1)

    step = {
        -1: row_of(toward_left + DIFFUSION),
        0: row_of(1.0 - 2.0 * DIFFUSION - speed),
        1: row_of(toward_right + DIFFUSION),
    }
    reach = dict(step)
    for _ in range(STEPS - 1):
        longer = {}
        for e in step:
            for d in reach:
                term = step[e] * (pltpu.roll(reach[d], -e % cells, 1) if e else reach[d])
                longer[d + e] = longer[d + e] + term if d + e in longer else term
        reach = longer
    row = lax.broadcasted_iota(jnp.int32, (LANES, LANES), 0)
    column = lax.broadcasted_iota(jnp.int32, (LANES, LANES), 1)
    ahead = row - column
    for t in range(tiles):
        rule = {d: reach[d][:, t * LANES : (t + 1) * LANES] for d in reach}

        def placed(distance, offsets):
            block = jnp.zeros(distance.shape, jnp.float32)
            for d in offsets:
                block = jnp.where(distance == d, rule[d], block)
            return block

        block = jnp.concatenate(
            [
                placed(ahead, range(-STEPS, STEPS + 1)),
                placed(ahead[:8] + LANES, range(1, STEPS + 1)),
                jnp.zeros((LANES - 16, LANES), jnp.float32),
                placed(ahead[LANES - 8 :] - LANES, range(-STEPS, 0)),
            ],
            axis=0,
        )
        for p, piece in enumerate(halves_of(block)):
            band_ref[2 * t * LANES : 2 * (t + 1) * LANES, p * LANES : (p + 1) * LANES] = piece


def fill_positions(send_ref, slots_ref):
    owners = send_ref.shape[1]
    count = owners // GROUPS
    rows = slots_ref.shape[0] // 2
    row = lax.broadcasted_iota(jnp.int32, (owners, owners), 0)
    column = lax.broadcasted_iota(jnp.int32, (owners, owners), 1)
    held = jnp.where(row == column, jnp.broadcast_to(send_ref[...], (owners, owners)), 0).astype(jnp.float32)
    held = jnp.broadcast_to(jnp.sum(held, axis=1, keepdims=True), (owners, LANES))
    ends = jnp.dot(
        jnp.where(column <= row, 1.0, 0.0).astype(jnp.bfloat16), held.astype(jnp.bfloat16),
        preferred_element_type=jnp.float32,
    )
    for r in range(rows):
        slot = (lax.broadcasted_iota(jnp.int32, (1, LANES), 1) + r * LANES).astype(jnp.float32)
        passed = ends <= slot
        owner = jnp.sum(jnp.where(passed, 1.0, 0.0), axis=0, keepdims=True).astype(jnp.int32)
        start = jnp.sum(jnp.where(passed, held, 0.0), axis=0, keepdims=True)
        group = lax.shift_right_logical(owner, count.bit_length() - 1)
        slots_ref[r : r + 1, :] = jnp.bitwise_and(owner, count - 1)
        slots_ref[rows + r : rows + r + 1, :] = group * CAP + (slot - start).astype(jnp.int32)


def forecast_kernel(extra_ref, source, from_ref, send_ref, state, edge, sums_ref, *refs, fields):
    members, _, cells = source.shape
    tiles = cells // LANES
    height = fields * members
    if len(refs) == 4:
        band_ref, powers_ref, split_ref, raw_ref = refs
        fill_powers(extra_ref, powers_ref)
        fill_band(from_ref, band_ref, cells)
    else:
        powers_ref, slots_ref, split_ref, raw_ref = (extra_ref,) + refs
        band_ref = from_ref
        fill_positions(send_ref, slots_ref)
    low = lax.broadcasted_iota(jnp.int32, (members, LANES), 1) < LANES // 2
    for f in range(fields):
        rows = slice(f * members, (f + 1) * members)
        raw_ref[rows, :] = source[:, f, :]
        x = raw_ref[rows, :]
        edge[rows, :] = jnp.where(
            low,
            pltpu.roll(x[:, :LANES], STEPS, 1),
            pltpu.roll(x[:, cells - LANES :], LANES // 2 + 3 * STEPS, 1),
        )
        for p, piece in enumerate(halves_of(x)):
            split_ref[p * height + f * members : p * height + (f + 1) * members, :] = piece
    mix = powers_of(powers_ref, fields)
    nearer = lax.broadcasted_iota(jnp.int32, (2 * height, LANES), 1) < LANES // 2
    for t in range(tiles):
        lanes, after, before = (
            slice(n % tiles * LANES, (n % tiles + 1) * LANES) for n in (t, t + 1, t - 1)
        )
        around = jnp.where(nearer, split_ref[:, after], split_ref[:, before])
        product = jnp.dot(
            jnp.concatenate([split_ref[:, lanes], around], axis=1),
            band_ref[2 * t * LANES : 2 * (t + 1) * LANES, :],
            preferred_element_type=jnp.float32,
        )
        moved = (
            product[height:, LANES:] + (product[:height, LANES:] + product[height:, :LANES])
        ) + product[:height, :LANES]
        for f in range(fields):
            value = sum(mix[f][g] * moved[g * members : (g + 1) * members] for g in range(fields))
            state[f * members : (f + 1) * members, lanes] = value
            place = (f * tiles + t) * 8
            sums_ref[place : place + 8, :] = sum(value[8 * i : 8 * i + 8] for i in range(members // 8))


def pieces_of(x):
    high = x.astype(jnp.bfloat16).astype(jnp.float32)
    rest = x - high
    middle = rest.astype(jnp.bfloat16).astype(jnp.float32)
    return high, middle, rest - middle


def sums_kernel(
    powers_ref, small_ref, own_state, own_edge, own_sums, other_state, other_edge, other_sums,
    kept, odd, swapped, even, *refs, owners, units, fields,
):
    carried = refs[: len(units) - 1]
    (
        stay_ref, odd_ref, even_ref, edge_ref, halo_ref, onehot_ref, spread_ref, split_ref,
    ) = refs[len(units) - 1 :]
    states, raw_edges = (own_state, other_state), (own_edge, other_edge)
    block, core = here()
    members = states[0].shape[0] // fields
    cells = states[0].shape[1]
    tiles = cells // LANES
    total = 2 * members
    places = fields * tiles
    has_left = (block > 0).astype(jnp.float32)
    has_right = (block < owners - 1).astype(jnp.float32)
    sub = lax.broadcasted_iota(jnp.int32, (8, LANES), 0)
    lane = lax.broadcasted_iota(jnp.int32, (1, LANES), 1)
    lane8 = lax.broadcasted_iota(jnp.int32, (8, LANES), 1)
    half_lanes = LANES // 2
    low = lane < half_lanes

    strips = incoming(digit_of(block, units[-1]), core, odd, swapped)
    for unit, earlier in reversed(list(zip(units, carried))):
        digit = digit_of(block, unit)
        rows = [earlier[8 * p : 8 * p + 8, :] for p in range(3)]
        picked = []
        for p in range(3):
            from_right = jnp.where(digit != 3, rows[p], strips[p])
            from_left = jnp.where(digit != 0, rows[p], strips[p])
            picked.append(jnp.where(sub < STEPS if p < 2 else lane8 < half_lanes, from_right, from_left))
        strips = picked

    right_first = half_lanes + 3 * STEPS
    strip_rows = fields * members
    for half in range(2):
        strip = strips[half]
        left = jnp.where(sub < STEPS, pltpu.roll(strip, STEPS, 0) * has_left, 0.0)
        at = right_first % 8
        right = jnp.where(
            (sub >= at) & (sub < at + STEPS), (pltpu.roll(strip, at, 0) if at else strip) * has_right, 0.0
        )
        gap = jnp.zeros((right_first - at - 8, LANES), jnp.float32)
        rest = jnp.zeros((LANES - (right_first - at) - 8, LANES), jnp.float32)
        halo_ref[half * strip_rows : (half + 1) * strip_rows, :] = jnp.transpose(
            jnp.concatenate([left, gap, right, rest], axis=0)
        )
    speed = small_ref[:tiles, :]
    toward_left = speed * small_ref[tiles : 2 * tiles, :]
    toward_right = speed - toward_left
    is_left = lane < STEPS
    is_right = (lane >= right_first) & (lane < right_first + STEPS)
    inside = jnp.where(is_left, has_left, jnp.where(is_right, has_right, 1.0))
    from_outside = (lane8 < STEPS) | ((lane8 >= right_first) & (lane8 < right_first + STEPS))

    def edge_row(rows, row):
        own = jnp.where(
            low, pltpu.roll(rows[:1], STEPS, 1), pltpu.roll(rows[tiles - 1 :], half_lanes + 3 * STEPS, 1)
        )
        left = pltpu.roll(strips[2][row : row + 1], STEPS, 1)
        right = pltpu.roll(strips[2][row : row + 1], right_first, 1)
        return jnp.where(is_left, left, jnp.where(is_right, right, own))

    edge_left = edge_row(toward_left, 3)
    edge_right = edge_row(toward_right, 4)
    from_left = jnp.broadcast_to((edge_left + DIFFUSION) * inside, (8, LANES))
    from_right = jnp.broadcast_to((edge_right + DIFFUSION) * inside, (8, LANES))
    stay = jnp.broadcast_to((1.0 - 2.0 * DIFFUSION - edge_left - edge_right) * inside, (8, LANES))
    mix = powers_of(powers_ref, fields)
    first_sums = [jnp.zeros((8, LANES), jnp.float32) for _ in range(fields)]
    last_sums = [jnp.zeros((8, LANES), jnp.float32) for _ in range(fields)]
    for half in range(2):
        state, edge = states[half], raw_edges[half]
        for i in range(members // 8):
            moved = []
            for f in range(fields):
                at = f * members + 8 * i
                x = edge[at : at + 8, :]
                x = jnp.where(from_outside, halo_ref[half * strip_rows + at : half * strip_rows + at + 8, :], x)
                moved.append(transport(x, from_left, stay, from_right))
            for f in range(fields):
                at = f * members + 8 * i
                value = sum(mix[f][g] * moved[g] for g in range(fields))
                first_tile = jnp.where(lane8 < STEPS, pltpu.roll(value, LANES - STEPS, 1), state[at : at + 8, :LANES])
                last_tile = jnp.where(
                    lane8 >= LANES - STEPS,
                    pltpu.roll(value, LANES - right_first, 1),
                    state[at : at + 8, cells - LANES :],
                )
                edge_ref[half * strip_rows + at : half * strip_rows + at + 8, :LANES] = first_tile
                edge_ref[half * strip_rows + at : half * strip_rows + at + 8, LANES:] = last_tile
                first_sums[f] = first_sums[f] + first_tile
                last_sums[f] = last_sums[f] + last_tile
    means = []
    for f in range(fields):
        for t in range(tiles):
            at = (f * tiles + t) * 8
            if t == 0:
                partial = first_sums[f]
            elif t == tiles - 1:
                partial = last_sums[f]
            else:
                partial = own_sums[at : at + 8, :] + other_sums[at : at + 8, :]
            means.append(jnp.sum(partial, axis=0, keepdims=True))
    mean = jnp.concatenate(means, axis=0) * (1.0 / total)

    place_ids = lax.broadcasted_iota(jnp.int32, (places, LANES), 0)
    lane_ids = lax.broadcasted_iota(jnp.int32, (LANES, LANES), 0)
    held = kept.shape[0] // 8
    sources = [(kept, 8 * j) for j in range(held)]
    for source, base in ((odd, 16), (swapped, 16), (even, 16)):
        sources += [(source, base + 8 * j) for j in range(held)]
    hits = []
    for n, (source, at) in enumerate(sources):
        local = source[at : at + 1, :].astype(jnp.int32)
        hit = place_ids == lax.shift_right_arithmetic(local, 7)
        hits.append(hit)
        onehot = (lane_ids == jnp.bitwise_and(local, LANES - 1)).astype(jnp.float32)
        lanes = slice(n * LANES, (n + 1) * LANES)
        onehot_ref[:, lanes] = onehot.astype(jnp.bfloat16)
        weight, pull = source[at + 1 : at + 2, :], source[at + 2 : at + 3, :]
        stack = [jnp.where(hit, piece, 0.0) for piece in pieces_of(weight) + pieces_of(pull)]
        spread_ref[:, lanes] = jnp.concatenate(stack, axis=0).astype(jnp.bfloat16)
    placed = lax.dot_general(
        spread_ref[...], onehot_ref[...], (((1,), (1,)), ((), ())), preferred_element_type=jnp.float32
    )
    placed = [placed[p * places : (p + 1) * places] for p in range(6)]
    weight = placed[0] + placed[1] + placed[2]
    pull = placed[3] + placed[4] + placed[5] - weight * mean

    root = jnp.sqrt(weight)
    pull = jnp.where(weight > 0.0, pull * lax.rsqrt(jnp.where(weight > 0.0, weight, 1.0)), 0.0)
    sub16 = lax.broadcasted_iota(jnp.int32, (16, LANES), 0)
    depth = total + 16

    def put(row, lanes, value):
        for p, piece in enumerate(halves_of(value)):
            split_ref[pl.ds(row + p * depth, value.shape[0]), lanes] = piece

    for f in range(fields):
        for t in range(tiles):
            at = f * tiles + t
            lanes = slice(t * LANES, (t + 1) * LANES)
            into = slice(at * LANES, (at + 1) * LANES)
            for half in range(2):
                if t in (0, tiles - 1):
                    column = slice(0, LANES) if t == 0 else slice(LANES, 2 * LANES)
                    value = edge_ref[half * strip_rows + f * members : half * strip_rows + (f + 1) * members, column]
                else:
                    value = states[half][f * members : (f + 1) * members, lanes]
                anomaly = (value - mean[at : at + 1]) * root[at : at + 1]
                side = core if half == 0 else 1 - core
                put(pl.multiple_of(side * members, 16), into, anomaly)
            put(total, into, jnp.where(sub16 == 0, pull[at : at + 1], 0.0))
    products = lax.dot_general(
        split_ref[...], split_ref[...], (((1,), (1,)), ((), ())), preferred_element_type=jnp.float32
    )
    gram = sum(
        products[p * depth : p * depth + total + 8, q * depth : q * depth + total]
        for p, q in ((1, 1), (1, 0), (0, 1), (0, 0))
    )
    gram = jnp.concatenate([gram, jnp.zeros((total + 8, LANES - total), jnp.float32)], axis=1)
    folded = gram[:members] + pltpu.roll(gram[members:total], total, 1)
    blank = jnp.zeros((stay_ref.shape[0] - members - 1, LANES), jnp.float32)
    for out in (stay_ref, odd_ref, even_ref):
        out[:members, :] = folded
        out[members : members + 1, :] = gram[total : total + 1]
        out[members + 1 :, :] = blank

    found = lax.dot_general(
        jnp.concatenate(pieces_of(mean), axis=0).astype(jnp.bfloat16), onehot_ref[...],
        (((1,), (0,)), ((), ())), preferred_element_type=jnp.float32,
    )
    found = found[:places] + found[places : 2 * places] + found[2 * places :]
    for out, source, partner in ((stay_ref, 0, 0), (odd_ref, 1, 1 + 2 * core), (even_ref, 3, 2)):
        for j in range(held):
            n = source * held + j
            center = jnp.sum(
                jnp.where(hits[n], found[:, n * LANES : (n + 1) * LANES], 0.0), axis=0, keepdims=True
            )
            out[pl.ds(members + 1 + partner * held + j, 1), :] = center


def spread_row(row):
    return jnp.broadcast_to(row, (8, LANES))


def eliminate(rows):
    count = len(rows)
    rows = list(rows)
    sub = lax.broadcasted_iota(jnp.int32, (8, LANES), 0)
    for b in range(count):
        columns = [
            [jnp.broadcast_to(rows[i][:, 8 * b + k : 8 * b + k + 1], (8, LANES)) for k in range(8)]
            for i in range(b, count)
        ]
        for j in range(8):
            scale = lax.rsqrt(spread_row(columns[0][j][j : j + 1, :]))
            upper = spread_row(rows[b][j : j + 1, :]) * scale
            lower = columns[0][j] * scale
            factors = [spread_row(lower[k : k + 1, :]) for k in range(8)]
            for i in range(b, count):
                here = lower if i == b else columns[i - b][j] * scale
                if i == b:
                    rows[b] = jnp.where(sub == j, upper, rows[b] - jnp.where(sub > j, here, 0.0) * upper)
                else:
                    rows[i] = rows[i] - here * upper
                for k in range(j + 1, 8):
                    columns[i - b][k] = columns[i - b][k] - here * factors[k]
    return rows


def analysis_kernel(
    own_ref, other_ref, edge_ref, small_ref, slots_ref, kept, odd, swapped, even,
    analysis_ref, innovation_ref, mixing_ref, center_ref, pieces_ref, *, units, obs_rows, count,
):
    block, core = here()
    members, fields, cells = analysis_ref.shape
    total = 2 * members
    strip_rows = fields * members
    for f in range(fields):
        for half, state in enumerate((own_ref, other_ref)):
            rows = slice(f * members, (f + 1) * members)
            edges = slice(half * strip_rows + f * members, half * strip_rows + (f + 1) * members)
            for lanes, value in (
                (slice(0, LANES), edge_ref[edges, :LANES]),
                (slice(LANES, cells - LANES), state[rows, LANES : cells - LANES]),
                (slice(cells - LANES, cells), edge_ref[edges, LANES:]),
            ):
                for p, piece in enumerate(halves_of(value)):
                    at = (f * 2 + p) * total + half * members
                    pieces_ref[at : at + members, lanes] = piece
    head = members + 1
    sums = (kept[:head, :] + even[:head, :]) + (odd[:head, :] + swapped[:head, :])
    returned = kept.shape[0] - head
    center_ref[:returned, :] = kept[head:, :]
    center_ref[returned : 2 * returned, :] = jnp.where(core == 0, odd[head:, :], swapped[head:, :])
    center_ref[2 * returned : 3 * returned, :] = even[head:, :]
    center_ref[3 * returned :, :] = jnp.where(core == 0, swapped[head:, :], odd[head:, :])
    lane = lax.broadcasted_iota(jnp.int32, (8, LANES), 1)
    sub = lax.broadcasted_iota(jnp.int32, (8, LANES), 0)
    shifted = pltpu.roll(sums[:members], LANES - total, 1)
    rows = []
    for b in range(total // 8):
        at = 8 * b
        source = sums[at : at + 8] if at < members else shifted[at - members : at - members + 8]
        own = jnp.where(lane == sub + at, total - 1.0, 0.0)
        unit = jnp.where(lane == sub + at + total, 1.0, 0.0)
        rows.append(jnp.where(lane < total, source + own, unit))
    rows = eliminate(rows)
    cross = sums[members : members + 1]
    inverse = [jnp.where(lane < total, pltpu.roll(r, LANES - total, 1), 0.0) for r in rows]
    carried = [jnp.sum(r * cross, axis=1, keepdims=True) for r in inverse]
    row_sums = [jnp.sum(r, axis=1, keepdims=True) for r in inverse]
    row_means = [r * (1.0 / total) for r in row_sums]
    weights = jnp.sum(sum(r * c for r, c in zip(inverse, carried)), axis=0, keepdims=True)
    column_mean = jnp.sum(sum(inverse), axis=0, keepdims=True) * (1.0 / total)
    grand = jnp.sum(sum(row_means), axis=0, keepdims=True) * (1.0 / total)
    weights = weights - jnp.sum(sum(r * c for r, c in zip(row_means, carried)), axis=0, keepdims=True)
    root = math.sqrt(total - 1.0)
    add = weights + 1.0 / total - root * (column_mean - grand)
    for b in range(total // 8):
        mixing_ref[8 * b : 8 * b + 8, :] = root * (inverse[b] - row_means[b]) + add
    own_rows = mixing_ref[pl.ds(pl.multiple_of(core * members, 8), members), :]
    rolled = pltpu.roll(own_rows, LANES - members, 1)
    to_own = jnp.where(core == 0, own_rows, rolled)[:, :members]
    to_other = jnp.where(core == 0, rolled, own_rows)[:, :members]
    high, rest = halves_of(jnp.concatenate([to_own, to_other], axis=1))
    mixing = jnp.concatenate(
        [jnp.concatenate([high, high], axis=1), jnp.concatenate([rest, rest], axis=1)], axis=0
    )
    for f in range(fields):
        product = jnp.dot(
            mixing, pieces_ref[f * 2 * total : (f + 1) * 2 * total, :], preferred_element_type=jnp.float32
        )
        analysis_ref[:, f, :] = product[:members] + product[members:]

    held = count // 4
    lane_group = lane // CAP
    table = []
    for r in range(count):
        merged = jnp.zeros((1, LANES), jnp.float32)
        for group in range(GROUPS):
            owner = group * count + r
            way = [jnp.bitwise_xor(digit_of(block, unit), (owner // unit) % 4) for unit in units]
            row = way[-1] * held
            if len(units) > 2:
                row = row + sum(step * 4**n for n, step in enumerate(way[:-2]))
            size = 4 * held
            for step in reversed(way[1:-1]):
                row = row + step * size
                size = size * 4
            row = row + way[0] * returned
            line = center_ref[pl.ds(row, 1), :]
            moved = pltpu.roll(line, jnp.bitwise_and(group - way[-2], 3) * CAP, 1)
            merged = jnp.where(lane_group[:1] == group, moved, merged)
        table.append(jnp.broadcast_to(merged, (8, LANES)))
    for r in range(obs_rows):
        center = jnp.zeros((8, LANES), jnp.float32)
        lanes = jnp.broadcast_to(slots_ref[obs_rows + r : obs_rows + r + 1, :], (8, LANES))
        for n in range(count):
            found = jnp.take_along_axis(table[n], lanes, axis=1, mode="promise_in_bounds")
            center = jnp.where(slots_ref[r : r + 1, :] == n, found, center)
        center = center[:1]
        at = small_ref.shape[0] - 2 * obs_rows + r
        value, sigma = small_ref[at : at + 1, :], small_ref[at + obs_rows : at + obs_rows + 1, :]
        innovation_ref[r : r + 1, :] = (value - center) / sigma


def shards(
    ensemble, speed, direction, couple, obs_place, obs_field, obs_value, obs_sigma, send_count
):
    members, fields, cells = ensemble.shape
    owners = lax.axis_size("cells")
    total = members * lax.axis_size("members")
    obs = obs_place.shape[0]
    obs_rows = obs // LANES
    tiles = cells // LANES
    places = fields * tiles
    units = stage_units(owners)
    block = lax.axis_index("cells").astype(jnp.int32)
    core = lax.axis_index("members").astype(jnp.int32)
    small = (
        speed.reshape(tiles, LANES), direction.reshape(tiles, LANES),
        *(x.reshape(obs_rows, LANES) for x in (obs_place, obs_field, obs_value, obs_sigma)),
    )
    whole = pl.BlockSpec(memory_space=pltpu.VMEM)
    params = pltpu.CompilerParams(vmem_limit_bytes=VMEM_BYTES)
    real = jnp.float32

    table_rows = 8 * (owners // GROUPS)
    part = table_rows // 4
    other = swap_cores(ensemble, owners)
    rows_of = lambda count: pl.BlockSpec((count, LANES), lambda i: (0, 0))
    small_rows = 2 * tiles + 2 * obs_rows
    strips = pl.pallas_call(
        strips_kernel,
        out_shape=jax.ShapeDtypeStruct((8, LANES), real),
        in_specs=[whole],
        out_specs=whole,
        compiler_params=params,
        name="strips",
    )(ensemble)
    kept, to_odd, to_even, small = pl.pallas_call(
        functools.partial(pack_kernel, rows=obs_rows, cells=cells, fields=fields),
        out_shape=(jax.ShapeDtypeStruct((part, LANES), real),) * 3
        + (jax.ShapeDtypeStruct((small_rows, LANES), real),),
        grid=(1,),
        in_specs=[whole] + [rows_of(x.shape[0]) for x in small],
        out_specs=(whole,) * 4,
        scratch_shapes=[pltpu.VMEM((table_rows, LANES), real)],
        compiler_params=params,
        name="pack",
    )(send_count, *small)
    to_odd, to_even = pl.pallas_call(
        join_kernel,
        out_shape=(jax.ShapeDtypeStruct((16 + part, LANES), real),) * 2,
        in_specs=[whole] * 4,
        out_specs=(whole,) * 2,
        compiler_params=params,
        name="join",
    )(strips, other, to_odd, to_even)

    strip_rows = fields * members
    band = jax.ShapeDtypeStruct((2 * cells, 2 * LANES), jnp.bfloat16)

    powers = jax.ShapeDtypeStruct((fields * fields, LANES), real)
    slots = jax.ShapeDtypeStruct((2 * obs_rows, LANES), jnp.int32)

    def forecast(mixed, half, source, extra):
        return pl.pallas_call(
            functools.partial(forecast_kernel, fields=fields),
            out_shape=(
                jax.ShapeDtypeStruct((strip_rows, cells), real),
                jax.ShapeDtypeStruct((strip_rows, LANES), real),
                jax.ShapeDtypeStruct((places * 8, LANES), real),
            )
            + extra,
            in_specs=[whole] * 4,
            out_specs=(whole,) * (3 + len(extra)),
            scratch_shapes=[pltpu.VMEM((2 * strip_rows, cells), jnp.bfloat16), pltpu.VMEM((strip_rows, cells), real)],
            compiler_params=params,
            cost_estimate=pl.CostEstimate(
                flops=80 * strip_rows * cells, bytes_accessed=8 * strip_rows * cells, transcendentals=0
            ),
            name="forecast",
        )(mixed, half, source, send_count)

    *own_forecast, rule, mixed = forecast(couple, ensemble, small, (band, powers))
    carried = []
    for n, unit in enumerate(units):
        arrived = exchange(to_odd, to_even, owners, unit)
        if n + 1 < len(units):
            to_odd, to_even, kept = pl.pallas_call(
                functools.partial(regroup_kernel, unit=unit, into_lanes=n + 2 == len(units)),
                out_shape=tuple(jax.ShapeDtypeStruct(x.shape, real) for x in (to_odd, to_even, kept)),
                in_specs=[whole] * 4 + [pl.BlockSpec(memory_space=pl.ANY)],
                out_specs=(whole,) * 3,
                compiler_params=params,
                name="regroup",
            )(kept, *arrived, own_forecast[2])
            carried.append(to_odd)
    *other_forecast, slots_of = forecast(mixed, other, rule, (slots,))

    held = kept.shape[0] // 8
    sums_rows = -(-(members + 1 + 4 * held) // 8) * 8
    all_slots = 4 * held * LANES
    sums = jax.ShapeDtypeStruct((sums_rows, LANES), real)
    stay, to_odd, to_even, edges = pl.pallas_call(
        functools.partial(sums_kernel, owners=owners, units=units, fields=fields),
        out_shape=(sums, sums, sums, jax.ShapeDtypeStruct((2 * strip_rows, 2 * LANES), real)),
        in_specs=[whole] * (12 + len(carried)),
        out_specs=(whole,) * 4,
        scratch_shapes=[
            pltpu.VMEM((2 * strip_rows, LANES), real),
            pltpu.VMEM((LANES, all_slots), jnp.bfloat16),
            pltpu.VMEM((6 * places, all_slots), jnp.bfloat16),
            pltpu.VMEM((2 * (total + 16), fields * cells), jnp.bfloat16),
        ],
        compiler_params=params,
        name="sums",
    )(
        mixed, small, *own_forecast, *other_forecast, kept, *arrived, *carried,
    )

    head = members + 1
    used = head + 4 * held
    for n, unit in enumerate(reversed(units)):
        odd, swapped, even = exchange(to_odd, to_even, owners, unit)
        if n + 1 < len(units):
            added = (stay + even) + (odd + swapped)
            if n > 0:
                first = jnp.where(core == 0, odd, swapped)
                third = jnp.where(core == 0, swapped, odd)
                added = jnp.concatenate(
                    [added[:head]] + [x[head:used] for x in (stay, first, even, third)], axis=0
                )
                used = added.shape[0]
            stay = to_odd = to_even = added

    analysis, innovation = pl.pallas_call(
        functools.partial(analysis_kernel, units=units, obs_rows=obs_rows, count=owners // GROUPS),
        out_shape=(
            jax.ShapeDtypeStruct((members, fields, cells), real),
            jax.ShapeDtypeStruct((obs_rows, LANES), real),
        ),
        in_specs=[whole] * 9,
        out_specs=(whole, whole),
        scratch_shapes=[
            pltpu.VMEM((total, LANES), real),
            pltpu.VMEM((4 * (stay.shape[0] - head), LANES), real),
            pltpu.VMEM((fields * 2 * total, cells), jnp.bfloat16),
        ],
        compiler_params=params,
        name="analysis",
    )(
        own_forecast[0], other_forecast[0], edges, small, slots_of,
        stay, odd, swapped, even,
    )
    return (analysis, innovation.reshape(obs))


def solution(mesh):
    return jax.shard_map(
        shards,
        mesh=mesh,
        in_specs=(
            P("members", None, "cells"),
            P("cells"),
            P("cells"),
            P(),
            P("cells"),
            P("cells"),
            P("cells"),
            P("cells"),
            P("cells", None),
        ),
        out_specs=(P("members", None, "cells"), P("cells")),
        check_vma=False,
    )
```

```python
import functools
import math

import jax
import jax.numpy as jnp
from jax import lax
from jax.experimental import pallas as pl
from jax.experimental.pallas import tpu as pltpu
from jax.sharding import PartitionSpec as P

STEPS = 4
DIFFUSION = 0.05
LANES = 128
CAP = 32
GROUPS = LANES // CAP
BOTH = ("cells", "members")
EXACT = lax.Precision.HIGHEST
VMEM_BYTES = 48 * 1024 * 1024


def core_pairs(owners, place):
    pairs = []
    for block in range(owners):
        for core in range(2):
            to_block, to_core = place(block, core)
            pairs.append((block * 2 + core, to_block * 2 + to_core))
    return pairs


def stage_units(owners):
    units = []
    unit = 1
    while unit < owners:
        units.append(unit)
        unit *= 4
    if unit != owners or len(units) < 2:
        raise ValueError("blocks not 4**n")
    return units


def swap_cores(x, owners):
    return lax.ppermute(x, BOTH, core_pairs(owners, lambda block, core: (block, 1 - core)))


def exchange(to_odd, to_even, owners, unit):
    odd = lax.ppermute(
        to_odd, BOTH, core_pairs(owners, lambda block, core: (block ^ (unit * (1 + 2 * core)), core))
    )
    even = lax.ppermute(
        to_even, BOTH, core_pairs(owners, lambda block, core: (block ^ (unit * 2), core))
    )
    return odd, swap_cores(odd, owners), even


def digit_of(block, unit):
    return jnp.bitwise_and(lax.shift_right_logical(block, jnp.int32(unit.bit_length() - 1)), 3)


def here():
    return lax.axis_index("cells"), lax.axis_index("members")


def table_row(number, count):
    return (number % 4) * (count // 4) + number // 4


def strips_of(ref):
    fields, cells = ref.shape[1:]
    lane = lax.broadcasted_iota(jnp.int32, (1, LANES), 1)
    ends = [jnp.where(lane < STEPS, ref[:, f, :LANES], ref[:, f, cells - LANES :]) for f in range(fields)]
    ends = jnp.transpose(jnp.concatenate(ends, axis=0))
    return jnp.concatenate([ends[:STEPS, :], ends[LANES - STEPS :, :]], axis=0)


def pack_kernel(
    send_ref, speed_ref, flag_ref, place_ref, field_ref, value_ref, sigma_ref,
    kept_ref, odd_ref, even_ref, small_ref, table_ref, *, rows, cells, fields,
):
    block, core = here()
    tiles = cells // LANES
    speed, value, sigma = speed_ref[...], value_ref[...], sigma_ref[...]
    flag, place, field = (ref[...].astype(jnp.float32) for ref in (flag_ref, place_ref, field_ref))
    at = 0
    for part in (speed, flag, value, sigma):
        small_ref[at : at + part.shape[0], :] = part
        at += part.shape[0]
    lane = lax.broadcasted_iota(jnp.int32, (1, LANES), 1)
    low = lane < LANES // 2
    toward_left = speed * flag
    toward_right = speed - toward_left
    edge_left = jnp.where(low, toward_left[:1], toward_left[tiles - 1 :])
    edge_right = jnp.where(low, toward_right[:1], toward_right[tiles - 1 :])
    ids = field * float(cells) + place
    weight = 1.0 / (sigma * sigma)
    pull = weight * value
    sub = lax.broadcasted_iota(jnp.int32, (8, LANES), 0)
    empty = jnp.where(sub == 0, -1.0, 0.0)
    empty = jnp.where(sub == 3, edge_left, jnp.where(sub == 4, edge_right, empty))
    listed = [
        jnp.where(sub == 0, ids[r : r + 1], jnp.where(sub == 1, weight[r : r + 1], pull[r : r + 1]))
        for r in range(rows)
    ]
    owners = send_ref.shape[1]
    count = owners // GROUPS
    sends = jnp.broadcast_to(send_ref[...], (8, owners)).astype(jnp.bfloat16)
    sender = lax.broadcasted_iota(jnp.int32, (owners, LANES), 0)
    group = lax.broadcasted_iota(jnp.int32, (owners, LANES), 1) // CAP
    slot = lax.broadcasted_iota(jnp.int32, (8, LANES), 1) % CAP
    one = lambda mask: jnp.where(mask, 1.0, 0.0)
    which = jnp.concatenate(
        [one(sender < group * count + r) for r in range(count)] + [one(sender == group * count + r) for r in range(count)],
        axis=1,
    )
    found = jnp.dot(sends, which.astype(jnp.bfloat16), preferred_element_type=jnp.float32).astype(jnp.int32)
    for r in range(count):
        index = found[:, r * LANES : (r + 1) * LANES] + slot
        held = found[:, (count + r) * LANES : (count + r + 1) * LANES]
        block_of = empty
        inside = (slot < held) & (sub < 3)
        for w in range(rows):
            moved = jnp.take_along_axis(
                listed[w], jnp.bitwise_and(index, LANES - 1), axis=1, mode="promise_in_bounds"
            )
            block_of = jnp.where(inside & (lax.shift_right_logical(index, 7) == w), moved, block_of)
        row = 8 * table_row(r, count)
        table_ref[row : row + 8, :] = block_of
    part = kept_ref.shape[0]
    digit = digit_of(block, 1)
    for out, partner in ((kept_ref, 0), (odd_ref, 1 + 2 * core), (even_ref, 2)):
        out[...] = table_ref[pl.ds(pl.multiple_of(jnp.bitwise_xor(digit, partner) * part, 8), part), :]


def strips_kernel(ensemble_ref, out_ref):
    out_ref[...] = strips_of(ensemble_ref)


def join_kernel(own_ref, other_ref, odd_part, even_part, odd_ref, even_ref):
    strips = jnp.concatenate([own_ref[...], strips_of(other_ref)], axis=0)
    for part, out in ((odd_part, odd_ref), (even_part, even_ref)):
        out[:16, :] = strips
        out[16:, :] = part[...]


def incoming(digit, core, odd, swapped):
    sub = lax.broadcasted_iota(jnp.int32, (8, LANES), 0)
    low = lax.broadcasted_iota(jnp.int32, (8, LANES), 1) < LANES // 2
    direct = jnp.bitwise_xor(jnp.bitwise_and(digit, 1), core) == 0
    result = []
    for part, other_part in ((0, 1), (1, 0), (2, 2)):
        mine = odd[8 * part : 8 * part + 8, :]
        others = swapped[8 * other_part : 8 * other_part + 8, :]
        from_right = jnp.where(direct, mine, others)
        from_left = jnp.where(direct, others, mine)
        result.append(jnp.where(sub < STEPS if part < 2 else low, from_right, from_left))
    return result


def regroup_kernel(
    kept, odd, swapped, even, _, to_odd, to_even, stay, *, unit, into_lanes,
):
    block, core = here()
    after = digit_of(block, unit * 4)
    own, other, coefs = incoming(digit_of(block, unit), core, odd, swapped)
    sub = lax.broadcasted_iota(jnp.int32, (8, LANES), 0)
    lane_group = lax.broadcasted_iota(jnp.int32, (8, LANES), 1) // CAP
    held = kept.shape[0] // 8

    def received(k, at):
        if k == 0:
            return kept[pl.ds(at, 8), :]
        if k == 2:
            return even[pl.ds(16 + at, 8), :]
        mine, others = odd[pl.ds(16 + at, 8), :], swapped[pl.ds(16 + at, 8), :]
        return jnp.where(core == k // 2, mine, others)

    for target in (to_odd, to_even):
        target[0:8, :] = own
        target[8:16, :] = other
    for target, base, partner in ((to_odd, 16, 1 + 2 * core), (to_even, 16, 2), (stay, 0, 0)):
        wanted = jnp.bitwise_xor(after, partner)
        if into_lanes:
            for j in range(held):
                merged = coefs
                for k in range(4):
                    moved = pltpu.roll(received(k, 8 * j), jnp.bitwise_and(k - wanted, 3) * CAP, 1)
                    merged = jnp.where((lane_group == k) & (sub < 3), moved, merged)
                target[base + 8 * j : base + 8 * j + 8, :] = merged
        else:
            rest = held // 4
            for k in range(4):
                for r in range(rest):
                    at = pl.multiple_of((wanted * rest + r) * 8, 8)
                    row = base + 8 * (r * 4 + k)
                    target[row : row + 8, :] = jnp.where(sub < 3, received(k, at), coefs)


def fill_powers(couple_ref, powers_ref):
    fields = couple_ref.shape[0]
    mix = [
        [
            jnp.broadcast_to(couple_ref[f : f + 1, g : g + 1], (1, LANES)) + (1.0 if f == g else 0.0)
            for g in range(fields)
        ]
        for f in range(fields)
    ]
    for _ in range(2):
        mix = [
            [sum(mix[f][h] * mix[h][g] for h in range(fields)) for g in range(fields)]
            for f in range(fields)
        ]
    for f in range(fields):
        for g in range(fields):
            powers_ref[f * fields + g : f * fields + g + 1, :] = mix[f][g]


def powers_of(powers_ref, fields):
    return [[powers_ref[f * fields + g : f * fields + g + 1, :] for g in range(fields)] for f in range(fields)]


def transport(x, from_left, stay, from_right):
    for _ in range(STEPS):
        x = from_left * pltpu.roll(x, 1, 1) + stay * x + from_right * pltpu.roll(x, x.shape[1] - 1, 1)
    return x


def halves_of(x):
    high = x.astype(jnp.bfloat16)
    return high, (x - high.astype(jnp.float32)).astype(jnp.bfloat16)


def fill_band(small_ref, band_ref, cells):
    tiles = cells // LANES
    speed = small_ref[:tiles, :]
    toward_left = speed * small_ref[tiles : 2 * tiles, :]
    toward_right = speed - toward_left

    def row_of(x):
        return jnp.concatenate([x[t : t + 1] for t in range(tiles)], axis=1)

    step = {
        -1: row_of(toward_left + DIFFUSION),
        0: row_of(1.0 - 2.0 * DIFFUSION - speed),
        1: row_of(toward_right + DIFFUSION),
    }
    reach = dict(step)
    for _ in range(STEPS - 1):
        longer = {}
        for e in step:
            for d in reach:
                term = step[e] * (pltpu.roll(reach[d], -e % cells, 1) if e else reach[d])
                longer[d + e] = longer[d + e] + term if d + e in longer else term
        reach = longer
    row = lax.broadcasted_iota(jnp.int32, (LANES, LANES), 0)
    column = lax.broadcasted_iota(jnp.int32, (LANES, LANES), 1)
    ahead = row - column
    for t in range(tiles):
        rule = {d: reach[d][:, t * LANES : (t + 1) * LANES] for d in reach}

        def placed(distance, offsets):
            block = jnp.zeros(distance.shape, jnp.float32)
            for d in offsets:
                block = jnp.where(distance == d, rule[d], block)
            return block

        block = jnp.concatenate(
            [
                placed(ahead, range(-STEPS, STEPS + 1)),
                placed(ahead[:8] + LANES, range(1, STEPS + 1)),
                jnp.zeros((LANES - 16, LANES), jnp.float32),
                placed(ahead[LANES - 8 :] - LANES, range(-STEPS, 0)),
            ],
            axis=0,
        )
        for p, piece in enumerate(halves_of(block)):
            band_ref[2 * t * LANES : 2 * (t + 1) * LANES, p * LANES : (p + 1) * LANES] = piece


def fill_positions(send_ref, slots_ref):
    owners = send_ref.shape[1]
    count = owners // GROUPS
    rows = slots_ref.shape[0] // 2
    row = lax.broadcasted_iota(jnp.int32, (owners, owners), 0)
    column = lax.broadcasted_iota(jnp.int32, (owners, owners), 1)
    held = jnp.where(row == column, jnp.broadcast_to(send_ref[...], (owners, owners)), 0).astype(jnp.float32)
    held = jnp.broadcast_to(jnp.sum(held, axis=1, keepdims=True), (owners, LANES))
    ends = jnp.dot(
        jnp.where(column <= row, 1.0, 0.0).astype(jnp.bfloat16), held.astype(jnp.bfloat16),
        preferred_element_type=jnp.float32,
    )
    for r in range(rows):
        slot = (lax.broadcasted_iota(jnp.int32, (1, LANES), 1) + r * LANES).astype(jnp.float32)
        passed = ends <= slot
        owner = jnp.sum(jnp.where(passed, 1.0, 0.0), axis=0, keepdims=True).astype(jnp.int32)
        start = jnp.sum(jnp.where(passed, held, 0.0), axis=0, keepdims=True)
        group = lax.shift_right_logical(owner, count.bit_length() - 1)
        slots_ref[r : r + 1, :] = jnp.bitwise_and(owner, count - 1)
        slots_ref[rows + r : rows + r + 1, :] = group * CAP + (slot - start).astype(jnp.int32)


def forecast_kernel(extra_ref, source, from_ref, *refs, fields, own):
    members, _, cells = source.shape
    tiles = cells // LANES
    height = fields * members
    if own:
        state, edge, sums_ref, band_ref, powers_ref, split_ref, raw_ref = refs
        fill_powers(extra_ref, powers_ref)
        fill_band(from_ref, band_ref, cells)
    else:
        send_ref, own_state, state, edge, sums_ref, slots_ref, pieces_ref, split_ref, raw_ref = refs
        powers_ref, band_ref = extra_ref, from_ref
        fill_positions(send_ref, slots_ref)
        core = here()[1]

        def put_pieces(side, f, lanes, value):
            for p, piece in enumerate(halves_of(value)):
                at = pl.multiple_of((f * 2 + p) * 2 * members + side * members, 16)
                pieces_ref[pl.ds(at, members), lanes] = piece

        for f in range(fields):
            put_pieces(core, f, slice(0, cells), own_state[f * members : (f + 1) * members, :])
    low = lax.broadcasted_iota(jnp.int32, (members, LANES), 1) < LANES // 2
    for f in range(fields):
        rows = slice(f * members, (f + 1) * members)
        raw_ref[rows, :] = source[:, f, :]
        x = raw_ref[rows, :]
        edge[rows, :] = jnp.where(
            low,
            pltpu.roll(x[:, :LANES], STEPS, 1),
            pltpu.roll(x[:, cells - LANES :], LANES // 2 + 3 * STEPS, 1),
        )
        for p, piece in enumerate(halves_of(x)):
            split_ref[p * height + f * members : p * height + (f + 1) * members, :] = piece
    mix = powers_of(powers_ref, fields)
    nearer = lax.broadcasted_iota(jnp.int32, (2 * height, LANES), 1) < LANES // 2
    for t in range(tiles):
        lanes, after, before = (
            slice(n % tiles * LANES, (n % tiles + 1) * LANES) for n in (t, t + 1, t - 1)
        )
        around = jnp.where(nearer, split_ref[:, after], split_ref[:, before])
        product = jnp.dot(
            jnp.concatenate([split_ref[:, lanes], around], axis=1),
            band_ref[2 * t * LANES : 2 * (t + 1) * LANES, :],
            preferred_element_type=jnp.float32,
        )
        moved = (
            product[height:, LANES:] + (product[:height, LANES:] + product[height:, :LANES])
        ) + product[:height, :LANES]
        for f in range(fields):
            value = sum(mix[f][g] * moved[g * members : (g + 1) * members] for g in range(fields))
            state[f * members : (f + 1) * members, lanes] = value
            if not own:
                put_pieces(1 - core, f, lanes, value)
            place = (f * tiles + t) * 8
            sums_ref[place : place + 8, :] = sum(value[8 * i : 8 * i + 8] for i in range(members // 8))


def pieces_of(x):
    high = x.astype(jnp.bfloat16).astype(jnp.float32)
    rest = x - high
    middle = rest.astype(jnp.bfloat16).astype(jnp.float32)
    return high, middle, rest - middle


def sums_kernel(
    powers_ref, small_ref, own_state, own_edge, own_sums, other_state, other_edge, other_sums,
    kept, odd, swapped, even, *refs, owners, units, fields,
):
    carried = refs[: len(units) - 1]
    (
        stay_ref, odd_ref, even_ref, edge_ref, halo_ref, onehot_ref, spread_ref, split_ref,
    ) = refs[len(units) - 1 :]
    states, raw_edges = (own_state, other_state), (own_edge, other_edge)
    block, core = here()
    members = states[0].shape[0] // fields
    cells = states[0].shape[1]
    tiles = cells // LANES
    total = 2 * members
    places = fields * tiles
    has_left = (block > 0).astype(jnp.float32)
    has_right = (block < owners - 1).astype(jnp.float32)
    sub = lax.broadcasted_iota(jnp.int32, (8, LANES), 0)
    lane = lax.broadcasted_iota(jnp.int32, (1, LANES), 1)
    lane8 = lax.broadcasted_iota(jnp.int32, (8, LANES), 1)
    half_lanes = LANES // 2
    low = lane < half_lanes

    strips = incoming(digit_of(block, units[-1]), core, odd, swapped)
    for unit, earlier in reversed(list(zip(units, carried))):
        digit = digit_of(block, unit)
        rows = [earlier[8 * p : 8 * p + 8, :] for p in range(3)]
        picked = []
        for p in range(3):
            from_right = jnp.where(digit != 3, rows[p], strips[p])
            from_left = jnp.where(digit != 0, rows[p], strips[p])
            picked.append(jnp.where(sub < STEPS if p < 2 else lane8 < half_lanes, from_right, from_left))
        strips = picked

    place_ids = lax.broadcasted_iota(jnp.int32, (places, LANES), 0)
    lane_ids = lax.broadcasted_iota(jnp.int32, (LANES, LANES), 0)
    held = kept.shape[0] // 8
    sources = [(kept, 8 * j) for j in range(held)]
    for source, base in ((odd, 16), (swapped, 16), (even, 16)):
        sources += [(source, base + 8 * j) for j in range(held)]
    hits = []
    for n, (source, at) in enumerate(sources):
        local = source[at : at + 1, :].astype(jnp.int32)
        hit = place_ids == lax.shift_right_arithmetic(local, 7)
        hits.append(hit)
        onehot = (lane_ids == jnp.bitwise_and(local, LANES - 1)).astype(jnp.float32)
        lanes = slice(n * LANES, (n + 1) * LANES)
        onehot_ref[:, lanes] = onehot.astype(jnp.bfloat16)
        weight, pull = source[at + 1 : at + 2, :], source[at + 2 : at + 3, :]
        stack = [jnp.where(hit, piece, 0.0) for piece in pieces_of(weight) + pieces_of(pull)]
        spread_ref[:, lanes] = jnp.concatenate(stack, axis=0).astype(jnp.bfloat16)
    placed = lax.dot_general(
        spread_ref[...], onehot_ref[...], (((1,), (1,)), ((), ())), preferred_element_type=jnp.float32
    )
    placed = [placed[p * places : (p + 1) * places] for p in range(6)]
    weight = placed[0] + placed[1] + placed[2]
    pull = placed[3] + placed[4] + placed[5]

    root = jnp.sqrt(weight)
    scale = jnp.where(weight > 0.0, lax.rsqrt(jnp.where(weight > 0.0, weight, 1.0)), 0.0)
    sub16 = lax.broadcasted_iota(jnp.int32, (16, LANES), 0)
    depth = total + 16
    means = {}

    def put(row, lanes, value):
        for p, piece in enumerate(halves_of(value)):
            split_ref[pl.ds(row + p * depth, value.shape[0]), lanes] = piece

    def put_tile(at, sums, halves, into):
        means[at] = jnp.sum(sums, axis=0, keepdims=True) * (1.0 / total)
        lanes = slice(into * LANES, (into + 1) * LANES)
        for half, value in enumerate(halves):
            side = core if half == 0 else 1 - core
            anomaly = (value - means[at]) * root[at : at + 1]
            put(pl.multiple_of(side * members, 16), lanes, anomaly)
        drawn = (pull[at : at + 1] - weight[at : at + 1] * means[at]) * scale[at : at + 1]
        put(total, lanes, jnp.where(sub16 == 0, drawn, 0.0))

    def product_of(first, last):
        lanes = slice(first * LANES, last * LANES)
        return lax.dot_general(
            split_ref[:, lanes], split_ref[:, lanes], (((1,), (1,)), ((), ())), preferred_element_type=jnp.float32
        )

    inner = tiles - 2
    products = []
    for f in range(fields):
        rows = slice(f * members, (f + 1) * members)
        for t in range(1, tiles - 1):
            at = f * tiles + t
            lanes = slice(t * LANES, (t + 1) * LANES)
            sums = own_sums[8 * at : 8 * at + 8, :] + other_sums[8 * at : 8 * at + 8, :]
            put_tile(at, sums, [state[rows, lanes] for state in states], f * inner + t - 1)
        products.append(product_of(f * inner, (f + 1) * inner))

    right_first = half_lanes + 3 * STEPS
    strip_rows = fields * members
    for half in range(2):
        strip = strips[half]
        left = jnp.where(sub < STEPS, pltpu.roll(strip, STEPS, 0) * has_left, 0.0)
        at = right_first % 8
        right = jnp.where(
            (sub >= at) & (sub < at + STEPS), (pltpu.roll(strip, at, 0) if at else strip) * has_right, 0.0
        )
        gap = jnp.zeros((right_first - at - 8, LANES), jnp.float32)
        rest = jnp.zeros((LANES - (right_first - at) - 8, LANES), jnp.float32)
        halo_ref[half * strip_rows : (half + 1) * strip_rows, :] = jnp.transpose(
            jnp.concatenate([left, gap, right, rest], axis=0)
        )
    speed = small_ref[:tiles, :]
    toward_left = speed * small_ref[tiles : 2 * tiles, :]
    toward_right = speed - toward_left
    is_left = lane < STEPS
    is_right = (lane >= right_first) & (lane < right_first + STEPS)
    inside = jnp.where(is_left, has_left, jnp.where(is_right, has_right, 1.0))
    from_outside = (lane8 < STEPS) | ((lane8 >= right_first) & (lane8 < right_first + STEPS))

    def edge_row(rows, row):
        own = jnp.where(
            low, pltpu.roll(rows[:1], STEPS, 1), pltpu.roll(rows[tiles - 1 :], half_lanes + 3 * STEPS, 1)
        )
        left = pltpu.roll(strips[2][row : row + 1], STEPS, 1)
        right = pltpu.roll(strips[2][row : row + 1], right_first, 1)
        return jnp.where(is_left, left, jnp.where(is_right, right, own))

    edge_left = edge_row(toward_left, 3)
    edge_right = edge_row(toward_right, 4)
    from_left = jnp.broadcast_to((edge_left + DIFFUSION) * inside, (8, LANES))
    from_right = jnp.broadcast_to((edge_right + DIFFUSION) * inside, (8, LANES))
    stay = jnp.broadcast_to((1.0 - 2.0 * DIFFUSION - edge_left - edge_right) * inside, (8, LANES))
    mix = powers_of(powers_ref, fields)
    first_sums = [jnp.zeros((8, LANES), jnp.float32) for _ in range(fields)]
    last_sums = [jnp.zeros((8, LANES), jnp.float32) for _ in range(fields)]
    for half in range(2):
        state, edge = states[half], raw_edges[half]
        for i in range(members // 8):
            moved = []
            for f in range(fields):
                at = f * members + 8 * i
                x = edge[at : at + 8, :]
                x = jnp.where(from_outside, halo_ref[half * strip_rows + at : half * strip_rows + at + 8, :], x)
                moved.append(transport(x, from_left, stay, from_right))
            for f in range(fields):
                at = f * members + 8 * i
                value = sum(mix[f][g] * moved[g] for g in range(fields))
                first_tile = jnp.where(lane8 < STEPS, pltpu.roll(value, LANES - STEPS, 1), state[at : at + 8, :LANES])
                last_tile = jnp.where(
                    lane8 >= LANES - STEPS,
                    pltpu.roll(value, LANES - right_first, 1),
                    state[at : at + 8, cells - LANES :],
                )
                edge_ref[half * strip_rows + at : half * strip_rows + at + 8, :LANES] = first_tile
                edge_ref[half * strip_rows + at : half * strip_rows + at + 8, LANES:] = last_tile
                first_sums[f] = first_sums[f] + first_tile
                last_sums[f] = last_sums[f] + last_tile
    edge_at = fields * inner
    for f in range(fields):
        for n, (t, sums) in enumerate(((0, first_sums[f]), (tiles - 1, last_sums[f]))):
            column = slice(n * LANES, (n + 1) * LANES)
            halves = [
                edge_ref[half * strip_rows + f * members : half * strip_rows + (f + 1) * members, column]
                for half in range(2)
            ]
            put_tile(f * tiles + t, sums, halves, edge_at + 2 * f + n)
    products.append(product_of(edge_at, edge_at + 2 * fields))
    products = sum(products)
    mean = jnp.concatenate([means[at] for at in range(places)], axis=0)
    gram = sum(
        products[p * depth : p * depth + total + 8, q * depth : q * depth + total]
        for p, q in ((1, 1), (1, 0), (0, 1), (0, 0))
    )
    gram = jnp.concatenate([gram, jnp.zeros((total + 8, LANES - total), jnp.float32)], axis=1)
    folded = pltpu.roll(gram[:members], total, 1) + gram[members:total]
    blank = jnp.zeros((stay_ref.shape[0] - members - 1, LANES), jnp.float32)
    for out in (stay_ref, odd_ref, even_ref):
        out[:members, :] = folded
        out[members : members + 1, :] = gram[total : total + 1]
        out[members + 1 :, :] = blank

    found = lax.dot_general(
        jnp.concatenate(pieces_of(mean), axis=0).astype(jnp.bfloat16), onehot_ref[...],
        (((1,), (0,)), ((), ())), preferred_element_type=jnp.float32,
    )
    found = found[:places] + found[places : 2 * places] + found[2 * places :]
    for out, source, partner in ((stay_ref, 0, 0), (odd_ref, 1, 1 + 2 * core), (even_ref, 3, 2)):
        for j in range(held):
            n = source * held + j
            center = jnp.sum(
                jnp.where(hits[n], found[:, n * LANES : (n + 1) * LANES], 0.0), axis=0, keepdims=True
            )
            out[pl.ds(members + 1 + partner * held + j, 1), :] = center


def spread_row(row):
    return jnp.broadcast_to(row, (8, LANES))


def eliminate(rows):
    count = len(rows)
    rows = list(rows)
    sub = lax.broadcasted_iota(jnp.int32, (8, LANES), 0)

    def columns_of(row, b):
        first = 8 * (count + b)
        return [jnp.broadcast_to(row[:, first + k : first + k + 1], (8, LANES)) for k in range(8)]

    upcoming = columns_of(rows[0], 0)
    for b in range(count):
        own = upcoming
        below = {i: columns_of(rows[i], b) for i in range(b + 1, count)}
        if b + 1 < count:
            upcoming = columns_of(rows[b + 1], b + 1)
        for j in range(8):
            scale = lax.rsqrt(spread_row(own[j][j : j + 1, :]))
            upper = spread_row(rows[b][j : j + 1, :]) * scale
            lower = own[j] * scale
            factors = {k: spread_row(lower[k : k + 1, :]) for k in range(j + 1, 8)}
            for k in range(j + 1, 8):
                own[k] = own[k] - lower * factors[k]
            rows[b] = jnp.where(sub == j, upper, rows[b] - jnp.where(sub > j, lower, 0.0) * upper)
            for i in range(b + 1, count):
                here = below[i][j] * scale
                if i == b + 1:
                    for k in range(8):
                        upcoming[k] = upcoming[k] - here * spread_row(here[k : k + 1, :])
                for k in range(j + 1, 8):
                    below[i][k] = below[i][k] - here * factors[k]
                rows[i] = rows[i] - here * upper
    return rows


def analysis_kernel(
    split_ref, edge_ref, small_ref, slots_ref, kept, odd, swapped, even,
    analysis_ref, innovation_ref, center_ref, pieces_ref, result_ref, sems, *, units, obs_rows, count,
):
    block, core = here()
    members, fields, cells = analysis_ref.shape
    total = 2 * members
    strip_rows = fields * members
    for f in range(fields):
        for half in range(2):
            rows = slice(half * strip_rows + f * members, half * strip_rows + (f + 1) * members)
            side = core if half == 0 else 1 - core
            for p, piece in enumerate(halves_of(edge_ref[rows, :])):
                at = pl.multiple_of((f * 2 + p) * total + side * members, 16)
                pieces_ref[pl.ds(at, members), :] = piece
    head = members + 1
    sums = (kept[:head, :] + even[:head, :]) + (odd[:head, :] + swapped[:head, :])
    returned = kept.shape[0] - head
    center_ref[:returned, :] = kept[head:, :]
    center_ref[returned : 2 * returned, :] = jnp.where(core == 0, odd[head:, :], swapped[head:, :])
    center_ref[2 * returned : 3 * returned, :] = even[head:, :]
    center_ref[3 * returned :, :] = jnp.where(core == 0, swapped[head:, :], odd[head:, :])
    lane = lax.broadcasted_iota(jnp.int32, (8, LANES), 1)
    sub = lax.broadcasted_iota(jnp.int32, (8, LANES), 0)
    shifted = pltpu.roll(sums[:members], total, 1)
    rows = []
    for b in range(total // 8):
        at = 8 * b
        source = sums[at : at + 8] if at < members else shifted[at - members : at - members + 8]
        own = jnp.where(lane == sub + at + total, total - 1.0, 0.0)
        unit = jnp.where(lane == sub + at, 1.0, 0.0)
        rows.append(jnp.where(lane >= total, source + own, unit))
    rows = eliminate(rows)
    cross = sums[members : members + 1]
    inverse = [jnp.where(lane < total, r, 0.0) for r in rows]
    carried = [jnp.sum(r * cross, axis=1, keepdims=True) for r in inverse]
    row_sums = [jnp.sum(r, axis=1, keepdims=True) for r in inverse]
    row_means = [r * (1.0 / total) for r in row_sums]
    weights = jnp.sum(sum(r * c for r, c in zip(inverse, carried)), axis=0, keepdims=True)
    column_mean = jnp.sum(sum(inverse), axis=0, keepdims=True) * (1.0 / total)
    grand = jnp.sum(sum(row_means), axis=0, keepdims=True) * (1.0 / total)
    weights = weights - jnp.sum(sum(r * c for r, c in zip(row_means, carried)), axis=0, keepdims=True)
    root = math.sqrt(total - 1.0)
    add = weights + 1.0 / total - root * (column_mean - grand)
    count_here = members // 8
    mixing = [
        root * jnp.where(core == 0, inverse[b] - row_means[b], inverse[b + count_here] - row_means[b + count_here]) + add
        for b in range(count_here)
    ]
    high, rest = halves_of(jnp.concatenate(mixing, axis=0)[:, :total])
    mixing = jnp.concatenate(
        [jnp.concatenate([high, high], axis=1), jnp.concatenate([rest, rest], axis=1)], axis=0
    )
    copies = []
    width = cells // 2
    for n in range(2):
        lanes = slice(n * width, (n + 1) * width)
        for f in range(fields):
            rows = slice(f * 2 * total, (f + 1) * 2 * total)
            if n == 0:
                states = [pieces_ref[rows, :LANES], split_ref[rows, LANES:width]]
            else:
                states = [split_ref[rows, width : cells - LANES], pieces_ref[rows, LANES:]]
            product = jnp.dot(mixing, jnp.concatenate(states, axis=1), preferred_element_type=jnp.float32)
            result_ref[:, f, lanes] = product[:members] + product[members:]
        copies.append(
            pltpu.make_async_copy(
                result_ref.at[:, :, pl.ds(n * width, width)],
                analysis_ref.at[:, :, pl.ds(n * width, width)],
                sems.at[n],
            )
        )
        copies[-1].start()

    held = count // 4
    lane_group = lane // CAP
    table = []
    for r in range(count):
        merged = jnp.zeros((1, LANES), jnp.float32)
        for group in range(GROUPS):
            owner = group * count + r
            way = [jnp.bitwise_xor(digit_of(block, unit), (owner // unit) % 4) for unit in units]
            row = way[-1] * held
            if len(units) > 2:
                row = row + sum(step * 4**n for n, step in enumerate(way[:-2]))
            size = 4 * held
            for step in reversed(way[1:-1]):
                row = row + step * size
                size = size * 4
            row = row + way[0] * returned
            line = center_ref[pl.ds(row, 1), :]
            moved = pltpu.roll(line, jnp.bitwise_and(group - way[-2], 3) * CAP, 1)
            merged = jnp.where(lane_group[:1] == group, moved, merged)
        table.append(jnp.broadcast_to(merged, (8, LANES)))
    for r in range(obs_rows):
        center = jnp.zeros((8, LANES), jnp.float32)
        lanes = jnp.broadcast_to(slots_ref[obs_rows + r : obs_rows + r + 1, :], (8, LANES))
        for n in range(count):
            found = jnp.take_along_axis(table[n], lanes, axis=1, mode="promise_in_bounds")
            center = jnp.where(slots_ref[r : r + 1, :] == n, found, center)
        center = center[:1]
        at = small_ref.shape[0] - 2 * obs_rows + r
        value, sigma = small_ref[at : at + 1, :], small_ref[at + obs_rows : at + obs_rows + 1, :]
        innovation_ref[r : r + 1, :] = (value - center) / sigma
    for copy in copies:
        copy.wait()


def shards(
    ensemble, speed, direction, couple, obs_place, obs_field, obs_value, obs_sigma, send_count
):
    members, fields, cells = ensemble.shape
    owners = lax.axis_size("cells")
    total = members * lax.axis_size("members")
    obs = obs_place.shape[0]
    obs_rows = obs // LANES
    tiles = cells // LANES
    places = fields * tiles
    units = stage_units(owners)
    block = lax.axis_index("cells").astype(jnp.int32)
    core = lax.axis_index("members").astype(jnp.int32)
    small = (
        speed.reshape(tiles, LANES), direction.reshape(tiles, LANES),
        *(x.reshape(obs_rows, LANES) for x in (obs_place, obs_field, obs_value, obs_sigma)),
    )
    whole = pl.BlockSpec(memory_space=pltpu.VMEM)
    params = pltpu.CompilerParams(vmem_limit_bytes=VMEM_BYTES)
    real = jnp.float32

    table_rows = 8 * (owners // GROUPS)
    part = table_rows // 4
    other = swap_cores(ensemble, owners)
    rows_of = lambda count: pl.BlockSpec((count, LANES), lambda i: (0, 0))
    small_rows = 2 * tiles + 2 * obs_rows
    strips = pl.pallas_call(
        strips_kernel,
        out_shape=jax.ShapeDtypeStruct((8, LANES), real),
        in_specs=[whole],
        out_specs=whole,
        compiler_params=params,
        name="strips",
    )(ensemble)
    kept, to_odd, to_even, small = pl.pallas_call(
        functools.partial(pack_kernel, rows=obs_rows, cells=cells, fields=fields),
        out_shape=(jax.ShapeDtypeStruct((part, LANES), real),) * 3
        + (jax.ShapeDtypeStruct((small_rows, LANES), real),),
        grid=(1,),
        in_specs=[whole] + [rows_of(x.shape[0]) for x in small],
        out_specs=(whole,) * 4,
        scratch_shapes=[pltpu.VMEM((table_rows, LANES), real)],
        compiler_params=params,
        name="pack",
    )(send_count, *small)
    to_odd, to_even = pl.pallas_call(
        join_kernel,
        out_shape=(jax.ShapeDtypeStruct((16 + part, LANES), real),) * 2,
        in_specs=[whole] * 4,
        out_specs=(whole,) * 2,
        compiler_params=params,
        name="join",
    )(strips, other, to_odd, to_even)

    strip_rows = fields * members
    band = jax.ShapeDtypeStruct((2 * cells, 2 * LANES), jnp.bfloat16)

    powers = jax.ShapeDtypeStruct((fields * fields, LANES), real)
    slots = jax.ShapeDtypeStruct((2 * obs_rows, LANES), jnp.int32)

    pieces = jax.ShapeDtypeStruct((fields * 2 * total, cells), jnp.bfloat16)

    def forecast(operands, extra, own):
        return pl.pallas_call(
            functools.partial(forecast_kernel, fields=fields, own=own),
            out_shape=(
                jax.ShapeDtypeStruct((strip_rows, cells), real),
                jax.ShapeDtypeStruct((strip_rows, LANES), real),
                jax.ShapeDtypeStruct((places * 8, LANES), real),
            )
            + extra,
            in_specs=[whole] * len(operands),
            out_specs=(whole,) * (3 + len(extra)),
            scratch_shapes=[pltpu.VMEM((2 * strip_rows, cells), jnp.bfloat16), pltpu.VMEM((strip_rows, cells), real)],
            compiler_params=params,
            cost_estimate=pl.CostEstimate(
                flops=80 * strip_rows * cells, bytes_accessed=8 * strip_rows * cells, transcendentals=0
            ),
            name="forecast",
        )(*operands)

    *own_forecast, rule, mixed = forecast((couple, ensemble, small), (band, powers), True)
    carried = []
    for n, unit in enumerate(units):
        arrived = exchange(to_odd, to_even, owners, unit)
        if n + 1 < len(units):
            to_odd, to_even, kept = pl.pallas_call(
                functools.partial(regroup_kernel, unit=unit, into_lanes=n + 2 == len(units)),
                out_shape=tuple(jax.ShapeDtypeStruct(x.shape, real) for x in (to_odd, to_even, kept)),
                in_specs=[whole] * 4 + [pl.BlockSpec(memory_space=pl.ANY)],
                out_specs=(whole,) * 3,
                compiler_params=params,
                name="regroup",
            )(kept, *arrived, own_forecast[2])
            carried.append(to_odd)
    *other_forecast, slots_of, split = forecast(
        (mixed, other, rule, send_count, own_forecast[0]), (slots, pieces), False
    )

    held = kept.shape[0] // 8
    sums_rows = -(-(members + 1 + 4 * held) // 8) * 8
    all_slots = 4 * held * LANES
    sums = jax.ShapeDtypeStruct((sums_rows, LANES), real)
    stay, to_odd, to_even, edges = pl.pallas_call(
        functools.partial(sums_kernel, owners=owners, units=units, fields=fields),
        out_shape=(sums, sums, sums, jax.ShapeDtypeStruct((2 * strip_rows, 2 * LANES), real)),
        in_specs=[whole] * (12 + len(carried)),
        out_specs=(whole,) * 4,
        scratch_shapes=[
            pltpu.VMEM((2 * strip_rows, LANES), real),
            pltpu.VMEM((LANES, all_slots), jnp.bfloat16),
            pltpu.VMEM((6 * places, all_slots), jnp.bfloat16),
            pltpu.VMEM((2 * (total + 16), fields * cells), jnp.bfloat16),
        ],
        compiler_params=params,
        name="sums",
    )(
        mixed, small, *own_forecast, *other_forecast, kept, *arrived, *carried,
    )

    head = members + 1
    used = head + 4 * held
    for n, unit in enumerate(reversed(units)):
        odd, swapped, even = exchange(to_odd, to_even, owners, unit)
        if n + 1 < len(units):
            added = (stay + even) + (odd + swapped)
            if n > 0:
                first = jnp.where(core == 0, odd, swapped)
                third = jnp.where(core == 0, swapped, odd)
                added = jnp.concatenate(
                    [added[:head]] + [x[head:used] for x in (stay, first, even, third)], axis=0
                )
                used = added.shape[0]
            stay = to_odd = to_even = added

    analysis, innovation = pl.pallas_call(
        functools.partial(analysis_kernel, units=units, obs_rows=obs_rows, count=owners // GROUPS),
        out_shape=(
            jax.ShapeDtypeStruct((members, fields, cells), real),
            jax.ShapeDtypeStruct((obs_rows, LANES), real),
        ),
        in_specs=[whole] * 8,
        out_specs=(pl.BlockSpec(memory_space=pl.ANY), whole),
        scratch_shapes=[
            pltpu.VMEM((4 * (stay.shape[0] - head), LANES), real),
            pltpu.VMEM((fields * 2 * total, 2 * LANES), jnp.bfloat16),
            pltpu.VMEM((members, fields, cells), real),
            pltpu.SemaphoreType.DMA((2,)),
        ],
        compiler_params=params,
        name="analysis",
    )(
        split, edges, small, slots_of,
        stay, odd, swapped, even,
    )
    return (analysis, innovation.reshape(obs))


def solution(mesh):
    return jax.shard_map(
        shards,
        mesh=mesh,
        in_specs=(
            P("members", None, "cells"),
            P("cells"),
            P("cells"),
            P(),
            P("cells"),
            P("cells"),
            P("cells"),
            P("cells"),
            P("cells", None),
        ),
        out_specs=(P("members", None, "cells"), P("cells")),
        check_vma=False,
    )
```

```python
import functools
import math

import jax
import jax.numpy as jnp
from jax import lax
from jax.experimental import pallas as pl
from jax.experimental.pallas import tpu as pltpu
from jax.sharding import PartitionSpec as P

STEPS = 4
DIFFUSION = 0.05
LANES = 128
CAP = 32
GROUPS = LANES // CAP
BOTH = ("cells", "members")
EXACT = lax.Precision.HIGHEST
VMEM_BYTES = 48 * 1024 * 1024


def core_pairs(owners, place):
    pairs = []
    for block in range(owners):
        for core in range(2):
            to_block, to_core = place(block, core)
            pairs.append((block * 2 + core, to_block * 2 + to_core))
    return pairs


def stage_units(owners):
    units = []
    unit = 1
    while unit < owners:
        units.append(unit)
        unit *= 4
    if unit != owners or len(units) < 2:
        raise ValueError("blocks not 4**n")
    return units


def swap_cores(x, owners):
    return lax.ppermute(x, BOTH, core_pairs(owners, lambda block, core: (block, 1 - core)))


def exchange(to_odd, to_even, owners, unit):
    odd = lax.ppermute(
        to_odd, BOTH, core_pairs(owners, lambda block, core: (block ^ (unit * (1 + 2 * core)), core))
    )
    even = lax.ppermute(
        to_even, BOTH, core_pairs(owners, lambda block, core: (block ^ (unit * 2), core))
    )
    return odd, swap_cores(odd, owners), even


def digit_of(block, unit):
    return jnp.bitwise_and(lax.shift_right_logical(block, jnp.int32(unit.bit_length() - 1)), 3)


def here():
    return lax.axis_index("cells"), lax.axis_index("members")


def table_row(number, count):
    return (number % 4) * (count // 4) + number // 4


def strips_of(ref):
    fields, cells = ref.shape[1:]
    lane = lax.broadcasted_iota(jnp.int32, (1, LANES), 1)
    ends = [jnp.where(lane < STEPS, ref[:, f, :LANES], ref[:, f, cells - LANES :]) for f in range(fields)]
    ends = jnp.transpose(jnp.concatenate(ends, axis=0))
    return jnp.concatenate([ends[:STEPS, :], ends[LANES - STEPS :, :]], axis=0)


def pack_kernel(
    send_ref, speed_ref, flag_ref, place_ref, field_ref, value_ref, sigma_ref,
    kept_ref, odd_ref, even_ref, small_ref, table_ref, *, rows, cells, fields,
):
    block, core = here()
    tiles = cells // LANES
    speed, value, sigma = speed_ref[...], value_ref[...], sigma_ref[...]
    flag, place, field = (ref[...].astype(jnp.float32) for ref in (flag_ref, place_ref, field_ref))
    at = 0
    for part in (speed, flag, value, sigma):
        small_ref[at : at + part.shape[0], :] = part
        at += part.shape[0]
    lane = lax.broadcasted_iota(jnp.int32, (1, LANES), 1)
    low = lane < LANES // 2
    toward_left = speed * flag
    toward_right = speed - toward_left
    edge_left = jnp.where(low, toward_left[:1], toward_left[tiles - 1 :])
    edge_right = jnp.where(low, toward_right[:1], toward_right[tiles - 1 :])
    ids = field * float(cells) + place
    weight = 1.0 / (sigma * sigma)
    pull = weight * value
    sub = lax.broadcasted_iota(jnp.int32, (8, LANES), 0)
    empty = jnp.where(sub == 0, -1.0, 0.0)
    empty = jnp.where(sub == 3, edge_left, jnp.where(sub == 4, edge_right, empty))
    listed = [
        jnp.where(sub == 0, ids[r : r + 1], jnp.where(sub == 1, weight[r : r + 1], pull[r : r + 1]))
        for r in range(rows)
    ]
    owners = send_ref.shape[1]
    count = owners // GROUPS
    sends = jnp.broadcast_to(send_ref[...], (8, owners)).astype(jnp.bfloat16)
    sender = lax.broadcasted_iota(jnp.int32, (owners, LANES), 0)
    group = lax.broadcasted_iota(jnp.int32, (owners, LANES), 1) // CAP
    slot = lax.broadcasted_iota(jnp.int32, (8, LANES), 1) % CAP
    one = lambda mask: jnp.where(mask, 1.0, 0.0)
    which = jnp.concatenate(
        [one(sender < group * count + r) for r in range(count)] + [one(sender == group * count + r) for r in range(count)],
        axis=1,
    )
    found = jnp.dot(sends, which.astype(jnp.bfloat16), preferred_element_type=jnp.float32).astype(jnp.int32)
    for r in range(count):
        index = found[:, r * LANES : (r + 1) * LANES] + slot
        held = found[:, (count + r) * LANES : (count + r + 1) * LANES]
        block_of = empty
        inside = (slot < held) & (sub < 3)
        for w in range(rows):
            moved = jnp.take_along_axis(
                listed[w], jnp.bitwise_and(index, LANES - 1), axis=1, mode="promise_in_bounds"
            )
            block_of = jnp.where(inside & (lax.shift_right_logical(index, 7) == w), moved, block_of)
        row = 8 * table_row(r, count)
        table_ref[row : row + 8, :] = block_of
    part = kept_ref.shape[0]
    digit = digit_of(block, 1)
    for out, partner in ((kept_ref, 0), (odd_ref, 1 + 2 * core), (even_ref, 2)):
        out[...] = table_ref[pl.ds(pl.multiple_of(jnp.bitwise_xor(digit, partner) * part, 8), part), :]


def strips_kernel(ensemble_ref, out_ref):
    out_ref[...] = strips_of(ensemble_ref)


def join_kernel(own_ref, other_ref, odd_part, even_part, odd_ref, even_ref):
    strips = jnp.concatenate([own_ref[...], strips_of(other_ref)], axis=0)
    for part, out in ((odd_part, odd_ref), (even_part, even_ref)):
        out[:16, :] = strips
        out[16:, :] = part[...]


def incoming(digit, core, odd, swapped):
    sub = lax.broadcasted_iota(jnp.int32, (8, LANES), 0)
    low = lax.broadcasted_iota(jnp.int32, (8, LANES), 1) < LANES // 2
    direct = jnp.bitwise_xor(jnp.bitwise_and(digit, 1), core) == 0
    result = []
    for part, other_part in ((0, 1), (1, 0), (2, 2)):
        mine = odd[8 * part : 8 * part + 8, :]
        others = swapped[8 * other_part : 8 * other_part + 8, :]
        from_right = jnp.where(direct, mine, others)
        from_left = jnp.where(direct, others, mine)
        result.append(jnp.where(sub < STEPS if part < 2 else low, from_right, from_left))
    return result


def regroup_kernel(
    kept, odd, swapped, even, _, to_odd, to_even, stay, *, unit, into_lanes,
):
    block, core = here()
    after = digit_of(block, unit * 4)
    own, other, coefs = incoming(digit_of(block, unit), core, odd, swapped)
    sub = lax.broadcasted_iota(jnp.int32, (8, LANES), 0)
    lane_group = lax.broadcasted_iota(jnp.int32, (8, LANES), 1) // CAP
    held = kept.shape[0] // 8

    def received(k, at):
        if k == 0:
            return kept[pl.ds(at, 8), :]
        if k == 2:
            return even[pl.ds(16 + at, 8), :]
        mine, others = odd[pl.ds(16 + at, 8), :], swapped[pl.ds(16 + at, 8), :]
        return jnp.where(core == k // 2, mine, others)

    for target in (to_odd, to_even):
        target[0:8, :] = own
        target[8:16, :] = other
    for target, base, partner in ((to_odd, 16, 1 + 2 * core), (to_even, 16, 2), (stay, 0, 0)):
        wanted = jnp.bitwise_xor(after, partner)
        if into_lanes:
            for j in range(held):
                merged = coefs
                for k in range(4):
                    moved = pltpu.roll(received(k, 8 * j), jnp.bitwise_and(k - wanted, 3) * CAP, 1)
                    merged = jnp.where((lane_group == k) & (sub < 3), moved, merged)
                target[base + 8 * j : base + 8 * j + 8, :] = merged
        else:
            rest = held // 4
            for k in range(4):
                for r in range(rest):
                    at = pl.multiple_of((wanted * rest + r) * 8, 8)
                    row = base + 8 * (r * 4 + k)
                    target[row : row + 8, :] = jnp.where(sub < 3, received(k, at), coefs)


def fill_powers(couple_ref, powers_ref):
    fields = couple_ref.shape[0]
    mix = [
        [
            jnp.broadcast_to(couple_ref[f : f + 1, g : g + 1], (1, LANES)) + (1.0 if f == g else 0.0)
            for g in range(fields)
        ]
        for f in range(fields)
    ]
    for _ in range(2):
        mix = [
            [sum(mix[f][h] * mix[h][g] for h in range(fields)) for g in range(fields)]
            for f in range(fields)
        ]
    for f in range(fields):
        for g in range(fields):
            powers_ref[f * fields + g : f * fields + g + 1, :] = mix[f][g]


def powers_of(powers_ref, fields):
    return [[powers_ref[f * fields + g : f * fields + g + 1, :] for g in range(fields)] for f in range(fields)]


def transport(x, from_left, stay, from_right):
    for _ in range(STEPS):
        x = from_left * pltpu.roll(x, 1, 1) + stay * x + from_right * pltpu.roll(x, x.shape[1] - 1, 1)
    return x


def halves_of(x):
    high = x.astype(jnp.bfloat16)
    return high, (x - high.astype(jnp.float32)).astype(jnp.bfloat16)


def band_maker(small_ref, band_ref, cells):
    tiles = cells // LANES
    speed = small_ref[:tiles, :]
    toward_left = speed * small_ref[tiles : 2 * tiles, :]
    toward_right = speed - toward_left

    lane = lax.broadcasted_iota(jnp.int32, (tiles, LANES), 1)

    def shifted(x, by):
        if by == 0:
            return x
        turned = pltpu.roll(x, 1 if by < 0 else LANES - 1, 1)
        carried = pltpu.roll(turned, 1 if by < 0 else tiles - 1, 0)
        return jnp.where(lane == (0 if by < 0 else LANES - 1), carried, turned)

    step = {-1: toward_left + DIFFUSION, 0: 1.0 - 2.0 * DIFFUSION - speed, 1: toward_right + DIFFUSION}
    reach = dict(step)
    for _ in range(STEPS - 1):
        longer = {}
        for e in step:
            for d in reach:
                term = step[e] * shifted(reach[d], e)
                longer[d + e] = longer[d + e] + term if d + e in longer else term
        reach = longer
    row = lax.broadcasted_iota(jnp.int32, (LANES, LANES), 0)
    column = lax.broadcasted_iota(jnp.int32, (LANES, LANES), 1)
    ahead = row - column

    def make(t):
        rule = {d: reach[d][t : t + 1, :] for d in reach}

        def placed(distance, offsets):
            block = jnp.zeros(distance.shape, jnp.float32)
            for d in offsets:
                block = jnp.where(distance == d, rule[d], block)
            return block

        block = jnp.concatenate(
            [
                placed(ahead, range(-STEPS, STEPS + 1)),
                placed(ahead[:8] + LANES, range(1, STEPS + 1)),
                jnp.zeros((LANES - 16, LANES), jnp.float32),
                placed(ahead[LANES - 8 :] - LANES, range(-STEPS, 0)),
            ],
            axis=0,
        )
        for p, piece in enumerate(halves_of(block)):
            band_ref[2 * t * LANES : 2 * (t + 1) * LANES, p * LANES : (p + 1) * LANES] = piece

    return make


def fill_positions(send_ref, slots_ref):
    owners = send_ref.shape[1]
    count = owners // GROUPS
    rows = slots_ref.shape[0] // 2
    row = lax.broadcasted_iota(jnp.int32, (owners, owners), 0)
    column = lax.broadcasted_iota(jnp.int32, (owners, owners), 1)
    held = jnp.where(row == column, jnp.broadcast_to(send_ref[...], (owners, owners)), 0).astype(jnp.float32)
    held = jnp.broadcast_to(jnp.sum(held, axis=1, keepdims=True), (owners, LANES))
    ends = jnp.dot(
        jnp.where(column <= row, 1.0, 0.0).astype(jnp.bfloat16), held.astype(jnp.bfloat16),
        preferred_element_type=jnp.float32,
    )
    for r in range(rows):
        slot = (lax.broadcasted_iota(jnp.int32, (1, LANES), 1) + r * LANES).astype(jnp.float32)
        passed = ends <= slot
        owner = jnp.sum(jnp.where(passed, 1.0, 0.0), axis=0, keepdims=True).astype(jnp.int32)
        start = jnp.sum(jnp.where(passed, held, 0.0), axis=0, keepdims=True)
        group = lax.shift_right_logical(owner, count.bit_length() - 1)
        slots_ref[r : r + 1, :] = jnp.bitwise_and(owner, count - 1)
        slots_ref[rows + r : rows + r + 1, :] = group * CAP + (slot - start).astype(jnp.int32)


def forecast_kernel(extra_ref, source, from_ref, *refs, fields, own):
    members, _, cells = source.shape
    tiles = cells // LANES
    height = fields * members
    if own:
        state, edge, sums_ref, band_ref, powers_ref, split_ref, raw_ref = refs
        fill_powers(extra_ref, powers_ref)
        make_band = band_maker(from_ref, band_ref, cells)
    else:
        send_ref, own_state, state, edge, sums_ref, slots_ref, pieces_ref, split_ref, raw_ref = refs
        powers_ref, band_ref = extra_ref, from_ref
        fill_positions(send_ref, slots_ref)
        core = here()[1]

        def put_pieces(side, f, lanes, value):
            for p, piece in enumerate(halves_of(value)):
                at = pl.multiple_of((f * 2 + p) * 2 * members + side * members, 16)
                pieces_ref[pl.ds(at, members), lanes] = piece

        for f in range(fields):
            put_pieces(core, f, slice(0, cells), own_state[f * members : (f + 1) * members, :])
    low = lax.broadcasted_iota(jnp.int32, (members, LANES), 1) < LANES // 2
    for f in range(fields):
        rows = slice(f * members, (f + 1) * members)
        raw_ref[rows, :] = source[:, f, :]
        x = raw_ref[rows, :]
        edge[rows, :] = jnp.where(
            low,
            pltpu.roll(x[:, :LANES], STEPS, 1),
            pltpu.roll(x[:, cells - LANES :], LANES // 2 + 3 * STEPS, 1),
        )
        for p, piece in enumerate(halves_of(x)):
            split_ref[p * height + f * members : p * height + (f + 1) * members, :] = piece
    mix = powers_of(powers_ref, fields)
    nearer = lax.broadcasted_iota(jnp.int32, (2 * height, LANES), 1) < LANES // 2
    for t in range(tiles):
        lanes, after, before = (
            slice(n % tiles * LANES, (n % tiles + 1) * LANES) for n in (t, t + 1, t - 1)
        )
        if own:
            make_band(t)
        around = jnp.where(nearer, split_ref[:, after], split_ref[:, before])
        product = jnp.dot(
            jnp.concatenate([split_ref[:, lanes], around], axis=1),
            band_ref[2 * t * LANES : 2 * (t + 1) * LANES, :],
            preferred_element_type=jnp.float32,
        )
        moved = (
            product[height:, LANES:] + (product[:height, LANES:] + product[height:, :LANES])
        ) + product[:height, :LANES]
        for f in range(fields):
            value = sum(mix[f][g] * moved[g * members : (g + 1) * members] for g in range(fields))
            state[f * members : (f + 1) * members, lanes] = value
            if not own:
                put_pieces(1 - core, f, lanes, value)
            place = (f * tiles + t) * 8
            sums_ref[place : place + 8, :] = sum(value[8 * i : 8 * i + 8] for i in range(members // 8))


def pieces_of(x):
    high = x.astype(jnp.bfloat16).astype(jnp.float32)
    rest = x - high
    middle = rest.astype(jnp.bfloat16).astype(jnp.float32)
    return high, middle, rest - middle


def sums_kernel(
    powers_ref, small_ref, own_state, own_edge, own_sums, other_state, other_edge, other_sums,
    kept, odd, swapped, even, *refs, owners, units, fields,
):
    carried = refs[: len(units) - 1]
    (
        stay_ref, odd_ref, even_ref, edge_ref, halo_ref, onehot_ref, spread_ref, split_ref,
    ) = refs[len(units) - 1 :]
    states, raw_edges = (own_state, other_state), (own_edge, other_edge)
    block, core = here()
    members = states[0].shape[0] // fields
    cells = states[0].shape[1]
    tiles = cells // LANES
    total = 2 * members
    places = fields * tiles
    has_left = (block > 0).astype(jnp.float32)
    has_right = (block < owners - 1).astype(jnp.float32)
    sub = lax.broadcasted_iota(jnp.int32, (8, LANES), 0)
    lane = lax.broadcasted_iota(jnp.int32, (1, LANES), 1)
    lane8 = lax.broadcasted_iota(jnp.int32, (8, LANES), 1)
    half_lanes = LANES // 2
    low = lane < half_lanes

    strips = incoming(digit_of(block, units[-1]), core, odd, swapped)
    for unit, earlier in reversed(list(zip(units, carried))):
        digit = digit_of(block, unit)
        rows = [earlier[8 * p : 8 * p + 8, :] for p in range(3)]
        picked = []
        for p in range(3):
            from_right = jnp.where(digit != 3, rows[p], strips[p])
            from_left = jnp.where(digit != 0, rows[p], strips[p])
            picked.append(jnp.where(sub < STEPS if p < 2 else lane8 < half_lanes, from_right, from_left))
        strips = picked

    place_ids = lax.broadcasted_iota(jnp.int32, (places, LANES), 0)
    lane_ids = lax.broadcasted_iota(jnp.int32, (LANES, LANES), 0)
    held = kept.shape[0] // 8
    sources = [(kept, 8 * j) for j in range(held)]
    for source, base in ((odd, 16), (swapped, 16), (even, 16)):
        sources += [(source, base + 8 * j) for j in range(held)]
    hits = []
    for n, (source, at) in enumerate(sources):
        local = source[at : at + 1, :].astype(jnp.int32)
        hit = place_ids == lax.shift_right_arithmetic(local, 7)
        hits.append(hit)
        onehot = (lane_ids == jnp.bitwise_and(local, LANES - 1)).astype(jnp.float32)
        lanes = slice(n * LANES, (n + 1) * LANES)
        onehot_ref[:, lanes] = onehot.astype(jnp.bfloat16)
        weight, pull = source[at + 1 : at + 2, :], source[at + 2 : at + 3, :]
        stack = [jnp.where(hit, piece, 0.0) for piece in pieces_of(weight) + pieces_of(pull)]
        spread_ref[:, lanes] = jnp.concatenate(stack, axis=0).astype(jnp.bfloat16)
    placed = lax.dot_general(
        spread_ref[...], onehot_ref[...], (((1,), (1,)), ((), ())), preferred_element_type=jnp.float32
    )
    placed = [placed[p * places : (p + 1) * places] for p in range(6)]
    weight = placed[0] + placed[1] + placed[2]
    pull = placed[3] + placed[4] + placed[5]

    root = jnp.sqrt(weight)
    scale = jnp.where(weight > 0.0, lax.rsqrt(jnp.where(weight > 0.0, weight, 1.0)), 0.0)
    sub16 = lax.broadcasted_iota(jnp.int32, (16, LANES), 0)
    depth = total + 16
    means = {}

    def put(row, lanes, value):
        for p, piece in enumerate(halves_of(value)):
            split_ref[pl.ds(row + p * depth, value.shape[0]), lanes] = piece

    def put_tile(at, sums, halves, into):
        means[at] = jnp.sum(sums, axis=0, keepdims=True) * (1.0 / total)
        lanes = slice(into * LANES, (into + 1) * LANES)
        for half, value in enumerate(halves):
            side = core if half == 0 else 1 - core
            anomaly = (value - means[at]) * root[at : at + 1]
            put(pl.multiple_of(side * members, 16), lanes, anomaly)
        drawn = (pull[at : at + 1] - weight[at : at + 1] * means[at]) * scale[at : at + 1]
        put(total, lanes, jnp.where(sub16 == 0, drawn, 0.0))

    def product_of(first, last):
        lanes = slice(first * LANES, last * LANES)
        anomalies = jnp.concatenate([split_ref[:total, lanes], split_ref[depth : depth + total, lanes]], axis=0)
        return lax.dot_general(
            split_ref[:, lanes], anomalies, (((1,), (1,)), ((), ())), preferred_element_type=jnp.float32
        )

    inner = tiles - 2
    products = []
    for f in range(fields):
        rows = slice(f * members, (f + 1) * members)
        for t in range(1, tiles - 1):
            at = f * tiles + t
            lanes = slice(t * LANES, (t + 1) * LANES)
            sums = own_sums[8 * at : 8 * at + 8, :] + other_sums[8 * at : 8 * at + 8, :]
            put_tile(at, sums, [state[rows, lanes] for state in states], f * inner + t - 1)
        products.append(product_of(f * inner, (f + 1) * inner))

    right_first = half_lanes + 3 * STEPS
    strip_rows = fields * members
    for half in range(2):
        strip = strips[half]
        left = jnp.where(sub < STEPS, pltpu.roll(strip, STEPS, 0) * has_left, 0.0)
        at = right_first % 8
        right = jnp.where(
            (sub >= at) & (sub < at + STEPS), (pltpu.roll(strip, at, 0) if at else strip) * has_right, 0.0
        )
        gap = jnp.zeros((right_first - at - 8, LANES), jnp.float32)
        rest = jnp.zeros((LANES - (right_first - at) - 8, LANES), jnp.float32)
        halo_ref[half * strip_rows : (half + 1) * strip_rows, :] = jnp.transpose(
            jnp.concatenate([left, gap, right, rest], axis=0)
        )
    speed = small_ref[:tiles, :]
    toward_left = speed * small_ref[tiles : 2 * tiles, :]
    toward_right = speed - toward_left
    is_left = lane < STEPS
    is_right = (lane >= right_first) & (lane < right_first + STEPS)
    inside = jnp.where(is_left, has_left, jnp.where(is_right, has_right, 1.0))
    from_outside = (lane8 < STEPS) | ((lane8 >= right_first) & (lane8 < right_first + STEPS))

    def edge_row(rows, row):
        own = jnp.where(
            low, pltpu.roll(rows[:1], STEPS, 1), pltpu.roll(rows[tiles - 1 :], half_lanes + 3 * STEPS, 1)
        )
        left = pltpu.roll(strips[2][row : row + 1], STEPS, 1)
        right = pltpu.roll(strips[2][row : row + 1], right_first, 1)
        return jnp.where(is_left, left, jnp.where(is_right, right, own))

    edge_left = edge_row(toward_left, 3)
    edge_right = edge_row(toward_right, 4)
    from_left = jnp.broadcast_to((edge_left + DIFFUSION) * inside, (8, LANES))
    from_right = jnp.broadcast_to((edge_right + DIFFUSION) * inside, (8, LANES))
    stay = jnp.broadcast_to((1.0 - 2.0 * DIFFUSION - edge_left - edge_right) * inside, (8, LANES))
    mix = powers_of(powers_ref, fields)
    first_sums = [[jnp.zeros((8, LANES), jnp.float32)] * fields for _ in range(2)]
    last_sums = [[jnp.zeros((8, LANES), jnp.float32)] * fields for _ in range(2)]
    for half in range(2):
        state, edge = states[half], raw_edges[half]
        for i in range(members // 8):
            moved = []
            for f in range(fields):
                at = f * members + 8 * i
                x = edge[at : at + 8, :]
                x = jnp.where(from_outside, halo_ref[half * strip_rows + at : half * strip_rows + at + 8, :], x)
                moved.append(transport(x, from_left, stay, from_right))
            for f in range(fields):
                at = f * members + 8 * i
                value = sum(mix[f][g] * moved[g] for g in range(fields))
                first_tile = jnp.where(lane8 < STEPS, pltpu.roll(value, LANES - STEPS, 1), state[at : at + 8, :LANES])
                last_tile = jnp.where(
                    lane8 >= LANES - STEPS,
                    pltpu.roll(value, LANES - right_first, 1),
                    state[at : at + 8, cells - LANES :],
                )
                edge_ref[half * strip_rows + at : half * strip_rows + at + 8, :LANES] = first_tile
                edge_ref[half * strip_rows + at : half * strip_rows + at + 8, LANES:] = last_tile
                first_sums[half][f] = first_sums[half][f] + first_tile
                last_sums[half][f] = last_sums[half][f] + last_tile
    edge_at = fields * inner
    for f in range(fields):
        for n, (t, sums) in enumerate(((0, first_sums), (tiles - 1, last_sums))):
            column = slice(n * LANES, (n + 1) * LANES)
            halves = [
                edge_ref[half * strip_rows + f * members : half * strip_rows + (f + 1) * members, column]
                for half in range(2)
            ]
            put_tile(f * tiles + t, sums[0][f] + sums[1][f], halves, edge_at + 2 * f + n)
    products.append(product_of(edge_at, edge_at + 2 * fields))
    products = sum(products)
    mean = jnp.concatenate([means[at] for at in range(places)], axis=0)
    gram = products[: total + 8] + products[depth : depth + total + 8]
    gram = gram + pltpu.roll(gram, total, 1)
    in_low = lax.broadcasted_iota(jnp.int32, (members, LANES), 1) < total
    folded = jnp.where(in_low, gram[members:total], gram[:members])
    blank = jnp.zeros((stay_ref.shape[0] - members - 1, LANES), jnp.float32)
    for out in (stay_ref, odd_ref, even_ref):
        out[:members, :] = folded
        out[members : members + 1, :] = gram[total : total + 1]
        out[members + 1 :, :] = blank

    found = lax.dot_general(
        jnp.concatenate(pieces_of(mean), axis=0).astype(jnp.bfloat16), onehot_ref[...],
        (((1,), (0,)), ((), ())), preferred_element_type=jnp.float32,
    )
    found = found[:places] + found[places : 2 * places] + found[2 * places :]
    for out, source, partner in ((stay_ref, 0, 0), (odd_ref, 1, 1 + 2 * core), (even_ref, 3, 2)):
        for j in range(held):
            n = source * held + j
            center = jnp.sum(
                jnp.where(hits[n], found[:, n * LANES : (n + 1) * LANES], 0.0), axis=0, keepdims=True
            )
            out[pl.ds(members + 1 + partner * held + j, 1), :] = center


def spread_row(row):
    return jnp.broadcast_to(row, (8, LANES))


def eliminate(rows):
    count = len(rows)
    rows = list(rows)
    sub = lax.broadcasted_iota(jnp.int32, (8, LANES), 0)

    def columns_of(row, b):
        first = 8 * (count + b)
        return [jnp.broadcast_to(row[:, first + k : first + k + 1], (8, LANES)) for k in range(8)]

    upcoming = columns_of(rows[0], 0)
    for b in range(count):
        own = upcoming
        below = {i: columns_of(rows[i], b) for i in range(b + 1, count)}
        if b + 1 < count:
            upcoming = columns_of(rows[b + 1], b + 1)
        for j in range(8):
            scale = lax.rsqrt(spread_row(own[j][j : j + 1, :]))
            upper = spread_row(rows[b][j : j + 1, :]) * scale
            lower = own[j] * scale
            factors = {k: spread_row(lower[k : k + 1, :]) for k in range(j + 1, 8)}
            for k in range(j + 1, 8):
                own[k] = own[k] - lower * factors[k]
            rows[b] = jnp.where(sub == j, upper, rows[b] - jnp.where(sub > j, lower, 0.0) * upper)
            for i in range(b + 1, count):
                here = below[i][j] * scale
                if i == b + 1:
                    for k in range(8):
                        upcoming[k] = upcoming[k] - here * spread_row(here[k : k + 1, :])
                for k in range(j + 1, 8):
                    below[i][k] = below[i][k] - here * factors[k]
                rows[i] = rows[i] - here * upper
    return rows


def analysis_kernel(
    split_ref, edge_ref, small_ref, slots_ref, kept, odd, swapped, even,
    analysis_ref, innovation_ref, center_ref, pieces_ref, result_ref, sems, *, units, obs_rows, count,
):
    block, core = here()
    members, fields, cells = analysis_ref.shape
    total = 2 * members
    strip_rows = fields * members
    for f in range(fields):
        for half in range(2):
            rows = slice(half * strip_rows + f * members, half * strip_rows + (f + 1) * members)
            side = core if half == 0 else 1 - core
            for p, piece in enumerate(halves_of(edge_ref[rows, :])):
                at = pl.multiple_of((f * 2 + p) * total + side * members, 16)
                pieces_ref[pl.ds(at, members), :] = piece
    head = members + 1
    sums = (kept[:head, :] + even[:head, :]) + (odd[:head, :] + swapped[:head, :])
    returned = kept.shape[0] - head
    center_ref[:returned, :] = kept[head:, :]
    center_ref[returned : 2 * returned, :] = jnp.where(core == 0, odd[head:, :], swapped[head:, :])
    center_ref[2 * returned : 3 * returned, :] = even[head:, :]
    center_ref[3 * returned :, :] = jnp.where(core == 0, swapped[head:, :], odd[head:, :])
    lane = lax.broadcasted_iota(jnp.int32, (8, LANES), 1)
    sub = lax.broadcasted_iota(jnp.int32, (8, LANES), 0)
    shifted = pltpu.roll(sums[:members], total, 1)
    rows = []
    for b in range(total // 8):
        at = 8 * b
        source = sums[at : at + 8] if at < members else shifted[at - members : at - members + 8]
        own = jnp.where(lane == sub + at + total, total - 1.0, 0.0)
        unit = jnp.where(lane == sub + at, 1.0, 0.0)
        rows.append(jnp.where(lane >= total, source + own, unit))
    rows = eliminate(rows)
    cross = sums[members : members + 1]
    inverse = [jnp.where(lane < total, r, 0.0) for r in rows]
    carried = [jnp.sum(r * cross, axis=1, keepdims=True) for r in inverse]
    row_sums = [jnp.sum(r, axis=1, keepdims=True) for r in inverse]
    row_means = [r * (1.0 / total) for r in row_sums]
    weights = jnp.sum(sum(r * c for r, c in zip(inverse, carried)), axis=0, keepdims=True)
    column_mean = jnp.sum(sum(inverse), axis=0, keepdims=True) * (1.0 / total)
    grand = jnp.sum(sum(row_means), axis=0, keepdims=True) * (1.0 / total)
    weights = weights - jnp.sum(sum(r * c for r, c in zip(row_means, carried)), axis=0, keepdims=True)
    root = math.sqrt(total - 1.0)
    add = weights + 1.0 / total - root * (column_mean - grand)
    count_here = members // 8
    mixing = [
        root * jnp.where(core == 0, inverse[b] - row_means[b], inverse[b + count_here] - row_means[b + count_here]) + add
        for b in range(count_here)
    ]
    high, rest = halves_of(jnp.concatenate(mixing, axis=0)[:, :total])
    mixing = jnp.concatenate(
        [jnp.concatenate([high, high], axis=1), jnp.concatenate([rest, rest], axis=1)], axis=0
    )
    copies = []
    width = cells // 2
    for n in range(2):
        lanes = slice(n * width, (n + 1) * width)
        for f in range(fields):
            rows = slice(f * 2 * total, (f + 1) * 2 * total)
            if n == 0:
                states = [pieces_ref[rows, :LANES], split_ref[rows, LANES:width]]
            else:
                states = [split_ref[rows, width : cells - LANES], pieces_ref[rows, LANES:]]
            product = jnp.dot(mixing, jnp.concatenate(states, axis=1), preferred_element_type=jnp.float32)
            result_ref[:, f, lanes] = product[:members] + product[members:]
        copies.append(
            pltpu.make_async_copy(
                result_ref.at[:, :, pl.ds(n * width, width)],
                analysis_ref.at[:, :, pl.ds(n * width, width)],
                sems.at[n],
            )
        )
        copies[-1].start()

    held = count // 4
    lane_group = lane // CAP
    table = []
    for r in range(count):
        merged = jnp.zeros((1, LANES), jnp.float32)
        for group in range(GROUPS):
            owner = group * count + r
            way = [jnp.bitwise_xor(digit_of(block, unit), (owner // unit) % 4) for unit in units]
            row = way[-1] * held
            if len(units) > 2:
                row = row + sum(step * 4**n for n, step in enumerate(way[:-2]))
            size = 4 * held
            for step in reversed(way[1:-1]):
                row = row + step * size
                size = size * 4
            row = row + way[0] * returned
            line = center_ref[pl.ds(row, 1), :]
            moved = pltpu.roll(line, jnp.bitwise_and(group - way[-2], 3) * CAP, 1)
            merged = jnp.where(lane_group[:1] == group, moved, merged)
        table.append(jnp.broadcast_to(merged, (8, LANES)))
    for r in range(obs_rows):
        center = jnp.zeros((8, LANES), jnp.float32)
        lanes = jnp.broadcast_to(slots_ref[obs_rows + r : obs_rows + r + 1, :], (8, LANES))
        for n in range(count):
            found = jnp.take_along_axis(table[n], lanes, axis=1, mode="promise_in_bounds")
            center = jnp.where(slots_ref[r : r + 1, :] == n, found, center)
        center = center[:1]
        at = small_ref.shape[0] - 2 * obs_rows + r
        value, sigma = small_ref[at : at + 1, :], small_ref[at + obs_rows : at + obs_rows + 1, :]
        innovation_ref[r : r + 1, :] = (value - center) / sigma
    for copy in copies:
        copy.wait()


def shards(
    ensemble, speed, direction, couple, obs_place, obs_field, obs_value, obs_sigma, send_count
):
    members, fields, cells = ensemble.shape
    owners = lax.axis_size("cells")
    total = members * lax.axis_size("members")
    obs = obs_place.shape[0]
    obs_rows = obs // LANES
    tiles = cells // LANES
    places = fields * tiles
    units = stage_units(owners)
    block = lax.axis_index("cells").astype(jnp.int32)
    core = lax.axis_index("members").astype(jnp.int32)
    small = (
        speed.reshape(tiles, LANES), direction.reshape(tiles, LANES),
        *(x.reshape(obs_rows, LANES) for x in (obs_place, obs_field, obs_value, obs_sigma)),
    )
    whole = pl.BlockSpec(memory_space=pltpu.VMEM)
    params = pltpu.CompilerParams(vmem_limit_bytes=VMEM_BYTES)
    real = jnp.float32

    table_rows = 8 * (owners // GROUPS)
    part = table_rows // 4
    other = swap_cores(ensemble, owners)
    rows_of = lambda count: pl.BlockSpec((count, LANES), lambda i: (0, 0))
    small_rows = 2 * tiles + 2 * obs_rows
    strips = pl.pallas_call(
        strips_kernel,
        out_shape=jax.ShapeDtypeStruct((8, LANES), real),
        in_specs=[whole],
        out_specs=whole,
        compiler_params=params,
        name="strips",
    )(ensemble)
    kept, to_odd, to_even, small = pl.pallas_call(
        functools.partial(pack_kernel, rows=obs_rows, cells=cells, fields=fields),
        out_shape=(jax.ShapeDtypeStruct((part, LANES), real),) * 3
        + (jax.ShapeDtypeStruct((small_rows, LANES), real),),
        grid=(1,),
        in_specs=[whole] + [rows_of(x.shape[0]) for x in small],
        out_specs=(whole,) * 4,
        scratch_shapes=[pltpu.VMEM((table_rows, LANES), real)],
        compiler_params=params,
        name="pack",
    )(send_count, *small)
    to_odd, to_even = pl.pallas_call(
        join_kernel,
        out_shape=(jax.ShapeDtypeStruct((16 + part, LANES), real),) * 2,
        in_specs=[whole] * 4,
        out_specs=(whole,) * 2,
        compiler_params=params,
        name="join",
    )(strips, other, to_odd, to_even)

    strip_rows = fields * members
    band = jax.ShapeDtypeStruct((2 * cells, 2 * LANES), jnp.bfloat16)

    powers = jax.ShapeDtypeStruct((fields * fields, LANES), real)
    slots = jax.ShapeDtypeStruct((2 * obs_rows, LANES), jnp.int32)

    pieces = jax.ShapeDtypeStruct((fields * 2 * total, cells), jnp.bfloat16)

    def forecast(operands, extra, own):
        return pl.pallas_call(
            functools.partial(forecast_kernel, fields=fields, own=own),
            out_shape=(
                jax.ShapeDtypeStruct((strip_rows, cells), real),
                jax.ShapeDtypeStruct((strip_rows, LANES), real),
                jax.ShapeDtypeStruct((places * 8, LANES), real),
            )
            + extra,
            in_specs=[whole] * len(operands),
            out_specs=(whole,) * (3 + len(extra)),
            scratch_shapes=[pltpu.VMEM((2 * strip_rows, cells), jnp.bfloat16), pltpu.VMEM((strip_rows, cells), real)],
            compiler_params=params,
            cost_estimate=pl.CostEstimate(
                flops=80 * strip_rows * cells, bytes_accessed=8 * strip_rows * cells, transcendentals=0
            ),
            name="forecast",
        )(*operands)

    *own_forecast, rule, mixed = forecast((couple, ensemble, small), (band, powers), True)
    carried = []
    for n, unit in enumerate(units):
        arrived = exchange(to_odd, to_even, owners, unit)
        if n + 1 < len(units):
            to_odd, to_even, kept = pl.pallas_call(
                functools.partial(regroup_kernel, unit=unit, into_lanes=n + 2 == len(units)),
                out_shape=tuple(jax.ShapeDtypeStruct(x.shape, real) for x in (to_odd, to_even, kept)),
                in_specs=[whole] * 4 + [pl.BlockSpec(memory_space=pl.ANY)],
                out_specs=(whole,) * 3,
                compiler_params=params,
                name="regroup",
            )(kept, *arrived, own_forecast[2])
            carried.append(to_odd)
    *other_forecast, slots_of, split = forecast(
        (mixed, other, rule, send_count, own_forecast[0]), (slots, pieces), False
    )

    held = kept.shape[0] // 8
    sums_rows = -(-(members + 1 + 4 * held) // 8) * 8
    all_slots = 4 * held * LANES
    sums = jax.ShapeDtypeStruct((sums_rows, LANES), real)
    stay, to_odd, to_even, edges = pl.pallas_call(
        functools.partial(sums_kernel, owners=owners, units=units, fields=fields),
        out_shape=(sums, sums, sums, jax.ShapeDtypeStruct((2 * strip_rows, 2 * LANES), real)),
        in_specs=[whole] * (12 + len(carried)),
        out_specs=(whole,) * 4,
        scratch_shapes=[
            pltpu.VMEM((2 * strip_rows, LANES), real),
            pltpu.VMEM((LANES, all_slots), jnp.bfloat16),
            pltpu.VMEM((6 * places, all_slots), jnp.bfloat16),
            pltpu.VMEM((2 * (total + 16), fields * cells), jnp.bfloat16),
        ],
        compiler_params=params,
        name="sums",
    )(
        mixed, small, *own_forecast, *other_forecast, kept, *arrived, *carried,
    )

    head = members + 1
    used = head + 4 * held
    for n, unit in enumerate(reversed(units)):
        odd, swapped, even = exchange(to_odd, to_even, owners, unit)
        if n + 1 < len(units):
            added = (stay + even) + (odd + swapped)
            if n > 0:
                first = jnp.where(core == 0, odd, swapped)
                third = jnp.where(core == 0, swapped, odd)
                added = jnp.concatenate(
                    [added[:head]] + [x[head:used] for x in (stay, first, even, third)], axis=0
                )
                used = added.shape[0]
            stay = to_odd = to_even = added

    analysis, innovation = pl.pallas_call(
        functools.partial(analysis_kernel, units=units, obs_rows=obs_rows, count=owners // GROUPS),
        out_shape=(
            jax.ShapeDtypeStruct((members, fields, cells), real),
            jax.ShapeDtypeStruct((obs_rows, LANES), real),
        ),
        in_specs=[whole] * 8,
        out_specs=(pl.BlockSpec(memory_space=pl.ANY), whole),
        scratch_shapes=[
            pltpu.VMEM((4 * (stay.shape[0] - head), LANES), real),
            pltpu.VMEM((fields * 2 * total, 2 * LANES), jnp.bfloat16),
            pltpu.VMEM((members, fields, cells), real),
            pltpu.SemaphoreType.DMA((2,)),
        ],
        compiler_params=params,
        name="analysis",
    )(
        split, edges, small, slots_of,
        stay, odd, swapped, even,
    )
    return (analysis, innovation.reshape(obs))


def solution(mesh):
    return jax.shard_map(
        shards,
        mesh=mesh,
        in_specs=(
            P("members", None, "cells"),
            P("cells"),
            P("cells"),
            P(),
            P("cells"),
            P("cells"),
            P("cells"),
            P("cells"),
            P("cells", None),
        ),
        out_specs=(P("members", None, "cells"), P("cells")),
        check_vma=False,
    )
```

```python
import functools
import math

import jax
import jax.numpy as jnp
from jax import lax
from jax.experimental import pallas as pl
from jax.experimental.pallas import tpu as pltpu
from jax.sharding import PartitionSpec as P

STEPS = 4
DIFFUSION = 0.05
LANES = 128
CAP = 32
GROUPS = LANES // CAP
BOTH = ("cells", "members")
EXACT = lax.Precision.HIGHEST
VMEM_BYTES = 48 * 1024 * 1024


def core_pairs(owners, place):
    pairs = []
    for block in range(owners):
        for core in range(2):
            to_block, to_core = place(block, core)
            pairs.append((block * 2 + core, to_block * 2 + to_core))
    return pairs


def stage_units(owners):
    units = []
    unit = 1
    while unit < owners:
        units.append(unit)
        unit *= 4
    if unit != owners or len(units) < 2:
        raise ValueError("blocks not 4**n")
    return units


def swap_cores(x, owners):
    return lax.ppermute(x, BOTH, core_pairs(owners, lambda block, core: (block, 1 - core)))


def exchange(to_odd, to_even, owners, unit):
    odd = lax.ppermute(
        to_odd, BOTH, core_pairs(owners, lambda block, core: (block ^ (unit * (1 + 2 * core)), core))
    )
    even = lax.ppermute(
        to_even, BOTH, core_pairs(owners, lambda block, core: (block ^ (unit * 2), core))
    )
    return odd, swap_cores(odd, owners), even


def digit_of(block, unit):
    return jnp.bitwise_and(lax.shift_right_logical(block, jnp.int32(unit.bit_length() - 1)), 3)


def here():
    return lax.axis_index("cells"), lax.axis_index("members")


def table_row(number, count):
    return (number % 4) * (count // 4) + number // 4


def strips_of(ref):
    fields, cells = ref.shape[1:]
    lane = lax.broadcasted_iota(jnp.int32, (1, LANES), 1)
    ends = [jnp.where(lane < STEPS, ref[:, f, :LANES], ref[:, f, cells - LANES :]) for f in range(fields)]
    ends = jnp.transpose(jnp.concatenate(ends, axis=0))
    return jnp.concatenate([ends[:STEPS, :], ends[LANES - STEPS :, :]], axis=0)


def pack_kernel(
    send_ref, speed_ref, flag_ref, place_ref, field_ref, value_ref, sigma_ref,
    kept_ref, odd_ref, even_ref, small_ref, table_ref, *, rows, cells, fields,
):
    block, core = here()
    tiles = cells // LANES
    speed, value, sigma = speed_ref[...], value_ref[...], sigma_ref[...]
    flag, place, field = (ref[...].astype(jnp.float32) for ref in (flag_ref, place_ref, field_ref))
    at = 0
    for part in (speed, flag, value, sigma):
        small_ref[at : at + part.shape[0], :] = part
        at += part.shape[0]
    lane = lax.broadcasted_iota(jnp.int32, (1, LANES), 1)
    low = lane < LANES // 2
    toward_left = speed * flag
    toward_right = speed - toward_left
    edge_left = jnp.where(low, toward_left[:1], toward_left[tiles - 1 :])
    edge_right = jnp.where(low, toward_right[:1], toward_right[tiles - 1 :])
    ids = field * float(cells) + place
    weight = 1.0 / (sigma * sigma)
    pull = weight * value
    sub = lax.broadcasted_iota(jnp.int32, (8, LANES), 0)
    empty = jnp.where(sub == 0, -1.0, 0.0)
    empty = jnp.where(sub == 3, edge_left, jnp.where(sub == 4, edge_right, empty))
    listed = [
        jnp.where(sub == 0, ids[r : r + 1], jnp.where(sub == 1, weight[r : r + 1], pull[r : r + 1]))
        for r in range(rows)
    ]
    owners = send_ref.shape[1]
    count = owners // GROUPS
    sends = jnp.broadcast_to(send_ref[...], (8, owners)).astype(jnp.bfloat16)
    sender = lax.broadcasted_iota(jnp.int32, (owners, LANES), 0)
    group = lax.broadcasted_iota(jnp.int32, (owners, LANES), 1) // CAP
    slot = lax.broadcasted_iota(jnp.int32, (8, LANES), 1) % CAP
    one = lambda mask: jnp.where(mask, 1.0, 0.0)
    which = jnp.concatenate(
        [one(sender < group * count + r) for r in range(count)] + [one(sender == group * count + r) for r in range(count)],
        axis=1,
    )
    found = jnp.dot(sends, which.astype(jnp.bfloat16), preferred_element_type=jnp.float32).astype(jnp.int32)
    for r in range(count):
        index = found[:, r * LANES : (r + 1) * LANES] + slot
        held = found[:, (count + r) * LANES : (count + r + 1) * LANES]
        block_of = empty
        inside = (slot < held) & (sub < 3)
        for w in range(rows):
            moved = jnp.take_along_axis(
                listed[w], jnp.bitwise_and(index, LANES - 1), axis=1, mode="promise_in_bounds"
            )
            block_of = jnp.where(inside & (lax.shift_right_logical(index, 7) == w), moved, block_of)
        row = 8 * table_row(r, count)
        table_ref[row : row + 8, :] = block_of
    part = kept_ref.shape[0]
    digit = digit_of(block, 1)
    for out, partner in ((kept_ref, 0), (odd_ref, 1 + 2 * core), (even_ref, 2)):
        out[...] = table_ref[pl.ds(pl.multiple_of(jnp.bitwise_xor(digit, partner) * part, 8), part), :]


def strips_kernel(ensemble_ref, out_ref):
    out_ref[...] = strips_of(ensemble_ref)


def join_kernel(own_ref, other_ref, odd_part, even_part, odd_ref, even_ref):
    strips = jnp.concatenate([own_ref[...], strips_of(other_ref)], axis=0)
    for part, out in ((odd_part, odd_ref), (even_part, even_ref)):
        out[:16, :] = strips
        out[16:, :] = part[...]


def incoming(digit, core, odd, swapped):
    sub = lax.broadcasted_iota(jnp.int32, (8, LANES), 0)
    low = lax.broadcasted_iota(jnp.int32, (8, LANES), 1) < LANES // 2
    direct = jnp.bitwise_xor(jnp.bitwise_and(digit, 1), core) == 0
    result = []
    for part, other_part in ((0, 1), (1, 0), (2, 2)):
        mine = odd[8 * part : 8 * part + 8, :]
        others = swapped[8 * other_part : 8 * other_part + 8, :]
        from_right = jnp.where(direct, mine, others)
        from_left = jnp.where(direct, others, mine)
        result.append(jnp.where(sub < STEPS if part < 2 else low, from_right, from_left))
    return result


def regroup_kernel(
    kept, odd, swapped, even, _, to_odd, to_even, stay, *, unit, into_lanes,
):
    block, core = here()
    after = digit_of(block, unit * 4)
    own, other, coefs = incoming(digit_of(block, unit), core, odd, swapped)
    sub = lax.broadcasted_iota(jnp.int32, (8, LANES), 0)
    lane_group = lax.broadcasted_iota(jnp.int32, (8, LANES), 1) // CAP
    held = kept.shape[0] // 8

    def received(k, at):
        if k == 0:
            return kept[pl.ds(at, 8), :]
        if k == 2:
            return even[pl.ds(16 + at, 8), :]
        mine, others = odd[pl.ds(16 + at, 8), :], swapped[pl.ds(16 + at, 8), :]
        return jnp.where(core == k // 2, mine, others)

    for target in (to_odd, to_even):
        target[0:8, :] = own
        target[8:16, :] = other
    for target, base, partner in ((to_odd, 16, 1 + 2 * core), (to_even, 16, 2), (stay, 0, 0)):
        wanted = jnp.bitwise_xor(after, partner)
        if into_lanes:
            for j in range(held):
                merged = coefs
                for k in range(4):
                    moved = pltpu.roll(received(k, 8 * j), jnp.bitwise_and(k - wanted, 3) * CAP, 1)
                    merged = jnp.where((lane_group == k) & (sub < 3), moved, merged)
                target[base + 8 * j : base + 8 * j + 8, :] = merged
        else:
            rest = held // 4
            for k in range(4):
                for r in range(rest):
                    at = pl.multiple_of((wanted * rest + r) * 8, 8)
                    row = base + 8 * (r * 4 + k)
                    target[row : row + 8, :] = jnp.where(sub < 3, received(k, at), coefs)


def fill_powers(couple_ref, powers_ref):
    fields = couple_ref.shape[0]
    mix = [
        [
            jnp.broadcast_to(couple_ref[f : f + 1, g : g + 1], (1, LANES)) + (1.0 if f == g else 0.0)
            for g in range(fields)
        ]
        for f in range(fields)
    ]
    for _ in range(2):
        mix = [
            [sum(mix[f][h] * mix[h][g] for h in range(fields)) for g in range(fields)]
            for f in range(fields)
        ]
    for f in range(fields):
        for g in range(fields):
            powers_ref[f * fields + g : f * fields + g + 1, :] = mix[f][g]


def powers_of(powers_ref, fields):
    return [[powers_ref[f * fields + g : f * fields + g + 1, :] for g in range(fields)] for f in range(fields)]


def transport(x, from_left, stay, from_right):
    for _ in range(STEPS):
        x = from_left * pltpu.roll(x, 1, 1) + stay * x + from_right * pltpu.roll(x, x.shape[1] - 1, 1)
    return x


def halves_of(x):
    high = x.astype(jnp.bfloat16)
    return high, (x - high.astype(jnp.float32)).astype(jnp.bfloat16)


def band_maker(small_ref, band_ref, cells):
    tiles = cells // LANES
    speed = small_ref[:tiles, :]
    toward_left = speed * small_ref[tiles : 2 * tiles, :]
    toward_right = speed - toward_left

    lane = lax.broadcasted_iota(jnp.int32, (tiles, LANES), 1)

    def shifted(x, by):
        if by == 0:
            return x
        turned = pltpu.roll(x, 1 if by < 0 else LANES - 1, 1)
        carried = pltpu.roll(turned, 1 if by < 0 else tiles - 1, 0)
        return jnp.where(lane == (0 if by < 0 else LANES - 1), carried, turned)

    step = {-1: toward_left + DIFFUSION, 0: 1.0 - 2.0 * DIFFUSION - speed, 1: toward_right + DIFFUSION}
    reach = dict(step)
    for _ in range(STEPS - 1):
        longer = {}
        for e in step:
            for d in reach:
                term = step[e] * shifted(reach[d], e)
                longer[d + e] = longer[d + e] + term if d + e in longer else term
        reach = longer
    row = lax.broadcasted_iota(jnp.int32, (LANES, LANES), 0)
    column = lax.broadcasted_iota(jnp.int32, (LANES, LANES), 1)
    ahead = row - column

    def make(t):
        rule = {d: reach[d][t : t + 1, :] for d in reach}

        def placed(distance, offsets):
            block = jnp.zeros(distance.shape, jnp.float32)
            for d in offsets:
                block = jnp.where(distance == d, rule[d], block)
            return block

        block = jnp.concatenate(
            [
                placed(ahead, range(-STEPS, STEPS + 1)),
                placed(ahead[:8] + LANES, range(1, STEPS + 1)),
                jnp.zeros((LANES - 16, LANES), jnp.float32),
                placed(ahead[LANES - 8 :] - LANES, range(-STEPS, 0)),
            ],
            axis=0,
        )
        for p, piece in enumerate(halves_of(block)):
            band_ref[2 * t * LANES : 2 * (t + 1) * LANES, p * LANES : (p + 1) * LANES] = piece

    return make


def fill_positions(send_ref, slots_ref):
    owners = send_ref.shape[1]
    count = owners // GROUPS
    rows = slots_ref.shape[0] // 2
    row = lax.broadcasted_iota(jnp.int32, (owners, owners), 0)
    column = lax.broadcasted_iota(jnp.int32, (owners, owners), 1)
    held = jnp.where(row == column, jnp.broadcast_to(send_ref[...], (owners, owners)), 0).astype(jnp.float32)
    held = jnp.broadcast_to(jnp.sum(held, axis=1, keepdims=True), (owners, LANES))
    ends = jnp.dot(
        jnp.where(column <= row, 1.0, 0.0).astype(jnp.bfloat16), held.astype(jnp.bfloat16),
        preferred_element_type=jnp.float32,
    )
    for r in range(rows):
        slot = (lax.broadcasted_iota(jnp.int32, (1, LANES), 1) + r * LANES).astype(jnp.float32)
        passed = ends <= slot
        owner = jnp.sum(jnp.where(passed, 1.0, 0.0), axis=0, keepdims=True).astype(jnp.int32)
        start = jnp.sum(jnp.where(passed, held, 0.0), axis=0, keepdims=True)
        group = lax.shift_right_logical(owner, count.bit_length() - 1)
        slots_ref[r : r + 1, :] = jnp.bitwise_and(owner, count - 1)
        slots_ref[rows + r : rows + r + 1, :] = group * CAP + (slot - start).astype(jnp.int32)


def forecast_kernel(extra_ref, source, from_ref, *refs, fields, own):
    members, _, cells = source.shape
    tiles = cells // LANES
    height = fields * members
    if own:
        state, edge, sums_ref, band_ref, powers_ref, split_ref, raw_ref = refs
        fill_powers(extra_ref, powers_ref)
        make_band = band_maker(from_ref, band_ref, cells)
    else:
        send_ref, own_state, state, edge, sums_ref, slots_ref, pieces_ref, split_ref, raw_ref = refs
        powers_ref, band_ref = extra_ref, from_ref
        fill_positions(send_ref, slots_ref)
        core = here()[1]

        def put_pieces(side, f, lanes, value):
            for p, piece in enumerate(halves_of(value)):
                at = pl.multiple_of((f * 2 + p) * 2 * members + side * members, 16)
                pieces_ref[pl.ds(at, members), lanes] = piece

        for f in range(fields):
            put_pieces(core, f, slice(0, cells), own_state[f * members : (f + 1) * members, :])
    low = lax.broadcasted_iota(jnp.int32, (members, LANES), 1) < LANES // 2
    for f in range(fields):
        rows = slice(f * members, (f + 1) * members)
        raw_ref[rows, :] = source[:, f, :]
        x = raw_ref[rows, :]
        edge[rows, :] = jnp.where(
            low,
            pltpu.roll(x[:, :LANES], STEPS, 1),
            pltpu.roll(x[:, cells - LANES :], LANES // 2 + 3 * STEPS, 1),
        )
        for p, piece in enumerate(halves_of(x)):
            split_ref[p * height + f * members : p * height + (f + 1) * members, :] = piece
    mix = powers_of(powers_ref, fields)
    nearer = lax.broadcasted_iota(jnp.int32, (2 * height, LANES), 1) < LANES // 2
    for t in range(tiles):
        lanes, after, before = (
            slice(n % tiles * LANES, (n % tiles + 1) * LANES) for n in (t, t + 1, t - 1)
        )
        if own:
            make_band(t)
        around = jnp.where(nearer, split_ref[:, after], split_ref[:, before])
        product = jnp.dot(
            jnp.concatenate([split_ref[:, lanes], around], axis=1),
            band_ref[2 * t * LANES : 2 * (t + 1) * LANES, :],
            preferred_element_type=jnp.float32,
        )
        moved = (
            product[height:, LANES:] + (product[:height, LANES:] + product[height:, :LANES])
        ) + product[:height, :LANES]
        for f in range(fields):
            value = sum(mix[f][g] * moved[g * members : (g + 1) * members] for g in range(fields))
            state[f * members : (f + 1) * members, lanes] = value
            if not own:
                put_pieces(1 - core, f, lanes, value)
            place = (f * tiles + t) * 8
            sums_ref[place : place + 8, :] = sum(value[8 * i : 8 * i + 8] for i in range(members // 8))


def pieces_of(x):
    high = x.astype(jnp.bfloat16).astype(jnp.float32)
    rest = x - high
    middle = rest.astype(jnp.bfloat16).astype(jnp.float32)
    return high, middle, rest - middle


def sums_kernel(
    powers_ref, small_ref, own_state, own_edge, own_sums, other_state, other_edge, other_sums,
    kept, odd, swapped, even, *refs, owners, units, fields,
):
    carried = refs[: len(units) - 1]
    (
        stay_ref, odd_ref, even_ref, edge_ref, halo_ref, onehot_ref, spread_ref, split_ref,
    ) = refs[len(units) - 1 :]
    states, raw_edges = (own_state, other_state), (own_edge, other_edge)
    block, core = here()
    members = states[0].shape[0] // fields
    cells = states[0].shape[1]
    tiles = cells // LANES
    total = 2 * members
    places = fields * tiles
    has_left = (block > 0).astype(jnp.float32)
    has_right = (block < owners - 1).astype(jnp.float32)
    sub = lax.broadcasted_iota(jnp.int32, (8, LANES), 0)
    lane = lax.broadcasted_iota(jnp.int32, (1, LANES), 1)
    lane8 = lax.broadcasted_iota(jnp.int32, (8, LANES), 1)
    half_lanes = LANES // 2
    low = lane < half_lanes

    strips = incoming(digit_of(block, units[-1]), core, odd, swapped)
    for unit, earlier in reversed(list(zip(units, carried))):
        digit = digit_of(block, unit)
        rows = [earlier[8 * p : 8 * p + 8, :] for p in range(3)]
        picked = []
        for p in range(3):
            from_right = jnp.where(digit != 3, rows[p], strips[p])
            from_left = jnp.where(digit != 0, rows[p], strips[p])
            picked.append(jnp.where(sub < STEPS if p < 2 else lane8 < half_lanes, from_right, from_left))
        strips = picked

    place_ids = lax.broadcasted_iota(jnp.int32, (places, LANES), 0)
    lane_ids = lax.broadcasted_iota(jnp.int32, (LANES, LANES), 0)
    held = kept.shape[0] // 8
    sources = [(kept, 8 * j) for j in range(held)]
    for source, base in ((odd, 16), (swapped, 16), (even, 16)):
        sources += [(source, base + 8 * j) for j in range(held)]
    hits = []
    for n, (source, at) in enumerate(sources):
        local = source[at : at + 1, :].astype(jnp.int32)
        hit = place_ids == lax.shift_right_arithmetic(local, 7)
        hits.append(hit)
        onehot = (lane_ids == jnp.bitwise_and(local, LANES - 1)).astype(jnp.float32)
        lanes = slice(n * LANES, (n + 1) * LANES)
        onehot_ref[:, lanes] = onehot.astype(jnp.bfloat16)
        weight, pull = source[at + 1 : at + 2, :], source[at + 2 : at + 3, :]
        stack = [jnp.where(hit, piece, 0.0) for piece in pieces_of(weight) + pieces_of(pull)]
        spread_ref[:, lanes] = jnp.concatenate(stack, axis=0).astype(jnp.bfloat16)
    placed = lax.dot_general(
        spread_ref[...], onehot_ref[...], (((1,), (1,)), ((), ())), preferred_element_type=jnp.float32
    )
    placed = [placed[p * places : (p + 1) * places] for p in range(6)]
    weight = placed[0] + placed[1] + placed[2]
    pull = placed[3] + placed[4] + placed[5]

    root = jnp.sqrt(weight)
    scale = jnp.where(weight > 0.0, lax.rsqrt(jnp.where(weight > 0.0, weight, 1.0)), 0.0)
    sub16 = lax.broadcasted_iota(jnp.int32, (16, LANES), 0)
    depth = total + 16
    means = {}

    def put(row, lanes, value):
        for p, piece in enumerate(halves_of(value)):
            split_ref[pl.ds(row + p * depth, value.shape[0]), lanes] = piece

    def put_tile(at, sums, halves, into):
        means[at] = jnp.sum(sums, axis=0, keepdims=True) * (1.0 / total)
        lanes = slice(into * LANES, (into + 1) * LANES)
        for half, value in enumerate(halves):
            side = core if half == 0 else 1 - core
            anomaly = (value - means[at]) * root[at : at + 1]
            put(pl.multiple_of(side * members, 16), lanes, anomaly)
        drawn = (pull[at : at + 1] - weight[at : at + 1] * means[at]) * scale[at : at + 1]
        put(total, lanes, jnp.where(sub16 == 0, drawn, 0.0))

    def product_of(first, last):
        lanes = slice(first * LANES, last * LANES)
        anomalies = jnp.concatenate([split_ref[:total, lanes], split_ref[depth : depth + total, lanes]], axis=0)
        return lax.dot_general(
            split_ref[:, lanes], anomalies, (((1,), (1,)), ((), ())), preferred_element_type=jnp.float32
        )

    inner = tiles - 2
    products = []
    for f in range(fields):
        rows = slice(f * members, (f + 1) * members)
        for t in range(1, tiles - 1):
            at = f * tiles + t
            lanes = slice(t * LANES, (t + 1) * LANES)
            sums = own_sums[8 * at : 8 * at + 8, :] + other_sums[8 * at : 8 * at + 8, :]
            put_tile(at, sums, [state[rows, lanes] for state in states], f * inner + t - 1)
        products.append(product_of(f * inner, (f + 1) * inner))

    right_first = half_lanes + 3 * STEPS
    strip_rows = fields * members
    for half in range(2):
        strip = strips[half]
        left = jnp.where(sub < STEPS, pltpu.roll(strip, STEPS, 0) * has_left, 0.0)
        at = right_first % 8
        right = jnp.where(
            (sub >= at) & (sub < at + STEPS), (pltpu.roll(strip, at, 0) if at else strip) * has_right, 0.0
        )
        gap = jnp.zeros((right_first - at - 8, LANES), jnp.float32)
        rest = jnp.zeros((LANES - (right_first - at) - 8, LANES), jnp.float32)
        halo_ref[half * strip_rows : (half + 1) * strip_rows, :] = jnp.transpose(
            jnp.concatenate([left, gap, right, rest], axis=0)
        )
    speed = small_ref[:tiles, :]
    toward_left = speed * small_ref[tiles : 2 * tiles, :]
    toward_right = speed - toward_left
    is_left = lane < STEPS
    is_right = (lane >= right_first) & (lane < right_first + STEPS)
    inside = jnp.where(is_left, has_left, jnp.where(is_right, has_right, 1.0))
    from_outside = (lane8 < STEPS) | ((lane8 >= right_first) & (lane8 < right_first + STEPS))

    def edge_row(rows, row):
        own = jnp.where(
            low, pltpu.roll(rows[:1], STEPS, 1), pltpu.roll(rows[tiles - 1 :], half_lanes + 3 * STEPS, 1)
        )
        left = pltpu.roll(strips[2][row : row + 1], STEPS, 1)
        right = pltpu.roll(strips[2][row : row + 1], right_first, 1)
        return jnp.where(is_left, left, jnp.where(is_right, right, own))

    edge_left = edge_row(toward_left, 3)
    edge_right = edge_row(toward_right, 4)
    from_left = jnp.broadcast_to((edge_left + DIFFUSION) * inside, (8, LANES))
    from_right = jnp.broadcast_to((edge_right + DIFFUSION) * inside, (8, LANES))
    stay = jnp.broadcast_to((1.0 - 2.0 * DIFFUSION - edge_left - edge_right) * inside, (8, LANES))
    mix = powers_of(powers_ref, fields)
    first_sums = [[jnp.zeros((8, LANES), jnp.float32)] * fields for _ in range(2)]
    last_sums = [[jnp.zeros((8, LANES), jnp.float32)] * fields for _ in range(2)]
    for half in range(2):
        state, edge = states[half], raw_edges[half]
        for i in range(members // 8):
            moved = []
            for f in range(fields):
                at = f * members + 8 * i
                x = edge[at : at + 8, :]
                x = jnp.where(from_outside, halo_ref[half * strip_rows + at : half * strip_rows + at + 8, :], x)
                moved.append(transport(x, from_left, stay, from_right))
            for f in range(fields):
                at = f * members + 8 * i
                value = sum(mix[f][g] * moved[g] for g in range(fields))
                first_tile = jnp.where(lane8 < STEPS, pltpu.roll(value, LANES - STEPS, 1), state[at : at + 8, :LANES])
                last_tile = jnp.where(
                    lane8 >= LANES - STEPS,
                    pltpu.roll(value, LANES - right_first, 1),
                    state[at : at + 8, cells - LANES :],
                )
                edge_ref[half * strip_rows + at : half * strip_rows + at + 8, :LANES] = first_tile
                edge_ref[half * strip_rows + at : half * strip_rows + at + 8, LANES:] = last_tile
                first_sums[half][f] = first_sums[half][f] + first_tile
                last_sums[half][f] = last_sums[half][f] + last_tile
    edge_at = fields * inner
    for f in range(fields):
        for n, (t, sums) in enumerate(((0, first_sums), (tiles - 1, last_sums))):
            column = slice(n * LANES, (n + 1) * LANES)
            halves = [
                edge_ref[half * strip_rows + f * members : half * strip_rows + (f + 1) * members, column]
                for half in range(2)
            ]
            put_tile(f * tiles + t, sums[0][f] + sums[1][f], halves, edge_at + 2 * f + n)
    products.append(product_of(edge_at, edge_at + 2 * fields))
    products = sum(products)
    mean = jnp.concatenate([means[at] for at in range(places)], axis=0)
    gram = products[: total + 8] + products[depth : depth + total + 8]
    gram = gram + pltpu.roll(gram, total, 1)
    in_low = lax.broadcasted_iota(jnp.int32, (members, LANES), 1) < total
    folded = jnp.where(in_low, gram[members:total], gram[:members])
    blank = jnp.zeros((stay_ref.shape[0] - members - 1, LANES), jnp.float32)
    for out in (stay_ref, odd_ref, even_ref):
        out[:members, :] = folded
        out[members : members + 1, :] = gram[total : total + 1]
        out[members + 1 :, :] = blank

    found = lax.dot_general(
        jnp.concatenate(pieces_of(mean), axis=0).astype(jnp.bfloat16), onehot_ref[...],
        (((1,), (0,)), ((), ())), preferred_element_type=jnp.float32,
    )
    found = found[:places] + found[places : 2 * places] + found[2 * places :]
    for out, source, partner in ((stay_ref, 0, 0), (odd_ref, 1, 1 + 2 * core), (even_ref, 3, 2)):
        for j in range(held):
            n = source * held + j
            center = jnp.sum(
                jnp.where(hits[n], found[:, n * LANES : (n + 1) * LANES], 0.0), axis=0, keepdims=True
            )
            out[pl.ds(members + 1 + partner * held + j, 1), :] = center


def spread_row(row):
    return jnp.broadcast_to(row, (8, LANES))


def eliminate(rows):
    count = len(rows)
    rows = list(rows)
    sub = lax.broadcasted_iota(jnp.int32, (8, LANES), 0)

    def columns_of(row, b):
        first = 8 * (count + b)
        return [jnp.broadcast_to(row[:, first + k : first + k + 1], (8, LANES)) for k in range(8)]

    upcoming = columns_of(rows[0], 0)
    for b in range(count):
        own = upcoming
        below = {i: columns_of(rows[i], b) for i in range(b + 1, count)}
        if b + 1 < count:
            upcoming = columns_of(rows[b + 1], b + 1)
        for j in range(8):
            scale = lax.rsqrt(spread_row(own[j][j : j + 1, :]))
            upper = spread_row(rows[b][j : j + 1, :]) * scale
            lower = own[j] * scale
            factors = {k: spread_row(lower[k : k + 1, :]) for k in range(j + 1, 8)}
            for k in range(j + 1, 8):
                own[k] = own[k] - lower * factors[k]
            rows[b] = jnp.where(sub == j, upper, rows[b] - jnp.where(sub > j, lower, 0.0) * upper)
            for i in range(b + 1, count):
                here = below[i][j] * scale
                if i == b + 1:
                    for k in range(8):
                        upcoming[k] = upcoming[k] - here * spread_row(here[k : k + 1, :])
                for k in range(j + 1, 8):
                    below[i][k] = below[i][k] - here * factors[k]
                rows[i] = rows[i] - here * upper
    return rows


def analysis_kernel(
    split_ref, edge_ref, small_ref, slots_ref, kept, odd, swapped, even,
    analysis_ref, innovation_ref, center_ref, pieces_ref, result_ref, departure_ref, sems, *, units, obs_rows, count,
):
    block, core = here()
    members, fields, cells = analysis_ref.shape
    total = 2 * members
    strip_rows = fields * members
    for f in range(fields):
        for half in range(2):
            rows = slice(half * strip_rows + f * members, half * strip_rows + (f + 1) * members)
            side = core if half == 0 else 1 - core
            for p, piece in enumerate(halves_of(edge_ref[rows, :])):
                at = pl.multiple_of((f * 2 + p) * total + side * members, 16)
                pieces_ref[pl.ds(at, members), :] = piece
    head = members + 1
    sums = (kept[:head, :] + even[:head, :]) + (odd[:head, :] + swapped[:head, :])
    returned = kept.shape[0] - head
    center_ref[:returned, :] = kept[head:, :]
    center_ref[returned : 2 * returned, :] = jnp.where(core == 0, odd[head:, :], swapped[head:, :])
    center_ref[2 * returned : 3 * returned, :] = even[head:, :]
    center_ref[3 * returned :, :] = jnp.where(core == 0, swapped[head:, :], odd[head:, :])
    lane = lax.broadcasted_iota(jnp.int32, (8, LANES), 1)
    sub = lax.broadcasted_iota(jnp.int32, (8, LANES), 0)
    shifted = pltpu.roll(sums[:members], total, 1)
    rows = []
    for b in range(total // 8):
        at = 8 * b
        source = sums[at : at + 8] if at < members else shifted[at - members : at - members + 8]
        own = jnp.where(lane == sub + at + total, total - 1.0, 0.0)
        unit = jnp.where(lane == sub + at, 1.0, 0.0)
        rows.append(jnp.where(lane >= total, source + own, unit))
    rows = eliminate(rows)
    cross = sums[members : members + 1]
    inverse = [jnp.where(lane < total, r, 0.0) for r in rows]
    carried = [jnp.sum(r * cross, axis=1, keepdims=True) for r in inverse]
    row_sums = [jnp.sum(r, axis=1, keepdims=True) for r in inverse]
    row_means = [r * (1.0 / total) for r in row_sums]
    weights = jnp.sum(sum(r * c for r, c in zip(inverse, carried)), axis=0, keepdims=True)
    column_mean = jnp.sum(sum(inverse), axis=0, keepdims=True) * (1.0 / total)
    grand = jnp.sum(sum(row_means), axis=0, keepdims=True) * (1.0 / total)
    weights = weights - jnp.sum(sum(r * c for r, c in zip(row_means, carried)), axis=0, keepdims=True)
    root = math.sqrt(total - 1.0)
    add = weights + 1.0 / total - root * (column_mean - grand)
    count_here = members // 8
    mixing = [
        root * jnp.where(core == 0, inverse[b] - row_means[b], inverse[b + count_here] - row_means[b + count_here]) + add
        for b in range(count_here)
    ]
    high, rest = halves_of(jnp.concatenate(mixing, axis=0)[:, :total])
    mixing = jnp.concatenate(
        [jnp.concatenate([high, high], axis=1), jnp.concatenate([rest, rest], axis=1)], axis=0
    )
    copies = []
    width = cells // 2
    for n in range(2):
        lanes = slice(n * width, (n + 1) * width)
        for f in range(fields):
            rows = slice(f * 2 * total, (f + 1) * 2 * total)
            if n == 0:
                states = [pieces_ref[rows, :LANES], split_ref[rows, LANES:width]]
            else:
                states = [split_ref[rows, width : cells - LANES], pieces_ref[rows, LANES:]]
            product = jnp.dot(mixing, jnp.concatenate(states, axis=1), preferred_element_type=jnp.float32)
            result_ref[:, f, lanes] = product[:members] + product[members:]
        copies.append(
            pltpu.make_async_copy(
                result_ref.at[:, :, pl.ds(n * width, width)],
                analysis_ref.at[:, :, pl.ds(n * width, width)],
                sems.at[n],
            )
        )
        copies[-1].start()

    held = count // 4
    lane_group = lane // CAP
    table = []
    for r in range(count):
        merged = jnp.zeros((1, LANES), jnp.float32)
        for group in range(GROUPS):
            owner = group * count + r
            way = [jnp.bitwise_xor(digit_of(block, unit), (owner // unit) % 4) for unit in units]
            row = way[-1] * held
            if len(units) > 2:
                row = row + sum(step * 4**n for n, step in enumerate(way[:-2]))
            size = 4 * held
            for step in reversed(way[1:-1]):
                row = row + step * size
                size = size * 4
            row = row + way[0] * returned
            line = center_ref[pl.ds(row, 1), :]
            moved = pltpu.roll(line, jnp.bitwise_and(group - way[-2], 3) * CAP, 1)
            merged = jnp.where(lane_group[:1] == group, moved, merged)
        table.append(jnp.broadcast_to(merged, (8, LANES)))
    for r in range(obs_rows):
        center = jnp.zeros((8, LANES), jnp.float32)
        lanes = jnp.broadcast_to(slots_ref[obs_rows + r : obs_rows + r + 1, :], (8, LANES))
        for n in range(count):
            found = jnp.take_along_axis(table[n], lanes, axis=1, mode="promise_in_bounds")
            center = jnp.where(slots_ref[r : r + 1, :] == n, found, center)
        center = center[:1]
        at = small_ref.shape[0] - 2 * obs_rows + r
        value, sigma = small_ref[at : at + 1, :], small_ref[at + obs_rows : at + obs_rows + 1, :]
        departure_ref[r : r + 1, :] = (value - center) / sigma
    copies.append(pltpu.make_async_copy(departure_ref, innovation_ref, sems.at[2]))
    copies[-1].start()
    for copy in copies:
        copy.wait()


def shards(
    ensemble, speed, direction, couple, obs_place, obs_field, obs_value, obs_sigma, send_count
):
    members, fields, cells = ensemble.shape
    owners = lax.axis_size("cells")
    total = members * lax.axis_size("members")
    obs = obs_place.shape[0]
    obs_rows = obs // LANES
    tiles = cells // LANES
    places = fields * tiles
    units = stage_units(owners)
    block = lax.axis_index("cells").astype(jnp.int32)
    core = lax.axis_index("members").astype(jnp.int32)
    small = (
        speed.reshape(tiles, LANES), direction.reshape(tiles, LANES),
        *(x.reshape(obs_rows, LANES) for x in (obs_place, obs_field, obs_value, obs_sigma)),
    )
    whole = pl.BlockSpec(memory_space=pltpu.VMEM)
    params = pltpu.CompilerParams(vmem_limit_bytes=VMEM_BYTES)
    real = jnp.float32

    table_rows = 8 * (owners // GROUPS)
    part = table_rows // 4
    other = swap_cores(ensemble, owners)
    rows_of = lambda count: pl.BlockSpec((count, LANES), lambda i: (0, 0))
    small_rows = 2 * tiles + 2 * obs_rows
    strips = pl.pallas_call(
        strips_kernel,
        out_shape=jax.ShapeDtypeStruct((8, LANES), real),
        in_specs=[whole],
        out_specs=whole,
        compiler_params=params,
        name="strips",
    )(ensemble)
    kept, to_odd, to_even, small = pl.pallas_call(
        functools.partial(pack_kernel, rows=obs_rows, cells=cells, fields=fields),
        out_shape=(jax.ShapeDtypeStruct((part, LANES), real),) * 3
        + (jax.ShapeDtypeStruct((small_rows, LANES), real),),
        grid=(1,),
        in_specs=[whole] + [rows_of(x.shape[0]) for x in small],
        out_specs=(whole,) * 4,
        scratch_shapes=[pltpu.VMEM((table_rows, LANES), real)],
        compiler_params=params,
        name="pack",
    )(send_count, *small)
    to_odd, to_even = pl.pallas_call(
        join_kernel,
        out_shape=(jax.ShapeDtypeStruct((16 + part, LANES), real),) * 2,
        in_specs=[whole] * 4,
        out_specs=(whole,) * 2,
        compiler_params=params,
        name="join",
    )(strips, other, to_odd, to_even)

    strip_rows = fields * members
    band = jax.ShapeDtypeStruct((2 * cells, 2 * LANES), jnp.bfloat16)

    powers = jax.ShapeDtypeStruct((fields * fields, LANES), real)
    slots = jax.ShapeDtypeStruct((2 * obs_rows, LANES), jnp.int32)

    pieces = jax.ShapeDtypeStruct((fields * 2 * total, cells), jnp.bfloat16)

    def forecast(operands, extra, own):
        return pl.pallas_call(
            functools.partial(forecast_kernel, fields=fields, own=own),
            out_shape=(
                jax.ShapeDtypeStruct((strip_rows, cells), real),
                jax.ShapeDtypeStruct((strip_rows, LANES), real),
                jax.ShapeDtypeStruct((places * 8, LANES), real),
            )
            + extra,
            in_specs=[whole] * len(operands),
            out_specs=(whole,) * (3 + len(extra)),
            scratch_shapes=[pltpu.VMEM((2 * strip_rows, cells), jnp.bfloat16), pltpu.VMEM((strip_rows, cells), real)],
            compiler_params=params,
            cost_estimate=pl.CostEstimate(
                flops=80 * strip_rows * cells, bytes_accessed=8 * strip_rows * cells, transcendentals=0
            ),
            name="forecast",
        )(*operands)

    *own_forecast, rule, mixed = forecast((couple, ensemble, small), (band, powers), True)
    carried = []
    for n, unit in enumerate(units):
        arrived = exchange(to_odd, to_even, owners, unit)
        if n + 1 < len(units):
            to_odd, to_even, kept = pl.pallas_call(
                functools.partial(regroup_kernel, unit=unit, into_lanes=n + 2 == len(units)),
                out_shape=tuple(jax.ShapeDtypeStruct(x.shape, real) for x in (to_odd, to_even, kept)),
                in_specs=[whole] * 4 + [pl.BlockSpec(memory_space=pl.ANY)],
                out_specs=(whole,) * 3,
                compiler_params=params,
                name="regroup",
            )(kept, *arrived, own_forecast[2])
            carried.append(to_odd)
    *other_forecast, slots_of, split = forecast(
        (mixed, other, rule, send_count, own_forecast[0]), (slots, pieces), False
    )

    held = kept.shape[0] // 8
    sums_rows = -(-(members + 1 + 4 * held) // 8) * 8
    all_slots = 4 * held * LANES
    sums = jax.ShapeDtypeStruct((sums_rows, LANES), real)
    stay, to_odd, to_even, edges = pl.pallas_call(
        functools.partial(sums_kernel, owners=owners, units=units, fields=fields),
        out_shape=(sums, sums, sums, jax.ShapeDtypeStruct((2 * strip_rows, 2 * LANES), real)),
        in_specs=[whole] * (12 + len(carried)),
        out_specs=(whole,) * 4,
        scratch_shapes=[
            pltpu.VMEM((2 * strip_rows, LANES), real),
            pltpu.VMEM((LANES, all_slots), jnp.bfloat16),
            pltpu.VMEM((6 * places, all_slots), jnp.bfloat16),
            pltpu.VMEM((2 * (total + 16), fields * cells), jnp.bfloat16),
        ],
        compiler_params=params,
        name="sums",
    )(
        mixed, small, *own_forecast, *other_forecast, kept, *arrived, *carried,
    )

    head = members + 1
    used = head + 4 * held
    for n, unit in enumerate(reversed(units)):
        odd, swapped, even = exchange(to_odd, to_even, owners, unit)
        if n + 1 < len(units):
            added = (stay + even) + (odd + swapped)
            if n > 0:
                first = jnp.where(core == 0, odd, swapped)
                third = jnp.where(core == 0, swapped, odd)
                added = jnp.concatenate(
                    [added[:head]] + [x[head:used] for x in (stay, first, even, third)], axis=0
                )
                used = added.shape[0]
            stay = to_odd = to_even = added

    analysis, innovation = pl.pallas_call(
        functools.partial(analysis_kernel, units=units, obs_rows=obs_rows, count=owners // GROUPS),
        out_shape=(
            jax.ShapeDtypeStruct((members, fields, cells), real),
            jax.ShapeDtypeStruct((obs_rows, LANES), real),
        ),
        in_specs=[whole] * 8,
        out_specs=(pl.BlockSpec(memory_space=pl.ANY),) * 2,
        scratch_shapes=[
            pltpu.VMEM((4 * (stay.shape[0] - head), LANES), real),
            pltpu.VMEM((fields * 2 * total, 2 * LANES), jnp.bfloat16),
            pltpu.VMEM((members, fields, cells), real),
            pltpu.VMEM((obs_rows, LANES), real),
            pltpu.SemaphoreType.DMA((3,)),
        ],
        compiler_params=params,
        name="analysis",
    )(
        split, edges, small, slots_of,
        stay, odd, swapped, even,
    )
    return (analysis, innovation.reshape(obs))


def solution(mesh):
    return jax.shard_map(
        shards,
        mesh=mesh,
        in_specs=(
            P("members", None, "cells"),
            P("cells"),
            P("cells"),
            P(),
            P("cells"),
            P("cells"),
            P("cells"),
            P("cells"),
            P("cells", None),
        ),
        out_specs=(P("members", None, "cells"), P("cells")),
        check_vma=False,
    )
```

```python
import functools
import math

import jax
import jax.numpy as jnp
from jax import lax
from jax.experimental import pallas as pl
from jax.experimental.pallas import tpu as pltpu
from jax.sharding import PartitionSpec as P

STEPS = 4
DIFFUSION = 0.05
LANES = 128
CAP = 32
GROUPS = LANES // CAP
BOTH = ("cells", "members")
EXACT = lax.Precision.HIGHEST
VMEM_BYTES = 48 * 1024 * 1024


def core_pairs(owners, place):
    pairs = []
    for block in range(owners):
        for core in range(2):
            to_block, to_core = place(block, core)
            pairs.append((block * 2 + core, to_block * 2 + to_core))
    return pairs


def stage_units(owners):
    units = []
    unit = 1
    while unit < owners:
        units.append(unit)
        unit *= 4
    if unit != owners or len(units) < 2:
        raise ValueError("blocks not 4**n")
    return units


def swap_cores(x, owners):
    return lax.ppermute(x, BOTH, core_pairs(owners, lambda block, core: (block, 1 - core)))


def exchange(to_odd, to_even, owners, unit):
    odd = lax.ppermute(
        to_odd, BOTH, core_pairs(owners, lambda block, core: (block ^ (unit * (1 + 2 * core)), core))
    )
    even = lax.ppermute(
        to_even, BOTH, core_pairs(owners, lambda block, core: (block ^ (unit * 2), core))
    )
    return odd, swap_cores(odd, owners), even


def digit_of(block, unit):
    return jnp.bitwise_and(lax.shift_right_logical(block, jnp.int32(unit.bit_length() - 1)), 3)


def here():
    return lax.axis_index("cells"), lax.axis_index("members")


def table_row(number, count):
    return (number % 4) * (count // 4) + number // 4


def strips_of(ref):
    fields, cells = ref.shape[1:]
    lane = lax.broadcasted_iota(jnp.int32, (1, LANES), 1)
    ends = [jnp.where(lane < STEPS, ref[:, f, :LANES], ref[:, f, cells - LANES :]) for f in range(fields)]
    ends = jnp.transpose(jnp.concatenate(ends, axis=0))
    return jnp.concatenate([ends[:STEPS, :], ends[LANES - STEPS :, :]], axis=0)


def pack_kernel(
    send_ref, speed_ref, flag_ref, place_ref, field_ref, value_ref, sigma_ref,
    kept_ref, odd_ref, even_ref, small_ref, table_ref, *, rows, cells, fields,
):
    block, core = here()
    tiles = cells // LANES
    speed, value, sigma = speed_ref[...], value_ref[...], sigma_ref[...]
    flag, place, field = (ref[...].astype(jnp.float32) for ref in (flag_ref, place_ref, field_ref))
    at = 0
    for part in (speed, flag, value, sigma):
        small_ref[at : at + part.shape[0], :] = part
        at += part.shape[0]
    lane = lax.broadcasted_iota(jnp.int32, (1, LANES), 1)
    low = lane < LANES // 2
    toward_left = speed * flag
    toward_right = speed - toward_left
    edge_left = jnp.where(low, toward_left[:1], toward_left[tiles - 1 :])
    edge_right = jnp.where(low, toward_right[:1], toward_right[tiles - 1 :])
    ids = field * float(cells) + place
    weight = 1.0 / (sigma * sigma)
    pull = weight * value
    sub = lax.broadcasted_iota(jnp.int32, (8, LANES), 0)
    empty = jnp.where(sub == 0, -1.0, 0.0)
    empty = jnp.where(sub == 3, edge_left, jnp.where(sub == 4, edge_right, empty))
    listed = [
        jnp.where(sub == 0, ids[r : r + 1], jnp.where(sub == 1, weight[r : r + 1], pull[r : r + 1]))
        for r in range(rows)
    ]
    owners = send_ref.shape[1]
    count = owners // GROUPS
    sends = jnp.broadcast_to(send_ref[...], (8, owners)).astype(jnp.bfloat16)
    sender = lax.broadcasted_iota(jnp.int32, (owners, LANES), 0)
    group = lax.broadcasted_iota(jnp.int32, (owners, LANES), 1) // CAP
    slot = lax.broadcasted_iota(jnp.int32, (8, LANES), 1) % CAP
    one = lambda mask: jnp.where(mask, 1.0, 0.0)
    which = jnp.concatenate(
        [one(sender < group * count + r) for r in range(count)] + [one(sender == group * count + r) for r in range(count)],
        axis=1,
    )
    found = jnp.dot(sends, which.astype(jnp.bfloat16), preferred_element_type=jnp.float32).astype(jnp.int32)
    for r in range(count):
        index = found[:, r * LANES : (r + 1) * LANES] + slot
        held = found[:, (count + r) * LANES : (count + r + 1) * LANES]
        block_of = empty
        inside = (slot < held) & (sub < 3)
        for w in range(rows):
            moved = jnp.take_along_axis(
                listed[w], jnp.bitwise_and(index, LANES - 1), axis=1, mode="promise_in_bounds"
            )
            block_of = jnp.where(inside & (lax.shift_right_logical(index, 7) == w), moved, block_of)
        row = 8 * table_row(r, count)
        table_ref[row : row + 8, :] = block_of
    part = kept_ref.shape[0]
    digit = digit_of(block, 1)
    for out, partner in ((kept_ref, 0), (odd_ref, 1 + 2 * core), (even_ref, 2)):
        out[...] = table_ref[pl.ds(pl.multiple_of(jnp.bitwise_xor(digit, partner) * part, 8), part), :]


def strips_kernel(ensemble_ref, out_ref):
    out_ref[...] = strips_of(ensemble_ref)


def join_kernel(own_ref, other_ref, odd_part, even_part, odd_ref, even_ref):
    strips = jnp.concatenate([own_ref[...], strips_of(other_ref)], axis=0)
    for part, out in ((odd_part, odd_ref), (even_part, even_ref)):
        out[:16, :] = strips
        out[16:, :] = part[...]


def incoming(digit, core, odd, swapped):
    sub = lax.broadcasted_iota(jnp.int32, (8, LANES), 0)
    low = lax.broadcasted_iota(jnp.int32, (8, LANES), 1) < LANES // 2
    direct = jnp.bitwise_xor(jnp.bitwise_and(digit, 1), core) == 0
    result = []
    for part, other_part in ((0, 1), (1, 0), (2, 2)):
        mine = odd[8 * part : 8 * part + 8, :]
        others = swapped[8 * other_part : 8 * other_part + 8, :]
        from_right = jnp.where(direct, mine, others)
        from_left = jnp.where(direct, others, mine)
        result.append(jnp.where(sub < STEPS if part < 2 else low, from_right, from_left))
    return result


def regroup_kernel(
    kept, odd, swapped, even, _, to_odd, to_even, stay, *, unit, into_lanes,
):
    block, core = here()
    after = digit_of(block, unit * 4)
    own, other, coefs = incoming(digit_of(block, unit), core, odd, swapped)
    sub = lax.broadcasted_iota(jnp.int32, (8, LANES), 0)
    lane_group = lax.broadcasted_iota(jnp.int32, (8, LANES), 1) // CAP
    held = kept.shape[0] // 8

    def received(k, at):
        if k == 0:
            return kept[pl.ds(at, 8), :]
        if k == 2:
            return even[pl.ds(16 + at, 8), :]
        mine, others = odd[pl.ds(16 + at, 8), :], swapped[pl.ds(16 + at, 8), :]
        return jnp.where(core == k // 2, mine, others)

    for target in (to_odd, to_even):
        target[0:8, :] = own
        target[8:16, :] = other
    for target, base, partner in ((to_odd, 16, 1 + 2 * core), (to_even, 16, 2), (stay, 0, 0)):
        wanted = jnp.bitwise_xor(after, partner)
        if into_lanes:
            for j in range(held):
                merged = coefs
                for k in range(4):
                    moved = pltpu.roll(received(k, 8 * j), jnp.bitwise_and(k - wanted, 3) * CAP, 1)
                    merged = jnp.where((lane_group == k) & (sub < 3), moved, merged)
                target[base + 8 * j : base + 8 * j + 8, :] = merged
        else:
            rest = held // 4
            for k in range(4):
                for r in range(rest):
                    at = pl.multiple_of((wanted * rest + r) * 8, 8)
                    row = base + 8 * (r * 4 + k)
                    target[row : row + 8, :] = jnp.where(sub < 3, received(k, at), coefs)


def fill_powers(couple_ref, powers_ref):
    fields = couple_ref.shape[0]
    mix = [
        [
            jnp.broadcast_to(couple_ref[f : f + 1, g : g + 1], (1, LANES)) + (1.0 if f == g else 0.0)
            for g in range(fields)
        ]
        for f in range(fields)
    ]
    for _ in range(2):
        mix = [
            [sum(mix[f][h] * mix[h][g] for h in range(fields)) for g in range(fields)]
            for f in range(fields)
        ]
    for f in range(fields):
        for g in range(fields):
            powers_ref[f * fields + g : f * fields + g + 1, :] = mix[f][g]


def powers_of(powers_ref, fields):
    return [[powers_ref[f * fields + g : f * fields + g + 1, :] for g in range(fields)] for f in range(fields)]


def transport(x, from_left, stay, from_right):
    for _ in range(STEPS):
        x = from_left * pltpu.roll(x, 1, 1) + stay * x + from_right * pltpu.roll(x, x.shape[1] - 1, 1)
    return x


def halves_of(x):
    high = x.astype(jnp.bfloat16)
    return high, (x - high.astype(jnp.float32)).astype(jnp.bfloat16)


def band_maker(small_ref, band_ref, cells):
    tiles = cells // LANES
    speed = small_ref[:tiles, :]
    toward_left = speed * small_ref[tiles : 2 * tiles, :]
    toward_right = speed - toward_left

    lane = lax.broadcasted_iota(jnp.int32, (tiles, LANES), 1)

    def shifted(x, by):
        if by == 0:
            return x
        turned = pltpu.roll(x, 1 if by < 0 else LANES - 1, 1)
        carried = pltpu.roll(turned, 1 if by < 0 else tiles - 1, 0)
        return jnp.where(lane == (0 if by < 0 else LANES - 1), carried, turned)

    step = {-1: toward_left + DIFFUSION, 0: 1.0 - 2.0 * DIFFUSION - speed, 1: toward_right + DIFFUSION}
    reach = dict(step)
    for _ in range(STEPS - 1):
        longer = {}
        for e in step:
            for d in reach:
                term = step[e] * shifted(reach[d], e)
                longer[d + e] = longer[d + e] + term if d + e in longer else term
        reach = longer
    row = lax.broadcasted_iota(jnp.int32, (LANES, LANES), 0)
    column = lax.broadcasted_iota(jnp.int32, (LANES, LANES), 1)
    ahead = row - column

    def make(t):
        rule = {d: reach[d][t : t + 1, :] for d in reach}

        def placed(distance, offsets):
            block = jnp.zeros(distance.shape, jnp.float32)
            for d in offsets:
                block = jnp.where(distance == d, rule[d], block)
            return block

        block = jnp.concatenate(
            [
                placed(ahead, range(-STEPS, STEPS + 1)),
                placed(ahead[:8] + LANES, range(1, STEPS + 1)),
                jnp.zeros((LANES - 16, LANES), jnp.float32),
                placed(ahead[LANES - 8 :] - LANES, range(-STEPS, 0)),
            ],
            axis=0,
        )
        for p, piece in enumerate(halves_of(block)):
            band_ref[2 * t * LANES : 2 * (t + 1) * LANES, p * LANES : (p + 1) * LANES] = piece

    return make


def fill_positions(send_ref, slots_ref):
    owners = send_ref.shape[1]
    count = owners // GROUPS
    rows = slots_ref.shape[0] // 2
    row = lax.broadcasted_iota(jnp.int32, (owners, owners), 0)
    column = lax.broadcasted_iota(jnp.int32, (owners, owners), 1)
    held = jnp.where(row == column, jnp.broadcast_to(send_ref[...], (owners, owners)), 0).astype(jnp.float32)
    held = jnp.broadcast_to(jnp.sum(held, axis=1, keepdims=True), (owners, LANES))
    ends = jnp.dot(
        jnp.where(column <= row, 1.0, 0.0).astype(jnp.bfloat16), held.astype(jnp.bfloat16),
        preferred_element_type=jnp.float32,
    )
    for r in range(rows):
        slot = (lax.broadcasted_iota(jnp.int32, (1, LANES), 1) + r * LANES).astype(jnp.float32)
        passed = ends <= slot
        owner = jnp.sum(jnp.where(passed, 1.0, 0.0), axis=0, keepdims=True).astype(jnp.int32)
        start = jnp.sum(jnp.where(passed, held, 0.0), axis=0, keepdims=True)
        group = lax.shift_right_logical(owner, count.bit_length() - 1)
        slots_ref[r : r + 1, :] = jnp.bitwise_and(owner, count - 1)
        slots_ref[rows + r : rows + r + 1, :] = group * CAP + (slot - start).astype(jnp.int32)


def rule_kernel(couple_ref, small_ref, band_ref, powers_ref, *, tiles):
    fill_powers(couple_ref, powers_ref)
    make_band = band_maker(small_ref, band_ref, tiles * LANES)
    for t in range(tiles):
        make_band(t)


def forecast_kernel(powers_ref, source, band_ref, *refs, fields, own):
    members, _, cells = source.shape
    tiles = cells // LANES
    height = fields * members
    if own:
        state, edge, sums_ref, split_ref, raw_ref = refs
    else:
        send_ref, own_state, state, edge, sums_ref, slots_ref, pieces_ref, split_ref, raw_ref = refs
        fill_positions(send_ref, slots_ref)
        core = here()[1]

        def put_pieces(side, f, lanes, value):
            for p, piece in enumerate(halves_of(value)):
                at = pl.multiple_of((f * 2 + p) * 2 * members + side * members, 16)
                pieces_ref[pl.ds(at, members), lanes] = piece

        for f in range(fields):
            put_pieces(core, f, slice(0, cells), own_state[f * members : (f + 1) * members, :])
    low = lax.broadcasted_iota(jnp.int32, (members, LANES), 1) < LANES // 2
    for f in range(fields):
        rows = slice(f * members, (f + 1) * members)
        raw_ref[rows, :] = source[:, f, :]
        x = raw_ref[rows, :]
        edge[rows, :] = jnp.where(
            low,
            pltpu.roll(x[:, :LANES], STEPS, 1),
            pltpu.roll(x[:, cells - LANES :], LANES // 2 + 3 * STEPS, 1),
        )
        for p, piece in enumerate(halves_of(x)):
            split_ref[p * height + f * members : p * height + (f + 1) * members, :] = piece
    mix = powers_of(powers_ref, fields)
    nearer = lax.broadcasted_iota(jnp.int32, (2 * height, LANES), 1) < LANES // 2
    for t in range(tiles):
        lanes, after, before = (
            slice(n % tiles * LANES, (n % tiles + 1) * LANES) for n in (t, t + 1, t - 1)
        )
        around = jnp.where(nearer, split_ref[:, after], split_ref[:, before])
        product = jnp.dot(
            jnp.concatenate([split_ref[:, lanes], around], axis=1),
            band_ref[2 * t * LANES : 2 * (t + 1) * LANES, :],
            preferred_element_type=jnp.float32,
        )
        moved = (
            product[height:, LANES:] + (product[:height, LANES:] + product[height:, :LANES])
        ) + product[:height, :LANES]
        for f in range(fields):
            value = sum(mix[f][g] * moved[g * members : (g + 1) * members] for g in range(fields))
            state[f * members : (f + 1) * members, lanes] = value
            if not own:
                put_pieces(1 - core, f, lanes, value)
            place = (f * tiles + t) * 8
            sums_ref[place : place + 8, :] = sum(value[8 * i : 8 * i + 8] for i in range(members // 8))


def pieces_of(x):
    high = x.astype(jnp.bfloat16).astype(jnp.float32)
    rest = x - high
    middle = rest.astype(jnp.bfloat16).astype(jnp.float32)
    return high, middle, rest - middle


def sums_kernel(
    powers_ref, small_ref, own_state, own_edge, own_sums, other_state, other_edge, other_sums,
    kept, odd, swapped, even, *refs, owners, units, fields,
):
    carried = refs[: len(units) - 1]
    (
        stay_ref, odd_ref, even_ref, edge_ref, halo_ref, onehot_ref, spread_ref, split_ref,
    ) = refs[len(units) - 1 :]
    states, raw_edges = (own_state, other_state), (own_edge, other_edge)
    block, core = here()
    members = states[0].shape[0] // fields
    cells = states[0].shape[1]
    tiles = cells // LANES
    total = 2 * members
    places = fields * tiles
    has_left = (block > 0).astype(jnp.float32)
    has_right = (block < owners - 1).astype(jnp.float32)
    sub = lax.broadcasted_iota(jnp.int32, (8, LANES), 0)
    lane = lax.broadcasted_iota(jnp.int32, (1, LANES), 1)
    lane8 = lax.broadcasted_iota(jnp.int32, (8, LANES), 1)
    half_lanes = LANES // 2
    low = lane < half_lanes

    strips = incoming(digit_of(block, units[-1]), core, odd, swapped)
    for unit, earlier in reversed(list(zip(units, carried))):
        digit = digit_of(block, unit)
        rows = [earlier[8 * p : 8 * p + 8, :] for p in range(3)]
        picked = []
        for p in range(3):
            from_right = jnp.where(digit != 3, rows[p], strips[p])
            from_left = jnp.where(digit != 0, rows[p], strips[p])
            picked.append(jnp.where(sub < STEPS if p < 2 else lane8 < half_lanes, from_right, from_left))
        strips = picked

    place_ids = lax.broadcasted_iota(jnp.int32, (places, LANES), 0)
    lane_ids = lax.broadcasted_iota(jnp.int32, (LANES, LANES), 0)
    held = kept.shape[0] // 8
    sources = [(kept, 8 * j) for j in range(held)]
    for source, base in ((odd, 16), (swapped, 16), (even, 16)):
        sources += [(source, base + 8 * j) for j in range(held)]
    hits = []
    for n, (source, at) in enumerate(sources):
        local = source[at : at + 1, :].astype(jnp.int32)
        hit = place_ids == lax.shift_right_arithmetic(local, 7)
        hits.append(hit)
        onehot = (lane_ids == jnp.bitwise_and(local, LANES - 1)).astype(jnp.float32)
        lanes = slice(n * LANES, (n + 1) * LANES)
        onehot_ref[:, lanes] = onehot.astype(jnp.bfloat16)
        weight, pull = source[at + 1 : at + 2, :], source[at + 2 : at + 3, :]
        stack = [jnp.where(hit, piece, 0.0) for piece in pieces_of(weight) + pieces_of(pull)]
        spread_ref[:, lanes] = jnp.concatenate(stack, axis=0).astype(jnp.bfloat16)
    placed = lax.dot_general(
        spread_ref[...], onehot_ref[...], (((1,), (1,)), ((), ())), preferred_element_type=jnp.float32
    )
    placed = [placed[p * places : (p + 1) * places] for p in range(6)]
    weight = placed[0] + placed[1] + placed[2]
    pull = placed[3] + placed[4] + placed[5]

    root = jnp.sqrt(weight)
    scale = jnp.where(weight > 0.0, lax.rsqrt(jnp.where(weight > 0.0, weight, 1.0)), 0.0)
    sub16 = lax.broadcasted_iota(jnp.int32, (16, LANES), 0)
    depth = total + 16
    means = {}

    def put(row, lanes, value):
        for p, piece in enumerate(halves_of(value)):
            split_ref[pl.ds(row + p * depth, value.shape[0]), lanes] = piece

    def put_tile(at, sums, halves, into):
        means[at] = jnp.sum(sums, axis=0, keepdims=True) * (1.0 / total)
        lanes = slice(into * LANES, (into + 1) * LANES)
        for half, value in enumerate(halves):
            side = core if half == 0 else 1 - core
            anomaly = (value - means[at]) * root[at : at + 1]
            put(pl.multiple_of(side * members, 16), lanes, anomaly)
        drawn = (pull[at : at + 1] - weight[at : at + 1] * means[at]) * scale[at : at + 1]
        put(total, lanes, jnp.where(sub16 == 0, drawn, 0.0))

    def product_of(first, last):
        lanes = slice(first * LANES, last * LANES)
        anomalies = jnp.concatenate([split_ref[:total, lanes], split_ref[depth : depth + total, lanes]], axis=0)
        return lax.dot_general(
            split_ref[:, lanes], anomalies, (((1,), (1,)), ((), ())), preferred_element_type=jnp.float32
        )

    inner = tiles - 2
    products = []
    for f in range(fields):
        rows = slice(f * members, (f + 1) * members)
        for t in range(1, tiles - 1):
            at = f * tiles + t
            lanes = slice(t * LANES, (t + 1) * LANES)
            sums = own_sums[8 * at : 8 * at + 8, :] + other_sums[8 * at : 8 * at + 8, :]
            put_tile(at, sums, [state[rows, lanes] for state in states], f * inner + t - 1)
        products.append(product_of(f * inner, (f + 1) * inner))

    right_first = half_lanes + 3 * STEPS
    strip_rows = fields * members
    for half in range(2):
        strip = strips[half]
        left = jnp.where(sub < STEPS, pltpu.roll(strip, STEPS, 0) * has_left, 0.0)
        at = right_first % 8
        right = jnp.where(
            (sub >= at) & (sub < at + STEPS), (pltpu.roll(strip, at, 0) if at else strip) * has_right, 0.0
        )
        gap = jnp.zeros((right_first - at - 8, LANES), jnp.float32)
        rest = jnp.zeros((LANES - (right_first - at) - 8, LANES), jnp.float32)
        halo_ref[half * strip_rows : (half + 1) * strip_rows, :] = jnp.transpose(
            jnp.concatenate([left, gap, right, rest], axis=0)
        )
    speed = small_ref[:tiles, :]
    toward_left = speed * small_ref[tiles : 2 * tiles, :]
    toward_right = speed - toward_left
    is_left = lane < STEPS
    is_right = (lane >= right_first) & (lane < right_first + STEPS)
    inside = jnp.where(is_left, has_left, jnp.where(is_right, has_right, 1.0))
    from_outside = (lane8 < STEPS) | ((lane8 >= right_first) & (lane8 < right_first + STEPS))

    def edge_row(rows, row):
        own = jnp.where(
            low, pltpu.roll(rows[:1], STEPS, 1), pltpu.roll(rows[tiles - 1 :], half_lanes + 3 * STEPS, 1)
        )
        left = pltpu.roll(strips[2][row : row + 1], STEPS, 1)
        right = pltpu.roll(strips[2][row : row + 1], right_first, 1)
        return jnp.where(is_left, left, jnp.where(is_right, right, own))

    edge_left = edge_row(toward_left, 3)
    edge_right = edge_row(toward_right, 4)
    from_left = jnp.broadcast_to((edge_left + DIFFUSION) * inside, (8, LANES))
    from_right = jnp.broadcast_to((edge_right + DIFFUSION) * inside, (8, LANES))
    stay = jnp.broadcast_to((1.0 - 2.0 * DIFFUSION - edge_left - edge_right) * inside, (8, LANES))
    mix = powers_of(powers_ref, fields)
    first_sums = [[jnp.zeros((8, LANES), jnp.float32)] * fields for _ in range(2)]
    last_sums = [[jnp.zeros((8, LANES), jnp.float32)] * fields for _ in range(2)]
    for half in range(2):
        state, edge = states[half], raw_edges[half]
        for i in range(members // 8):
            moved = []
            for f in range(fields):
                at = f * members + 8 * i
                x = edge[at : at + 8, :]
                x = jnp.where(from_outside, halo_ref[half * strip_rows + at : half * strip_rows + at + 8, :], x)
                moved.append(transport(x, from_left, stay, from_right))
            for f in range(fields):
                at = f * members + 8 * i
                value = sum(mix[f][g] * moved[g] for g in range(fields))
                first_tile = jnp.where(lane8 < STEPS, pltpu.roll(value, LANES - STEPS, 1), state[at : at + 8, :LANES])
                last_tile = jnp.where(
                    lane8 >= LANES - STEPS,
                    pltpu.roll(value, LANES - right_first, 1),
                    state[at : at + 8, cells - LANES :],
                )
                edge_ref[half * strip_rows + at : half * strip_rows + at + 8, :LANES] = first_tile
                edge_ref[half * strip_rows + at : half * strip_rows + at + 8, LANES:] = last_tile
                first_sums[half][f] = first_sums[half][f] + first_tile
                last_sums[half][f] = last_sums[half][f] + last_tile
    edge_at = fields * inner
    for f in range(fields):
        for n, (t, sums) in enumerate(((0, first_sums), (tiles - 1, last_sums))):
            column = slice(n * LANES, (n + 1) * LANES)
            halves = [
                edge_ref[half * strip_rows + f * members : half * strip_rows + (f + 1) * members, column]
                for half in range(2)
            ]
            put_tile(f * tiles + t, sums[0][f] + sums[1][f], halves, edge_at + 2 * f + n)
    products.append(product_of(edge_at, edge_at + 2 * fields))
    products = sum(products)
    mean = jnp.concatenate([means[at] for at in range(places)], axis=0)
    gram = products[: total + 8] + products[depth : depth + total + 8]
    gram = gram + pltpu.roll(gram, total, 1)
    in_low = lax.broadcasted_iota(jnp.int32, (members, LANES), 1) < total
    folded = jnp.where(in_low, gram[members:total], gram[:members])
    blank = jnp.zeros((stay_ref.shape[0] - members - 1, LANES), jnp.float32)
    for out in (stay_ref, odd_ref, even_ref):
        out[:members, :] = folded
        out[members : members + 1, :] = gram[total : total + 1]
        out[members + 1 :, :] = blank

    found = lax.dot_general(
        jnp.concatenate(pieces_of(mean), axis=0).astype(jnp.bfloat16), onehot_ref[...],
        (((1,), (0,)), ((), ())), preferred_element_type=jnp.float32,
    )
    found = found[:places] + found[places : 2 * places] + found[2 * places :]
    for out, source, partner in ((stay_ref, 0, 0), (odd_ref, 1, 1 + 2 * core), (even_ref, 3, 2)):
        for j in range(held):
            n = source * held + j
            center = jnp.sum(
                jnp.where(hits[n], found[:, n * LANES : (n + 1) * LANES], 0.0), axis=0, keepdims=True
            )
            out[pl.ds(members + 1 + partner * held + j, 1), :] = center


def spread_row(row):
    return jnp.broadcast_to(row, (8, LANES))


def eliminate(rows):
    count = len(rows)
    rows = list(rows)
    sub = lax.broadcasted_iota(jnp.int32, (8, LANES), 0)

    def columns_of(row, b):
        first = 8 * (count + b)
        return [jnp.broadcast_to(row[:, first + k : first + k + 1], (8, LANES)) for k in range(8)]

    upcoming = columns_of(rows[0], 0)
    for b in range(count):
        own = upcoming
        below = {i: columns_of(rows[i], b) for i in range(b + 1, count)}
        if b + 1 < count:
            upcoming = columns_of(rows[b + 1], b + 1)
        for j in range(8):
            scale = lax.rsqrt(spread_row(own[j][j : j + 1, :]))
            upper = spread_row(rows[b][j : j + 1, :]) * scale
            lower = own[j] * scale
            factors = {k: spread_row(lower[k : k + 1, :]) for k in range(j + 1, 8)}
            for k in range(j + 1, 8):
                own[k] = own[k] - lower * factors[k]
            rows[b] = jnp.where(sub == j, upper, rows[b] - jnp.where(sub > j, lower, 0.0) * upper)
            for i in range(b + 1, count):
                here = below[i][j] * scale
                if i == b + 1:
                    for k in range(8):
                        upcoming[k] = upcoming[k] - here * spread_row(here[k : k + 1, :])
                for k in range(j + 1, 8):
                    below[i][k] = below[i][k] - here * factors[k]
                rows[i] = rows[i] - here * upper
    return rows


def analysis_kernel(
    split_ref, edge_ref, small_ref, slots_ref, kept, odd, swapped, even,
    analysis_ref, innovation_ref, center_ref, pieces_ref, result_ref, departure_ref, sems, *, units, obs_rows, count,
):
    block, core = here()
    members, fields, cells = analysis_ref.shape
    total = 2 * members
    strip_rows = fields * members
    for f in range(fields):
        for half in range(2):
            rows = slice(half * strip_rows + f * members, half * strip_rows + (f + 1) * members)
            side = core if half == 0 else 1 - core
            for p, piece in enumerate(halves_of(edge_ref[rows, :])):
                at = pl.multiple_of((f * 2 + p) * total + side * members, 16)
                pieces_ref[pl.ds(at, members), :] = piece
    head = members + 1
    sums = (kept[:head, :] + even[:head, :]) + (odd[:head, :] + swapped[:head, :])
    returned = kept.shape[0] - head
    center_ref[:returned, :] = kept[head:, :]
    center_ref[returned : 2 * returned, :] = jnp.where(core == 0, odd[head:, :], swapped[head:, :])
    center_ref[2 * returned : 3 * returned, :] = even[head:, :]
    center_ref[3 * returned :, :] = jnp.where(core == 0, swapped[head:, :], odd[head:, :])
    lane = lax.broadcasted_iota(jnp.int32, (8, LANES), 1)
    sub = lax.broadcasted_iota(jnp.int32, (8, LANES), 0)
    shifted = pltpu.roll(sums[:members], total, 1)
    rows = []
    for b in range(total // 8):
        at = 8 * b
        source = sums[at : at + 8] if at < members else shifted[at - members : at - members + 8]
        own = jnp.where(lane == sub + at + total, total - 1.0, 0.0)
        unit = jnp.where(lane == sub + at, 1.0, 0.0)
        rows.append(jnp.where(lane >= total, source + own, unit))
    rows = eliminate(rows)
    cross = sums[members : members + 1]
    inverse = [jnp.where(lane < total, r, 0.0) for r in rows]
    carried = [jnp.sum(r * cross, axis=1, keepdims=True) for r in inverse]
    row_sums = [jnp.sum(r, axis=1, keepdims=True) for r in inverse]
    row_means = [r * (1.0 / total) for r in row_sums]
    weights = jnp.sum(sum(r * c for r, c in zip(inverse, carried)), axis=0, keepdims=True)
    column_mean = jnp.sum(sum(inverse), axis=0, keepdims=True) * (1.0 / total)
    grand = jnp.sum(sum(row_means), axis=0, keepdims=True) * (1.0 / total)
    weights = weights - jnp.sum(sum(r * c for r, c in zip(row_means, carried)), axis=0, keepdims=True)
    root = math.sqrt(total - 1.0)
    add = weights + 1.0 / total - root * (column_mean - grand)
    count_here = members // 8
    mixing = [
        root * jnp.where(core == 0, inverse[b] - row_means[b], inverse[b + count_here] - row_means[b + count_here]) + add
        for b in range(count_here)
    ]
    high, rest = halves_of(jnp.concatenate(mixing, axis=0)[:, :total])
    mixing = jnp.concatenate(
        [jnp.concatenate([high, high], axis=1), jnp.concatenate([rest, rest], axis=1)], axis=0
    )
    copies = []
    width = cells // 2
    for n in range(2):
        lanes = slice(n * width, (n + 1) * width)
        for f in range(fields):
            rows = slice(f * 2 * total, (f + 1) * 2 * total)
            if n == 0:
                states = [pieces_ref[rows, :LANES], split_ref[rows, LANES:width]]
            else:
                states = [split_ref[rows, width : cells - LANES], pieces_ref[rows, LANES:]]
            product = jnp.dot(mixing, jnp.concatenate(states, axis=1), preferred_element_type=jnp.float32)
            result_ref[:, f, lanes] = product[:members] + product[members:]
        copies.append(
            pltpu.make_async_copy(
                result_ref.at[:, :, pl.ds(n * width, width)],
                analysis_ref.at[:, :, pl.ds(n * width, width)],
                sems.at[n],
            )
        )
        copies[-1].start()

    held = count // 4
    lane_group = lane // CAP
    table = []
    for r in range(count):
        merged = jnp.zeros((1, LANES), jnp.float32)
        for group in range(GROUPS):
            owner = group * count + r
            way = [jnp.bitwise_xor(digit_of(block, unit), (owner // unit) % 4) for unit in units]
            row = way[-1] * held
            if len(units) > 2:
                row = row + sum(step * 4**n for n, step in enumerate(way[:-2]))
            size = 4 * held
            for step in reversed(way[1:-1]):
                row = row + step * size
                size = size * 4
            row = row + way[0] * returned
            line = center_ref[pl.ds(row, 1), :]
            moved = pltpu.roll(line, jnp.bitwise_and(group - way[-2], 3) * CAP, 1)
            merged = jnp.where(lane_group[:1] == group, moved, merged)
        table.append(jnp.broadcast_to(merged, (8, LANES)))
    for r in range(obs_rows):
        center = jnp.zeros((8, LANES), jnp.float32)
        lanes = jnp.broadcast_to(slots_ref[obs_rows + r : obs_rows + r + 1, :], (8, LANES))
        for n in range(count):
            found = jnp.take_along_axis(table[n], lanes, axis=1, mode="promise_in_bounds")
            center = jnp.where(slots_ref[r : r + 1, :] == n, found, center)
        center = center[:1]
        at = small_ref.shape[0] - 2 * obs_rows + r
        value, sigma = small_ref[at : at + 1, :], small_ref[at + obs_rows : at + obs_rows + 1, :]
        departure_ref[r : r + 1, :] = (value - center) / sigma
    copies.append(pltpu.make_async_copy(departure_ref, innovation_ref, sems.at[2]))
    copies[-1].start()
    for copy in copies:
        copy.wait()


def shards(
    ensemble, speed, direction, couple, obs_place, obs_field, obs_value, obs_sigma, send_count
):
    members, fields, cells = ensemble.shape
    owners = lax.axis_size("cells")
    total = members * lax.axis_size("members")
    obs = obs_place.shape[0]
    obs_rows = obs // LANES
    tiles = cells // LANES
    places = fields * tiles
    units = stage_units(owners)
    block = lax.axis_index("cells").astype(jnp.int32)
    core = lax.axis_index("members").astype(jnp.int32)
    small = (
        speed.reshape(tiles, LANES), direction.reshape(tiles, LANES),
        *(x.reshape(obs_rows, LANES) for x in (obs_place, obs_field, obs_value, obs_sigma)),
    )
    whole = pl.BlockSpec(memory_space=pltpu.VMEM)
    params = pltpu.CompilerParams(vmem_limit_bytes=VMEM_BYTES)
    real = jnp.float32

    table_rows = 8 * (owners // GROUPS)
    part = table_rows // 4
    other = swap_cores(ensemble, owners)
    rows_of = lambda count: pl.BlockSpec((count, LANES), lambda i: (0, 0))
    small_rows = 2 * tiles + 2 * obs_rows
    strips = pl.pallas_call(
        strips_kernel,
        out_shape=jax.ShapeDtypeStruct((8, LANES), real),
        in_specs=[whole],
        out_specs=whole,
        compiler_params=params,
        name="strips",
    )(ensemble)
    kept, to_odd, to_even, small = pl.pallas_call(
        functools.partial(pack_kernel, rows=obs_rows, cells=cells, fields=fields),
        out_shape=(jax.ShapeDtypeStruct((part, LANES), real),) * 3
        + (jax.ShapeDtypeStruct((small_rows, LANES), real),),
        grid=(1,),
        in_specs=[whole] + [rows_of(x.shape[0]) for x in small],
        out_specs=(whole,) * 4,
        scratch_shapes=[pltpu.VMEM((table_rows, LANES), real)],
        compiler_params=params,
        name="pack",
    )(send_count, *small)
    to_odd, to_even = pl.pallas_call(
        join_kernel,
        out_shape=(jax.ShapeDtypeStruct((16 + part, LANES), real),) * 2,
        in_specs=[whole] * 4,
        out_specs=(whole,) * 2,
        compiler_params=params,
        name="join",
    )(strips, other, to_odd, to_even)

    strip_rows = fields * members
    band = jax.ShapeDtypeStruct((2 * cells, 2 * LANES), jnp.bfloat16)

    powers = jax.ShapeDtypeStruct((fields * fields, LANES), real)
    slots = jax.ShapeDtypeStruct((2 * obs_rows, LANES), jnp.int32)

    pieces = jax.ShapeDtypeStruct((fields * 2 * total, cells), jnp.bfloat16)

    def forecast(operands, extra, own):
        return pl.pallas_call(
            functools.partial(forecast_kernel, fields=fields, own=own),
            out_shape=(
                jax.ShapeDtypeStruct((strip_rows, cells), real),
                jax.ShapeDtypeStruct((strip_rows, LANES), real),
                jax.ShapeDtypeStruct((places * 8, LANES), real),
            )
            + extra,
            in_specs=[whole] * len(operands),
            out_specs=(whole,) * (3 + len(extra)),
            scratch_shapes=[pltpu.VMEM((2 * strip_rows, cells), jnp.bfloat16), pltpu.VMEM((strip_rows, cells), real)],
            compiler_params=params,
            cost_estimate=pl.CostEstimate(
                flops=80 * strip_rows * cells, bytes_accessed=8 * strip_rows * cells, transcendentals=0
            ),
            name="forecast",
        )(*operands)

    rule, mixed = pl.pallas_call(
        functools.partial(rule_kernel, tiles=tiles),
        out_shape=(band, powers),
        in_specs=[whole] * 2,
        out_specs=(whole,) * 2,
        compiler_params=params,
        cost_estimate=pl.CostEstimate(
            flops=40 * strip_rows * cells, bytes_accessed=4 * strip_rows * cells, transcendentals=0
        ),
        name="rule",
    )(couple, small)
    own_forecast = forecast((mixed, ensemble, rule), (), True)
    carried = []
    for n, unit in enumerate(units):
        arrived = exchange(to_odd, to_even, owners, unit)
        if n + 1 < len(units):
            to_odd, to_even, kept = pl.pallas_call(
                functools.partial(regroup_kernel, unit=unit, into_lanes=n + 2 == len(units)),
                out_shape=tuple(jax.ShapeDtypeStruct(x.shape, real) for x in (to_odd, to_even, kept)),
                in_specs=[whole] * 4 + [pl.BlockSpec(memory_space=pl.ANY)],
                out_specs=(whole,) * 3,
                compiler_params=params,
                name="regroup",
            )(kept, *arrived, mixed)
            carried.append(to_odd)
    *other_forecast, slots_of, split = forecast(
        (mixed, other, rule, send_count, own_forecast[0]), (slots, pieces), False
    )

    held = kept.shape[0] // 8
    sums_rows = -(-(members + 1 + 4 * held) // 8) * 8
    all_slots = 4 * held * LANES
    sums = jax.ShapeDtypeStruct((sums_rows, LANES), real)
    stay, to_odd, to_even, edges = pl.pallas_call(
        functools.partial(sums_kernel, owners=owners, units=units, fields=fields),
        out_shape=(sums, sums, sums, jax.ShapeDtypeStruct((2 * strip_rows, 2 * LANES), real)),
        in_specs=[whole] * (12 + len(carried)),
        out_specs=(whole,) * 4,
        scratch_shapes=[
            pltpu.VMEM((2 * strip_rows, LANES), real),
            pltpu.VMEM((LANES, all_slots), jnp.bfloat16),
            pltpu.VMEM((6 * places, all_slots), jnp.bfloat16),
            pltpu.VMEM((2 * (total + 16), fields * cells), jnp.bfloat16),
        ],
        compiler_params=params,
        name="sums",
    )(
        mixed, small, *own_forecast, *other_forecast, kept, *arrived, *carried,
    )

    head = members + 1
    used = head + 4 * held
    for n, unit in enumerate(reversed(units)):
        odd, swapped, even = exchange(to_odd, to_even, owners, unit)
        if n + 1 < len(units):
            added = (stay + even) + (odd + swapped)
            if n > 0:
                first = jnp.where(core == 0, odd, swapped)
                third = jnp.where(core == 0, swapped, odd)
                added = jnp.concatenate(
                    [added[:head]] + [x[head:used] for x in (stay, first, even, third)], axis=0
                )
                used = added.shape[0]
            stay = to_odd = to_even = added

    analysis, innovation = pl.pallas_call(
        functools.partial(analysis_kernel, units=units, obs_rows=obs_rows, count=owners // GROUPS),
        out_shape=(
            jax.ShapeDtypeStruct((members, fields, cells), real),
            jax.ShapeDtypeStruct((obs_rows, LANES), real),
        ),
        in_specs=[whole] * 8,
        out_specs=(pl.BlockSpec(memory_space=pl.ANY),) * 2,
        scratch_shapes=[
            pltpu.VMEM((4 * (stay.shape[0] - head), LANES), real),
            pltpu.VMEM((fields * 2 * total, 2 * LANES), jnp.bfloat16),
            pltpu.VMEM((members, fields, cells), real),
            pltpu.VMEM((obs_rows, LANES), real),
            pltpu.SemaphoreType.DMA((3,)),
        ],
        compiler_params=params,
        name="analysis",
    )(
        split, edges, small, slots_of,
        stay, odd, swapped, even,
    )
    return (analysis, innovation.reshape(obs))


def solution(mesh):
    return jax.shard_map(
        shards,
        mesh=mesh,
        in_specs=(
            P("members", None, "cells"),
            P("cells"),
            P("cells"),
            P(),
            P("cells"),
            P("cells"),
            P("cells"),
            P("cells"),
            P("cells", None),
        ),
        out_specs=(P("members", None, "cells"), P("cells")),
        check_vma=False,
    )
```

```python
import functools
import math

import jax
import jax.numpy as jnp
from jax import lax
from jax.experimental import pallas as pl
from jax.experimental.pallas import tpu as pltpu
from jax.sharding import PartitionSpec as P

STEPS = 4
DIFFUSION = 0.05
LANES = 128
CAP = 32
GROUPS = LANES // CAP
BOTH = ("cells", "members")
EXACT = lax.Precision.HIGHEST
VMEM_BYTES = 48 * 1024 * 1024


def core_pairs(owners, place):
    pairs = []
    for block in range(owners):
        for core in range(2):
            to_block, to_core = place(block, core)
            pairs.append((block * 2 + core, to_block * 2 + to_core))
    return pairs


def stage_units(owners):
    units = []
    unit = 1
    while unit < owners:
        units.append(unit)
        unit *= 4
    if unit != owners or len(units) < 2:
        raise ValueError("blocks not 4**n")
    return units


def swap_cores(x, owners):
    return lax.ppermute(x, BOTH, core_pairs(owners, lambda block, core: (block, 1 - core)))


def exchange(to_odd, to_even, owners, unit):
    odd = lax.ppermute(
        to_odd, BOTH, core_pairs(owners, lambda block, core: (block ^ (unit * (1 + 2 * core)), core))
    )
    even = lax.ppermute(
        to_even, BOTH, core_pairs(owners, lambda block, core: (block ^ (unit * 2), core))
    )
    return odd, swap_cores(odd, owners), even


def digit_of(block, unit):
    return jnp.bitwise_and(lax.shift_right_logical(block, jnp.int32(unit.bit_length() - 1)), 3)


def here():
    return lax.axis_index("cells"), lax.axis_index("members")


def table_row(number, count):
    return (number % 4) * (count // 4) + number // 4


def strips_of(ref):
    fields, cells = ref.shape[1:]
    lane = lax.broadcasted_iota(jnp.int32, (1, LANES), 1)
    ends = [jnp.where(lane < STEPS, ref[:, f, :LANES], ref[:, f, cells - LANES :]) for f in range(fields)]
    ends = jnp.transpose(jnp.concatenate(ends, axis=0))
    return jnp.concatenate([ends[:STEPS, :], ends[LANES - STEPS :, :]], axis=0)


def pack_kernel(
    send_ref, speed_ref, flag_ref, place_ref, field_ref, value_ref, sigma_ref,
    kept_ref, odd_ref, even_ref, small_ref, table_ref, *, rows, cells, fields,
):
    block, core = here()
    tiles = cells // LANES
    speed, value, sigma = speed_ref[...], value_ref[...], sigma_ref[...]
    flag, place, field = (ref[...].astype(jnp.float32) for ref in (flag_ref, place_ref, field_ref))
    at = 0
    for part in (speed, flag, value, sigma):
        small_ref[at : at + part.shape[0], :] = part
        at += part.shape[0]
    lane = lax.broadcasted_iota(jnp.int32, (1, LANES), 1)
    low = lane < LANES // 2
    toward_left = speed * flag
    toward_right = speed - toward_left
    edge_left = jnp.where(low, toward_left[:1], toward_left[tiles - 1 :])
    edge_right = jnp.where(low, toward_right[:1], toward_right[tiles - 1 :])
    ids = field * float(cells) + place
    weight = 1.0 / (sigma * sigma)
    pull = weight * value
    sub = lax.broadcasted_iota(jnp.int32, (8, LANES), 0)
    empty = jnp.where(sub == 0, -1.0, 0.0)
    empty = jnp.where(sub == 3, edge_left, jnp.where(sub == 4, edge_right, empty))
    listed = [
        jnp.where(sub == 0, ids[r : r + 1], jnp.where(sub == 1, weight[r : r + 1], pull[r : r + 1]))
        for r in range(rows)
    ]
    owners = send_ref.shape[1]
    count = owners // GROUPS
    sends = jnp.broadcast_to(send_ref[...], (8, owners)).astype(jnp.bfloat16)
    sender = lax.broadcasted_iota(jnp.int32, (owners, LANES), 0)
    group = lax.broadcasted_iota(jnp.int32, (owners, LANES), 1) // CAP
    slot = lax.broadcasted_iota(jnp.int32, (8, LANES), 1) % CAP
    one = lambda mask: jnp.where(mask, 1.0, 0.0)
    which = jnp.concatenate(
        [one(sender < group * count + r) for r in range(count)] + [one(sender == group * count + r) for r in range(count)],
        axis=1,
    )
    found = jnp.dot(sends, which.astype(jnp.bfloat16), preferred_element_type=jnp.float32).astype(jnp.int32)
    for r in range(count):
        index = found[:, r * LANES : (r + 1) * LANES] + slot
        held = found[:, (count + r) * LANES : (count + r + 1) * LANES]
        block_of = empty
        inside = (slot < held) & (sub < 3)
        for w in range(rows):
            moved = jnp.take_along_axis(
                listed[w], jnp.bitwise_and(index, LANES - 1), axis=1, mode="promise_in_bounds"
            )
            block_of = jnp.where(inside & (lax.shift_right_logical(index, 7) == w), moved, block_of)
        row = 8 * table_row(r, count)
        table_ref[row : row + 8, :] = block_of
    part = kept_ref.shape[0]
    digit = digit_of(block, 1)
    for out, partner in ((kept_ref, 0), (odd_ref, 1 + 2 * core), (even_ref, 2)):
        out[...] = table_ref[pl.ds(pl.multiple_of(jnp.bitwise_xor(digit, partner) * part, 8), part), :]


def strips_kernel(ensemble_ref, out_ref):
    out_ref[...] = strips_of(ensemble_ref)


def join_kernel(own_ref, other_ref, odd_part, even_part, odd_ref, even_ref):
    strips = jnp.concatenate([own_ref[...], strips_of(other_ref)], axis=0)
    for part, out in ((odd_part, odd_ref), (even_part, even_ref)):
        out[:16, :] = strips
        out[16:, :] = part[...]


def incoming(digit, core, odd, swapped):
    sub = lax.broadcasted_iota(jnp.int32, (8, LANES), 0)
    low = lax.broadcasted_iota(jnp.int32, (8, LANES), 1) < LANES // 2
    direct = jnp.bitwise_xor(jnp.bitwise_and(digit, 1), core) == 0
    result = []
    for part, other_part in ((0, 1), (1, 0), (2, 2)):
        mine = odd[8 * part : 8 * part + 8, :]
        others = swapped[8 * other_part : 8 * other_part + 8, :]
        from_right = jnp.where(direct, mine, others)
        from_left = jnp.where(direct, others, mine)
        result.append(jnp.where(sub < STEPS if part < 2 else low, from_right, from_left))
    return result


def regroup_kernel(
    kept, odd, swapped, even, _, to_odd, to_even, stay, *, unit, into_lanes,
):
    block, core = here()
    after = digit_of(block, unit * 4)
    own, other, coefs = incoming(digit_of(block, unit), core, odd, swapped)
    sub = lax.broadcasted_iota(jnp.int32, (8, LANES), 0)
    lane_group = lax.broadcasted_iota(jnp.int32, (8, LANES), 1) // CAP
    held = kept.shape[0] // 8

    def received(k, at):
        if k == 0:
            return kept[pl.ds(at, 8), :]
        if k == 2:
            return even[pl.ds(16 + at, 8), :]
        mine, others = odd[pl.ds(16 + at, 8), :], swapped[pl.ds(16 + at, 8), :]
        return jnp.where(core == k // 2, mine, others)

    for target in (to_odd, to_even):
        target[0:8, :] = own
        target[8:16, :] = other
    for target, base, partner in ((to_odd, 16, 1 + 2 * core), (to_even, 16, 2), (stay, 0, 0)):
        wanted = jnp.bitwise_xor(after, partner)
        if into_lanes:
            for j in range(held):
                merged = coefs
                for k in range(4):
                    moved = pltpu.roll(received(k, 8 * j), jnp.bitwise_and(k - wanted, 3) * CAP, 1)
                    merged = jnp.where((lane_group == k) & (sub < 3), moved, merged)
                target[base + 8 * j : base + 8 * j + 8, :] = merged
        else:
            rest = held // 4
            for k in range(4):
                for r in range(rest):
                    at = pl.multiple_of((wanted * rest + r) * 8, 8)
                    row = base + 8 * (r * 4 + k)
                    target[row : row + 8, :] = jnp.where(sub < 3, received(k, at), coefs)


def fill_powers(couple_ref, powers_ref):
    fields = couple_ref.shape[0]
    mix = [
        [
            jnp.broadcast_to(couple_ref[f : f + 1, g : g + 1], (1, LANES)) + (1.0 if f == g else 0.0)
            for g in range(fields)
        ]
        for f in range(fields)
    ]
    for _ in range(2):
        mix = [
            [sum(mix[f][h] * mix[h][g] for h in range(fields)) for g in range(fields)]
            for f in range(fields)
        ]
    for f in range(fields):
        for g in range(fields):
            powers_ref[f * fields + g : f * fields + g + 1, :] = mix[f][g]


def powers_of(powers_ref, fields):
    return [[powers_ref[f * fields + g : f * fields + g + 1, :] for g in range(fields)] for f in range(fields)]


def transport(x, from_left, stay, from_right):
    for _ in range(STEPS):
        x = from_left * pltpu.roll(x, 1, 1) + stay * x + from_right * pltpu.roll(x, x.shape[1] - 1, 1)
    return x


def halves_of(x):
    high = x.astype(jnp.bfloat16)
    return high, (x - high.astype(jnp.float32)).astype(jnp.bfloat16)


def band_maker(small_ref, band_ref, cells):
    tiles = cells // LANES
    speed = small_ref[:tiles, :]
    toward_left = speed * small_ref[tiles : 2 * tiles, :]
    toward_right = speed - toward_left

    lane = lax.broadcasted_iota(jnp.int32, (tiles, LANES), 1)

    def shifted(x, by):
        if by == 0:
            return x
        turned = pltpu.roll(x, 1 if by < 0 else LANES - 1, 1)
        carried = pltpu.roll(turned, 1 if by < 0 else tiles - 1, 0)
        return jnp.where(lane == (0 if by < 0 else LANES - 1), carried, turned)

    step = {-1: toward_left + DIFFUSION, 0: 1.0 - 2.0 * DIFFUSION - speed, 1: toward_right + DIFFUSION}
    reach = dict(step)
    for _ in range(STEPS - 1):
        longer = {}
        for e in step:
            for d in reach:
                term = step[e] * shifted(reach[d], e)
                longer[d + e] = longer[d + e] + term if d + e in longer else term
        reach = longer
    row = lax.broadcasted_iota(jnp.int32, (LANES, LANES), 0)
    column = lax.broadcasted_iota(jnp.int32, (LANES, LANES), 1)
    ahead = row - column

    def make(t):
        rule = {d: reach[d][t : t + 1, :] for d in reach}

        def placed(distance, offsets):
            block = jnp.zeros(distance.shape, jnp.float32)
            for d in offsets:
                block = jnp.where(distance == d, rule[d], block)
            return block

        block = jnp.concatenate(
            [
                placed(ahead, range(-STEPS, STEPS + 1)),
                placed(ahead[:8] + LANES, range(1, STEPS + 1)),
                jnp.zeros((LANES - 16, LANES), jnp.float32),
                placed(ahead[LANES - 8 :] - LANES, range(-STEPS, 0)),
            ],
            axis=0,
        )
        for p, piece in enumerate(halves_of(block)):
            band_ref[2 * t * LANES : 2 * (t + 1) * LANES, p * LANES : (p + 1) * LANES] = piece

    return make


def fill_positions(send_ref, slots_ref):
    owners = send_ref.shape[1]
    count = owners // GROUPS
    rows = slots_ref.shape[0] // 2
    row = lax.broadcasted_iota(jnp.int32, (owners, owners), 0)
    column = lax.broadcasted_iota(jnp.int32, (owners, owners), 1)
    held = jnp.where(row == column, jnp.broadcast_to(send_ref[...], (owners, owners)), 0).astype(jnp.float32)
    held = jnp.broadcast_to(jnp.sum(held, axis=1, keepdims=True), (owners, LANES))
    ends = jnp.dot(
        jnp.where(column <= row, 1.0, 0.0).astype(jnp.bfloat16), held.astype(jnp.bfloat16),
        preferred_element_type=jnp.float32,
    )
    for r in range(rows):
        slot = (lax.broadcasted_iota(jnp.int32, (1, LANES), 1) + r * LANES).astype(jnp.float32)
        passed = ends <= slot
        owner = jnp.sum(jnp.where(passed, 1.0, 0.0), axis=0, keepdims=True).astype(jnp.int32)
        start = jnp.sum(jnp.where(passed, held, 0.0), axis=0, keepdims=True)
        group = lax.shift_right_logical(owner, count.bit_length() - 1)
        slots_ref[r : r + 1, :] = jnp.bitwise_and(owner, count - 1)
        slots_ref[rows + r : rows + r + 1, :] = group * CAP + (slot - start).astype(jnp.int32)


def fill_split(source, edge, split_ref, raw_ref):
    members, fields, cells = source.shape
    height = fields * members
    low = lax.broadcasted_iota(jnp.int32, (members, LANES), 1) < LANES // 2
    for f in range(fields):
        rows = slice(f * members, (f + 1) * members)
        raw_ref[rows, :] = source[:, f, :]
        x = raw_ref[rows, :]
        edge[rows, :] = jnp.where(
            low,
            pltpu.roll(x[:, :LANES], STEPS, 1),
            pltpu.roll(x[:, cells - LANES :], LANES // 2 + 3 * STEPS, 1),
        )
        for p, piece in enumerate(halves_of(x)):
            split_ref[p * height + f * members : p * height + (f + 1) * members, :] = piece


def rule_kernel(
    couple_ref, small_ref, send_ref, source, band_ref, powers_ref, slots_ref, split_ref, edge, raw_ref, *, tiles,
):
    fill_split(source, edge, split_ref, raw_ref)
    fill_powers(couple_ref, powers_ref)
    fill_positions(send_ref, slots_ref)
    make_band = band_maker(small_ref, band_ref, tiles * LANES)
    for t in range(tiles):
        make_band(t)


def forecast_kernel(powers_ref, source, band_ref, *refs, fields, own):
    cells = source.shape[-1]
    members = source.shape[0] // (2 * fields) if own else source.shape[0]
    tiles = cells // LANES
    height = fields * members
    if own:
        split_ref, (state, sums_ref) = source, refs
    else:
        own_state, state, edge, sums_ref, pieces_ref, split_ref, raw_ref = refs
        core = here()[1]

        def put_pieces(side, f, lanes, value):
            for p, piece in enumerate(halves_of(value)):
                at = pl.multiple_of((f * 2 + p) * 2 * members + side * members, 16)
                pieces_ref[pl.ds(at, members), lanes] = piece

        for f in range(fields):
            put_pieces(core, f, slice(0, cells), own_state[f * members : (f + 1) * members, :])
    if not own:
        fill_split(source, edge, split_ref, raw_ref)
    mix = powers_of(powers_ref, fields)
    nearer = lax.broadcasted_iota(jnp.int32, (2 * height, LANES), 1) < LANES // 2
    for t in range(tiles):
        lanes, after, before = (
            slice(n % tiles * LANES, (n % tiles + 1) * LANES) for n in (t, t + 1, t - 1)
        )
        around = jnp.where(nearer, split_ref[:, after], split_ref[:, before])
        product = jnp.dot(
            jnp.concatenate([split_ref[:, lanes], around], axis=1),
            band_ref[2 * t * LANES : 2 * (t + 1) * LANES, :],
            preferred_element_type=jnp.float32,
        )
        moved = (
            product[height:, LANES:] + (product[:height, LANES:] + product[height:, :LANES])
        ) + product[:height, :LANES]
        for f in range(fields):
            value = sum(mix[f][g] * moved[g * members : (g + 1) * members] for g in range(fields))
            state[f * members : (f + 1) * members, lanes] = value
            if not own:
                put_pieces(1 - core, f, lanes, value)
            place = (f * tiles + t) * 8
            sums_ref[place : place + 8, :] = sum(value[8 * i : 8 * i + 8] for i in range(members // 8))


def pieces_of(x):
    high = x.astype(jnp.bfloat16).astype(jnp.float32)
    rest = x - high
    middle = rest.astype(jnp.bfloat16).astype(jnp.float32)
    return high, middle, rest - middle


def sums_kernel(
    powers_ref, small_ref, own_state, own_edge, own_sums, other_state, other_edge, other_sums,
    kept, odd, swapped, even, *refs, owners, units, fields,
):
    carried = refs[: len(units) - 1]
    (
        stay_ref, odd_ref, even_ref, edge_ref, halo_ref, onehot_ref, spread_ref, split_ref,
    ) = refs[len(units) - 1 :]
    states, raw_edges = (own_state, other_state), (own_edge, other_edge)
    block, core = here()
    members = states[0].shape[0] // fields
    cells = states[0].shape[1]
    tiles = cells // LANES
    total = 2 * members
    places = fields * tiles
    has_left = (block > 0).astype(jnp.float32)
    has_right = (block < owners - 1).astype(jnp.float32)
    sub = lax.broadcasted_iota(jnp.int32, (8, LANES), 0)
    lane = lax.broadcasted_iota(jnp.int32, (1, LANES), 1)
    lane8 = lax.broadcasted_iota(jnp.int32, (8, LANES), 1)
    half_lanes = LANES // 2
    low = lane < half_lanes

    strips = incoming(digit_of(block, units[-1]), core, odd, swapped)
    for unit, earlier in reversed(list(zip(units, carried))):
        digit = digit_of(block, unit)
        rows = [earlier[8 * p : 8 * p + 8, :] for p in range(3)]
        picked = []
        for p in range(3):
            from_right = jnp.where(digit != 3, rows[p], strips[p])
            from_left = jnp.where(digit != 0, rows[p], strips[p])
            picked.append(jnp.where(sub < STEPS if p < 2 else lane8 < half_lanes, from_right, from_left))
        strips = picked

    place_ids = lax.broadcasted_iota(jnp.int32, (places, LANES), 0)
    lane_ids = lax.broadcasted_iota(jnp.int32, (LANES, LANES), 0)
    held = kept.shape[0] // 8
    sources = [(kept, 8 * j) for j in range(held)]
    for source, base in ((odd, 16), (swapped, 16), (even, 16)):
        sources += [(source, base + 8 * j) for j in range(held)]
    hits = []
    for n, (source, at) in enumerate(sources):
        local = source[at : at + 1, :].astype(jnp.int32)
        hit = place_ids == lax.shift_right_arithmetic(local, 7)
        hits.append(hit)
        onehot = (lane_ids == jnp.bitwise_and(local, LANES - 1)).astype(jnp.float32)
        lanes = slice(n * LANES, (n + 1) * LANES)
        onehot_ref[:, lanes] = onehot.astype(jnp.bfloat16)
        weight, pull = source[at + 1 : at + 2, :], source[at + 2 : at + 3, :]
        stack = [jnp.where(hit, piece, 0.0) for piece in pieces_of(weight) + pieces_of(pull)]
        spread_ref[:, lanes] = jnp.concatenate(stack, axis=0).astype(jnp.bfloat16)
    placed = lax.dot_general(
        spread_ref[...], onehot_ref[...], (((1,), (1,)), ((), ())), preferred_element_type=jnp.float32
    )
    placed = [placed[p * places : (p + 1) * places] for p in range(6)]
    weight = placed[0] + placed[1] + placed[2]
    pull = placed[3] + placed[4] + placed[5]

    root = jnp.sqrt(weight)
    scale = jnp.where(weight > 0.0, lax.rsqrt(jnp.where(weight > 0.0, weight, 1.0)), 0.0)
    sub16 = lax.broadcasted_iota(jnp.int32, (16, LANES), 0)
    depth = total + 16
    means = {}

    def put(row, lanes, value):
        for p, piece in enumerate(halves_of(value)):
            split_ref[pl.ds(row + p * depth, value.shape[0]), lanes] = piece

    def put_tile(at, sums, halves, into):
        means[at] = jnp.sum(sums, axis=0, keepdims=True) * (1.0 / total)
        lanes = slice(into * LANES, (into + 1) * LANES)
        for half, value in enumerate(halves):
            side = core if half == 0 else 1 - core
            anomaly = (value - means[at]) * root[at : at + 1]
            put(pl.multiple_of(side * members, 16), lanes, anomaly)
        drawn = (pull[at : at + 1] - weight[at : at + 1] * means[at]) * scale[at : at + 1]
        put(total, lanes, jnp.where(sub16 == 0, drawn, 0.0))

    def product_of(first, last):
        lanes = slice(first * LANES, last * LANES)
        anomalies = jnp.concatenate([split_ref[:total, lanes], split_ref[depth : depth + total, lanes]], axis=0)
        return lax.dot_general(
            split_ref[:, lanes], anomalies, (((1,), (1,)), ((), ())), preferred_element_type=jnp.float32
        )

    inner = tiles - 2
    products = []
    for f in range(fields):
        rows = slice(f * members, (f + 1) * members)
        for t in range(1, tiles - 1):
            at = f * tiles + t
            lanes = slice(t * LANES, (t + 1) * LANES)
            sums = own_sums[8 * at : 8 * at + 8, :] + other_sums[8 * at : 8 * at + 8, :]
            put_tile(at, sums, [state[rows, lanes] for state in states], f * inner + t - 1)
        products.append(product_of(f * inner, (f + 1) * inner))

    right_first = half_lanes + 3 * STEPS
    strip_rows = fields * members
    for half in range(2):
        strip = strips[half]
        left = jnp.where(sub < STEPS, pltpu.roll(strip, STEPS, 0) * has_left, 0.0)
        at = right_first % 8
        right = jnp.where(
            (sub >= at) & (sub < at + STEPS), (pltpu.roll(strip, at, 0) if at else strip) * has_right, 0.0
        )
        gap = jnp.zeros((right_first - at - 8, LANES), jnp.float32)
        rest = jnp.zeros((LANES - (right_first - at) - 8, LANES), jnp.float32)
        halo_ref[half * strip_rows : (half + 1) * strip_rows, :] = jnp.transpose(
            jnp.concatenate([left, gap, right, rest], axis=0)
        )
    speed = small_ref[:tiles, :]
    toward_left = speed * small_ref[tiles : 2 * tiles, :]
    toward_right = speed - toward_left
    is_left = lane < STEPS
    is_right = (lane >= right_first) & (lane < right_first + STEPS)
    inside = jnp.where(is_left, has_left, jnp.where(is_right, has_right, 1.0))
    from_outside = (lane8 < STEPS) | ((lane8 >= right_first) & (lane8 < right_first + STEPS))

    def edge_row(rows, row):
        own = jnp.where(
            low, pltpu.roll(rows[:1], STEPS, 1), pltpu.roll(rows[tiles - 1 :], half_lanes + 3 * STEPS, 1)
        )
        left = pltpu.roll(strips[2][row : row + 1], STEPS, 1)
        right = pltpu.roll(strips[2][row : row + 1], right_first, 1)
        return jnp.where(is_left, left, jnp.where(is_right, right, own))

    edge_left = edge_row(toward_left, 3)
    edge_right = edge_row(toward_right, 4)
    from_left = jnp.broadcast_to((edge_left + DIFFUSION) * inside, (8, LANES))
    from_right = jnp.broadcast_to((edge_right + DIFFUSION) * inside, (8, LANES))
    stay = jnp.broadcast_to((1.0 - 2.0 * DIFFUSION - edge_left - edge_right) * inside, (8, LANES))
    mix = powers_of(powers_ref, fields)
    first_sums = [[jnp.zeros((8, LANES), jnp.float32)] * fields for _ in range(2)]
    last_sums = [[jnp.zeros((8, LANES), jnp.float32)] * fields for _ in range(2)]
    for half in range(2):
        state, edge = states[half], raw_edges[half]
        for i in range(members // 8):
            moved = []
            for f in range(fields):
                at = f * members + 8 * i
                x = edge[at : at + 8, :]
                x = jnp.where(from_outside, halo_ref[half * strip_rows + at : half * strip_rows + at + 8, :], x)
                moved.append(transport(x, from_left, stay, from_right))
            for f in range(fields):
                at = f * members + 8 * i
                value = sum(mix[f][g] * moved[g] for g in range(fields))
                first_tile = jnp.where(lane8 < STEPS, pltpu.roll(value, LANES - STEPS, 1), state[at : at + 8, :LANES])
                last_tile = jnp.where(
                    lane8 >= LANES - STEPS,
                    pltpu.roll(value, LANES - right_first, 1),
                    state[at : at + 8, cells - LANES :],
                )
                edge_ref[half * strip_rows + at : half * strip_rows + at + 8, :LANES] = first_tile
                edge_ref[half * strip_rows + at : half * strip_rows + at + 8, LANES:] = last_tile
                first_sums[half][f] = first_sums[half][f] + first_tile
                last_sums[half][f] = last_sums[half][f] + last_tile
    edge_at = fields * inner
    for f in range(fields):
        for n, (t, sums) in enumerate(((0, first_sums), (tiles - 1, last_sums))):
            column = slice(n * LANES, (n + 1) * LANES)
            halves = [
                edge_ref[half * strip_rows + f * members : half * strip_rows + (f + 1) * members, column]
                for half in range(2)
            ]
            put_tile(f * tiles + t, sums[0][f] + sums[1][f], halves, edge_at + 2 * f + n)
    products.append(product_of(edge_at, edge_at + 2 * fields))
    products = sum(products)
    mean = jnp.concatenate([means[at] for at in range(places)], axis=0)
    gram = products[: total + 8] + products[depth : depth + total + 8]
    gram = gram + pltpu.roll(gram, total, 1)
    in_low = lax.broadcasted_iota(jnp.int32, (members, LANES), 1) < total
    folded = jnp.where(in_low, gram[members:total], gram[:members])
    blank = jnp.zeros((stay_ref.shape[0] - members - 1, LANES), jnp.float32)
    for out in (stay_ref, odd_ref, even_ref):
        out[:members, :] = folded
        out[members : members + 1, :] = gram[total : total + 1]
        out[members + 1 :, :] = blank

    found = lax.dot_general(
        jnp.concatenate(pieces_of(mean), axis=0).astype(jnp.bfloat16), onehot_ref[...],
        (((1,), (0,)), ((), ())), preferred_element_type=jnp.float32,
    )
    found = found[:places] + found[places : 2 * places] + found[2 * places :]
    for out, source, partner in ((stay_ref, 0, 0), (odd_ref, 1, 1 + 2 * core), (even_ref, 3, 2)):
        for j in range(held):
            n = source * held + j
            center = jnp.sum(
                jnp.where(hits[n], found[:, n * LANES : (n + 1) * LANES], 0.0), axis=0, keepdims=True
            )
            out[pl.ds(members + 1 + partner * held + j, 1), :] = center


def spread_row(row):
    return jnp.broadcast_to(row, (8, LANES))


def eliminate(rows):
    count = len(rows)
    rows = list(rows)
    sub = lax.broadcasted_iota(jnp.int32, (8, LANES), 0)

    def columns_of(row, b):
        first = 8 * (count + b)
        return [jnp.broadcast_to(row[:, first + k : first + k + 1], (8, LANES)) for k in range(8)]

    upcoming = columns_of(rows[0], 0)
    for b in range(count):
        own = upcoming
        below = {i: columns_of(rows[i], b) for i in range(b + 1, count)}
        if b + 1 < count:
            upcoming = columns_of(rows[b + 1], b + 1)
        for j in range(8):
            scale = lax.rsqrt(spread_row(own[j][j : j + 1, :]))
            upper = spread_row(rows[b][j : j + 1, :]) * scale
            lower = own[j] * scale
            factors = {k: spread_row(lower[k : k + 1, :]) for k in range(j + 1, 8)}
            for k in range(j + 1, 8):
                own[k] = own[k] - lower * factors[k]
            rows[b] = jnp.where(sub == j, upper, rows[b] - jnp.where(sub > j, lower, 0.0) * upper)
            for i in range(b + 1, count):
                here = below[i][j] * scale
                if i == b + 1:
                    for k in range(8):
                        upcoming[k] = upcoming[k] - here * spread_row(here[k : k + 1, :])
                for k in range(j + 1, 8):
                    below[i][k] = below[i][k] - here * factors[k]
                rows[i] = rows[i] - here * upper
    return rows


def analysis_kernel(
    split_ref, edge_ref, small_ref, slots_ref, kept, odd, swapped, even,
    analysis_ref, innovation_ref, center_ref, pieces_ref, result_ref, departure_ref, sems, *, units, obs_rows, count,
):
    block, core = here()
    members, fields, cells = analysis_ref.shape
    total = 2 * members
    strip_rows = fields * members
    for f in range(fields):
        for half in range(2):
            rows = slice(half * strip_rows + f * members, half * strip_rows + (f + 1) * members)
            side = core if half == 0 else 1 - core
            for p, piece in enumerate(halves_of(edge_ref[rows, :])):
                at = pl.multiple_of((f * 2 + p) * total + side * members, 16)
                pieces_ref[pl.ds(at, members), :] = piece
    head = members + 1
    sums = (kept[:head, :] + even[:head, :]) + (odd[:head, :] + swapped[:head, :])
    returned = kept.shape[0] - head
    center_ref[:returned, :] = kept[head:, :]
    center_ref[returned : 2 * returned, :] = jnp.where(core == 0, odd[head:, :], swapped[head:, :])
    center_ref[2 * returned : 3 * returned, :] = even[head:, :]
    center_ref[3 * returned :, :] = jnp.where(core == 0, swapped[head:, :], odd[head:, :])
    lane = lax.broadcasted_iota(jnp.int32, (8, LANES), 1)
    sub = lax.broadcasted_iota(jnp.int32, (8, LANES), 0)
    shifted = pltpu.roll(sums[:members], total, 1)
    rows = []
    for b in range(total // 8):
        at = 8 * b
        source = sums[at : at + 8] if at < members else shifted[at - members : at - members + 8]
        own = jnp.where(lane == sub + at + total, total - 1.0, 0.0)
        unit = jnp.where(lane == sub + at, 1.0, 0.0)
        rows.append(jnp.where(lane >= total, source + own, unit))
    rows = eliminate(rows)
    cross = sums[members : members + 1]
    inverse = [jnp.where(lane < total, r, 0.0) for r in rows]
    carried = [jnp.sum(r * cross, axis=1, keepdims=True) for r in inverse]
    row_sums = [jnp.sum(r, axis=1, keepdims=True) for r in inverse]
    row_means = [r * (1.0 / total) for r in row_sums]
    weights = jnp.sum(sum(r * c for r, c in zip(inverse, carried)), axis=0, keepdims=True)
    column_mean = jnp.sum(sum(inverse), axis=0, keepdims=True) * (1.0 / total)
    grand = jnp.sum(sum(row_means), axis=0, keepdims=True) * (1.0 / total)
    weights = weights - jnp.sum(sum(r * c for r, c in zip(row_means, carried)), axis=0, keepdims=True)
    root = math.sqrt(total - 1.0)
    add = weights + 1.0 / total - root * (column_mean - grand)
    count_here = members // 8
    mixing = [
        root * jnp.where(core == 0, inverse[b] - row_means[b], inverse[b + count_here] - row_means[b + count_here]) + add
        for b in range(count_here)
    ]
    high, rest = halves_of(jnp.concatenate(mixing, axis=0)[:, :total])
    mixing = jnp.concatenate(
        [jnp.concatenate([high, high], axis=1), jnp.concatenate([rest, rest], axis=1)], axis=0
    )
    copies = []
    width = cells // 2
    for n in range(2):
        lanes = slice(n * width, (n + 1) * width)
        for f in range(fields):
            rows = slice(f * 2 * total, (f + 1) * 2 * total)
            if n == 0:
                states = [pieces_ref[rows, :LANES], split_ref[rows, LANES:width]]
            else:
                states = [split_ref[rows, width : cells - LANES], pieces_ref[rows, LANES:]]
            product = jnp.dot(mixing, jnp.concatenate(states, axis=1), preferred_element_type=jnp.float32)
            result_ref[:, f, lanes] = product[:members] + product[members:]
        copies.append(
            pltpu.make_async_copy(
                result_ref.at[:, :, pl.ds(n * width, width)],
                analysis_ref.at[:, :, pl.ds(n * width, width)],
                sems.at[n],
            )
        )
        copies[-1].start()

    held = count // 4
    lane_group = lane // CAP
    table = []
    for r in range(count):
        merged = jnp.zeros((1, LANES), jnp.float32)
        for group in range(GROUPS):
            owner = group * count + r
            way = [jnp.bitwise_xor(digit_of(block, unit), (owner // unit) % 4) for unit in units]
            row = way[-1] * held
            if len(units) > 2:
                row = row + sum(step * 4**n for n, step in enumerate(way[:-2]))
            size = 4 * held
            for step in reversed(way[1:-1]):
                row = row + step * size
                size = size * 4
            row = row + way[0] * returned
            line = center_ref[pl.ds(row, 1), :]
            moved = pltpu.roll(line, jnp.bitwise_and(group - way[-2], 3) * CAP, 1)
            merged = jnp.where(lane_group[:1] == group, moved, merged)
        table.append(jnp.broadcast_to(merged, (8, LANES)))
    for r in range(obs_rows):
        center = jnp.zeros((8, LANES), jnp.float32)
        lanes = jnp.broadcast_to(slots_ref[obs_rows + r : obs_rows + r + 1, :], (8, LANES))
        for n in range(count):
            found = jnp.take_along_axis(table[n], lanes, axis=1, mode="promise_in_bounds")
            center = jnp.where(slots_ref[r : r + 1, :] == n, found, center)
        center = center[:1]
        at = small_ref.shape[0] - 2 * obs_rows + r
        value, sigma = small_ref[at : at + 1, :], small_ref[at + obs_rows : at + obs_rows + 1, :]
        departure_ref[r : r + 1, :] = (value - center) / sigma
    copies.append(pltpu.make_async_copy(departure_ref, innovation_ref, sems.at[2]))
    copies[-1].start()
    for copy in copies:
        copy.wait()


def shards(
    ensemble, speed, direction, couple, obs_place, obs_field, obs_value, obs_sigma, send_count
):
    members, fields, cells = ensemble.shape
    owners = lax.axis_size("cells")
    total = members * lax.axis_size("members")
    obs = obs_place.shape[0]
    obs_rows = obs // LANES
    tiles = cells // LANES
    places = fields * tiles
    units = stage_units(owners)
    block = lax.axis_index("cells").astype(jnp.int32)
    core = lax.axis_index("members").astype(jnp.int32)
    small = (
        speed.reshape(tiles, LANES), direction.reshape(tiles, LANES),
        *(x.reshape(obs_rows, LANES) for x in (obs_place, obs_field, obs_value, obs_sigma)),
    )
    whole = pl.BlockSpec(memory_space=pltpu.VMEM)
    params = pltpu.CompilerParams(vmem_limit_bytes=VMEM_BYTES)
    real = jnp.float32

    table_rows = 8 * (owners // GROUPS)
    part = table_rows // 4
    other = swap_cores(ensemble, owners)
    rows_of = lambda count: pl.BlockSpec((count, LANES), lambda i: (0, 0))
    small_rows = 2 * tiles + 2 * obs_rows
    strips = pl.pallas_call(
        strips_kernel,
        out_shape=jax.ShapeDtypeStruct((8, LANES), real),
        in_specs=[whole],
        out_specs=whole,
        compiler_params=params,
        name="strips",
    )(ensemble)
    kept, to_odd, to_even, small = pl.pallas_call(
        functools.partial(pack_kernel, rows=obs_rows, cells=cells, fields=fields),
        out_shape=(jax.ShapeDtypeStruct((part, LANES), real),) * 3
        + (jax.ShapeDtypeStruct((small_rows, LANES), real),),
        grid=(1,),
        in_specs=[whole] + [rows_of(x.shape[0]) for x in small],
        out_specs=(whole,) * 4,
        scratch_shapes=[pltpu.VMEM((table_rows, LANES), real)],
        compiler_params=params,
        name="pack",
    )(send_count, *small)
    to_odd, to_even = pl.pallas_call(
        join_kernel,
        out_shape=(jax.ShapeDtypeStruct((16 + part, LANES), real),) * 2,
        in_specs=[whole] * 4,
        out_specs=(whole,) * 2,
        compiler_params=params,
        name="join",
    )(strips, other, to_odd, to_even)

    strip_rows = fields * members
    band = jax.ShapeDtypeStruct((2 * cells, 2 * LANES), jnp.bfloat16)

    powers = jax.ShapeDtypeStruct((fields * fields, LANES), real)
    slots = jax.ShapeDtypeStruct((2 * obs_rows, LANES), jnp.int32)

    pieces = jax.ShapeDtypeStruct((fields * 2 * total, cells), jnp.bfloat16)

    def forecast(operands, extra, own):
        states = jax.ShapeDtypeStruct((strip_rows, cells), real)
        edges = () if own else (jax.ShapeDtypeStruct((strip_rows, LANES), real),)
        outs = (states,) + edges + (jax.ShapeDtypeStruct((places * 8, LANES), real),) + extra
        return pl.pallas_call(
            functools.partial(forecast_kernel, fields=fields, own=own),
            out_shape=outs,
            in_specs=[whole] * len(operands),
            out_specs=(whole,) * len(outs),
            scratch_shapes=[]
            if own
            else [pltpu.VMEM((2 * strip_rows, cells), jnp.bfloat16), pltpu.VMEM((strip_rows, cells), real)],
            compiler_params=params,
            cost_estimate=pl.CostEstimate(
                flops=80 * strip_rows * cells, bytes_accessed=8 * strip_rows * cells, transcendentals=0
            ),
            name="forecast",
        )(*operands)

    split_shape = jax.ShapeDtypeStruct((2 * strip_rows, cells), jnp.bfloat16)
    edge_shape = jax.ShapeDtypeStruct((strip_rows, LANES), real)
    rule, mixed, slots_of, own_split, own_edge = pl.pallas_call(
        functools.partial(rule_kernel, tiles=tiles),
        out_shape=(band, powers, slots, split_shape, edge_shape),
        in_specs=[whole] * 4,
        out_specs=(whole,) * 5,
        scratch_shapes=[pltpu.VMEM((strip_rows, cells), real)],
        compiler_params=params,
        cost_estimate=pl.CostEstimate(
            flops=40 * strip_rows * cells, bytes_accessed=4 * strip_rows * cells, transcendentals=0
        ),
        name="rule",
    )(couple, small, send_count, ensemble)
    own_state, own_sums = forecast((mixed, own_split, rule), (), True)
    own_forecast = (own_state, own_edge, own_sums)
    carried = []
    for n, unit in enumerate(units):
        arrived = exchange(to_odd, to_even, owners, unit)
        if n + 1 < len(units):
            to_odd, to_even, kept = pl.pallas_call(
                functools.partial(regroup_kernel, unit=unit, into_lanes=n + 2 == len(units)),
                out_shape=tuple(jax.ShapeDtypeStruct(x.shape, real) for x in (to_odd, to_even, kept)),
                in_specs=[whole] * 4 + [pl.BlockSpec(memory_space=pl.ANY)],
                out_specs=(whole,) * 3,
                compiler_params=params,
                name="regroup",
            )(kept, *arrived, mixed)
            carried.append(to_odd)
    *other_forecast, split = forecast((mixed, other, rule, own_forecast[0]), (pieces,), False)

    held = kept.shape[0] // 8
    sums_rows = -(-(members + 1 + 4 * held) // 8) * 8
    all_slots = 4 * held * LANES
    sums = jax.ShapeDtypeStruct((sums_rows, LANES), real)
    stay, to_odd, to_even, edges = pl.pallas_call(
        functools.partial(sums_kernel, owners=owners, units=units, fields=fields),
        out_shape=(sums, sums, sums, jax.ShapeDtypeStruct((2 * strip_rows, 2 * LANES), real)),
        in_specs=[whole] * (12 + len(carried)),
        out_specs=(whole,) * 4,
        scratch_shapes=[
            pltpu.VMEM((2 * strip_rows, LANES), real),
            pltpu.VMEM((LANES, all_slots), jnp.bfloat16),
            pltpu.VMEM((6 * places, all_slots), jnp.bfloat16),
            pltpu.VMEM((2 * (total + 16), fields * cells), jnp.bfloat16),
        ],
        compiler_params=params,
        name="sums",
    )(
        mixed, small, *own_forecast, *other_forecast, kept, *arrived, *carried,
    )

    head = members + 1
    used = head + 4 * held
    for n, unit in enumerate(reversed(units)):
        odd, swapped, even = exchange(to_odd, to_even, owners, unit)
        if n + 1 < len(units):
            added = (stay + even) + (odd + swapped)
            if n > 0:
                first = jnp.where(core == 0, odd, swapped)
                third = jnp.where(core == 0, swapped, odd)
                added = jnp.concatenate(
                    [added[:head]] + [x[head:used] for x in (stay, first, even, third)], axis=0
                )
                used = added.shape[0]
            stay = to_odd = to_even = added

    analysis, innovation = pl.pallas_call(
        functools.partial(analysis_kernel, units=units, obs_rows=obs_rows, count=owners // GROUPS),
        out_shape=(
            jax.ShapeDtypeStruct((members, fields, cells), real),
            jax.ShapeDtypeStruct((obs_rows, LANES), real),
        ),
        in_specs=[whole] * 8,
        out_specs=(pl.BlockSpec(memory_space=pl.ANY),) * 2,
        scratch_shapes=[
            pltpu.VMEM((4 * (stay.shape[0] - head), LANES), real),
            pltpu.VMEM((fields * 2 * total, 2 * LANES), jnp.bfloat16),
            pltpu.VMEM((members, fields, cells), real),
            pltpu.VMEM((obs_rows, LANES), real),
            pltpu.SemaphoreType.DMA((3,)),
        ],
        compiler_params=params,
        name="analysis",
    )(
        split, edges, small, slots_of,
        stay, odd, swapped, even,
    )
    return (analysis, innovation.reshape(obs))


def solution(mesh):
    return jax.shard_map(
        shards,
        mesh=mesh,
        in_specs=(
            P("members", None, "cells"),
            P("cells"),
            P("cells"),
            P(),
            P("cells"),
            P("cells"),
            P("cells"),
            P("cells"),
            P("cells", None),
        ),
        out_specs=(P("members", None, "cells"), P("cells")),
        check_vma=False,
    )
```

```python
import functools
import math

import jax
import jax.numpy as jnp
from jax import lax
from jax.experimental import pallas as pl
from jax.experimental.pallas import tpu as pltpu
from jax.sharding import PartitionSpec as P

STEPS = 4
DIFFUSION = 0.05
LANES = 128
CAP = 32
GROUPS = LANES // CAP
BOTH = ("cells", "members")
EXACT = lax.Precision.HIGHEST
VMEM_BYTES = 48 * 1024 * 1024


def core_pairs(owners, place):
    pairs = []
    for block in range(owners):
        for core in range(2):
            to_block, to_core = place(block, core)
            pairs.append((block * 2 + core, to_block * 2 + to_core))
    return pairs


def stage_units(owners):
    units = []
    unit = 1
    while unit < owners:
        units.append(unit)
        unit *= 4
    if unit != owners or len(units) < 2:
        raise ValueError("blocks not 4**n")
    return units


def swap_cores(x, owners):
    return lax.ppermute(x, BOTH, core_pairs(owners, lambda block, core: (block, 1 - core)))


def exchange(to_odd, to_even, owners, unit):
    odd = lax.ppermute(
        to_odd, BOTH, core_pairs(owners, lambda block, core: (block ^ (unit * (1 + 2 * core)), core))
    )
    even = lax.ppermute(
        to_even, BOTH, core_pairs(owners, lambda block, core: (block ^ (unit * 2), core))
    )
    return odd, swap_cores(odd, owners), even


def digit_of(block, unit):
    return jnp.bitwise_and(lax.shift_right_logical(block, jnp.int32(unit.bit_length() - 1)), 3)


def here():
    return lax.axis_index("cells"), lax.axis_index("members")


def table_row(number, count):
    return (number % 4) * (count // 4) + number // 4


def strips_of(ref):
    fields, cells = ref.shape[1:]
    lane = lax.broadcasted_iota(jnp.int32, (1, LANES), 1)
    ends = [jnp.where(lane < STEPS, ref[:, f, :LANES], ref[:, f, cells - LANES :]) for f in range(fields)]
    ends = jnp.transpose(jnp.concatenate(ends, axis=0))
    return jnp.concatenate([ends[:STEPS, :], ends[LANES - STEPS :, :]], axis=0)


def pack_kernel(
    send_ref, speed_ref, flag_ref, place_ref, field_ref, value_ref, sigma_ref,
    kept_ref, odd_ref, even_ref, small_ref, table_ref, *, rows, cells, fields,
):
    block, core = here()
    tiles = cells // LANES
    speed, value, sigma = speed_ref[...], value_ref[...], sigma_ref[...]
    flag, place, field = (ref[...].astype(jnp.float32) for ref in (flag_ref, place_ref, field_ref))
    at = 0
    for part in (speed, flag, value, sigma):
        small_ref[at : at + part.shape[0], :] = part
        at += part.shape[0]
    lane = lax.broadcasted_iota(jnp.int32, (1, LANES), 1)
    low = lane < LANES // 2
    toward_left = speed * flag
    toward_right = speed - toward_left
    edge_left = jnp.where(low, toward_left[:1], toward_left[tiles - 1 :])
    edge_right = jnp.where(low, toward_right[:1], toward_right[tiles - 1 :])
    ids = field * float(cells) + place
    weight = 1.0 / (sigma * sigma)
    pull = weight * value
    sub = lax.broadcasted_iota(jnp.int32, (8, LANES), 0)
    empty = jnp.where(sub == 0, -1.0, 0.0)
    empty = jnp.where(sub == 3, edge_left, jnp.where(sub == 4, edge_right, empty))
    listed = [
        jnp.where(sub == 0, ids[r : r + 1], jnp.where(sub == 1, weight[r : r + 1], pull[r : r + 1]))
        for r in range(rows)
    ]
    owners = send_ref.shape[1]
    count = owners // GROUPS
    sends = jnp.broadcast_to(send_ref[...], (8, owners)).astype(jnp.bfloat16)
    sender = lax.broadcasted_iota(jnp.int32, (owners, LANES), 0)
    group = lax.broadcasted_iota(jnp.int32, (owners, LANES), 1) // CAP
    slot = lax.broadcasted_iota(jnp.int32, (8, LANES), 1) % CAP
    one = lambda mask: jnp.where(mask, 1.0, 0.0)
    which = jnp.concatenate(
        [one(sender < group * count + r) for r in range(count)] + [one(sender == group * count + r) for r in range(count)],
        axis=1,
    )
    found = jnp.dot(sends, which.astype(jnp.bfloat16), preferred_element_type=jnp.float32).astype(jnp.int32)
    for r in range(count):
        index = found[:, r * LANES : (r + 1) * LANES] + slot
        held = found[:, (count + r) * LANES : (count + r + 1) * LANES]
        block_of = empty
        inside = (slot < held) & (sub < 3)
        for w in range(rows):
            moved = jnp.take_along_axis(
                listed[w], jnp.bitwise_and(index, LANES - 1), axis=1, mode="promise_in_bounds"
            )
            block_of = jnp.where(inside & (lax.shift_right_logical(index, 7) == w), moved, block_of)
        row = 8 * table_row(r, count)
        table_ref[row : row + 8, :] = block_of
    part = kept_ref.shape[0]
    digit = digit_of(block, 1)
    for out, partner in ((kept_ref, 0), (odd_ref, 1 + 2 * core), (even_ref, 2)):
        out[...] = table_ref[pl.ds(pl.multiple_of(jnp.bitwise_xor(digit, partner) * part, 8), part), :]


def strips_kernel(ensemble_ref, out_ref):
    out_ref[...] = strips_of(ensemble_ref)


def join_kernel(own_ref, other_ref, odd_part, even_part, odd_ref, even_ref):
    strips = jnp.concatenate([own_ref[...], strips_of(other_ref)], axis=0)
    for part, out in ((odd_part, odd_ref), (even_part, even_ref)):
        out[:16, :] = strips
        out[16:, :] = part[...]


def incoming(digit, core, odd, swapped):
    sub = lax.broadcasted_iota(jnp.int32, (8, LANES), 0)
    low = lax.broadcasted_iota(jnp.int32, (8, LANES), 1) < LANES // 2
    direct = jnp.bitwise_xor(jnp.bitwise_and(digit, 1), core) == 0
    result = []
    for part, other_part in ((0, 1), (1, 0), (2, 2)):
        mine = odd[8 * part : 8 * part + 8, :]
        others = swapped[8 * other_part : 8 * other_part + 8, :]
        from_right = jnp.where(direct, mine, others)
        from_left = jnp.where(direct, others, mine)
        result.append(jnp.where(sub < STEPS if part < 2 else low, from_right, from_left))
    return result


def regroup_kernel(
    kept, odd, swapped, even, _, to_odd, to_even, stay, *, unit, into_lanes,
):
    block, core = here()
    after = digit_of(block, unit * 4)
    own, other, coefs = incoming(digit_of(block, unit), core, odd, swapped)
    sub = lax.broadcasted_iota(jnp.int32, (8, LANES), 0)
    lane_group = lax.broadcasted_iota(jnp.int32, (8, LANES), 1) // CAP
    held = kept.shape[0] // 8

    def received(k, at):
        if k == 0:
            return kept[pl.ds(at, 8), :]
        if k == 2:
            return even[pl.ds(16 + at, 8), :]
        mine, others = odd[pl.ds(16 + at, 8), :], swapped[pl.ds(16 + at, 8), :]
        return jnp.where(core == k // 2, mine, others)

    for target in (to_odd, to_even):
        target[0:8, :] = own
        target[8:16, :] = other
    for target, base, partner in ((to_odd, 16, 1 + 2 * core), (to_even, 16, 2), (stay, 0, 0)):
        wanted = jnp.bitwise_xor(after, partner)
        if into_lanes:
            for j in range(held):
                merged = coefs
                for k in range(4):
                    moved = pltpu.roll(received(k, 8 * j), jnp.bitwise_and(k - wanted, 3) * CAP, 1)
                    merged = jnp.where((lane_group == k) & (sub < 3), moved, merged)
                target[base + 8 * j : base + 8 * j + 8, :] = merged
        else:
            rest = held // 4
            for k in range(4):
                for r in range(rest):
                    at = pl.multiple_of((wanted * rest + r) * 8, 8)
                    row = base + 8 * (r * 4 + k)
                    target[row : row + 8, :] = jnp.where(sub < 3, received(k, at), coefs)


def fill_powers(couple_ref, powers_ref):
    fields = couple_ref.shape[0]
    mix = [
        [
            jnp.broadcast_to(couple_ref[f : f + 1, g : g + 1], (1, LANES)) + (1.0 if f == g else 0.0)
            for g in range(fields)
        ]
        for f in range(fields)
    ]
    for _ in range(2):
        mix = [
            [sum(mix[f][h] * mix[h][g] for h in range(fields)) for g in range(fields)]
            for f in range(fields)
        ]
    for f in range(fields):
        for g in range(fields):
            powers_ref[f * fields + g : f * fields + g + 1, :] = mix[f][g]


def powers_of(powers_ref, fields):
    return [[powers_ref[f * fields + g : f * fields + g + 1, :] for g in range(fields)] for f in range(fields)]


def transport(x, from_left, stay, from_right):
    for _ in range(STEPS):
        x = from_left * pltpu.roll(x, 1, 1) + stay * x + from_right * pltpu.roll(x, x.shape[1] - 1, 1)
    return x


def halves_of(x):
    high = x.astype(jnp.bfloat16)
    return high, (x - high.astype(jnp.float32)).astype(jnp.bfloat16)


def band_maker(small_ref, band_ref, cells):
    tiles = cells // LANES
    speed = small_ref[:tiles, :]
    toward_left = speed * small_ref[tiles : 2 * tiles, :]
    toward_right = speed - toward_left

    lane = lax.broadcasted_iota(jnp.int32, (tiles, LANES), 1)

    def shifted(x, by):
        if by == 0:
            return x
        turned = pltpu.roll(x, 1 if by < 0 else LANES - 1, 1)
        carried = pltpu.roll(turned, 1 if by < 0 else tiles - 1, 0)
        return jnp.where(lane == (0 if by < 0 else LANES - 1), carried, turned)

    step = {-1: toward_left + DIFFUSION, 0: 1.0 - 2.0 * DIFFUSION - speed, 1: toward_right + DIFFUSION}
    reach = dict(step)
    for _ in range(STEPS - 1):
        longer = {}
        for e in step:
            for d in reach:
                term = step[e] * shifted(reach[d], e)
                longer[d + e] = longer[d + e] + term if d + e in longer else term
        reach = longer
    row = lax.broadcasted_iota(jnp.int32, (LANES, LANES), 0)
    column = lax.broadcasted_iota(jnp.int32, (LANES, LANES), 1)
    ahead = row - column

    def make(t):
        rule = {d: reach[d][t : t + 1, :] for d in reach}

        def placed(distance, offsets):
            block = jnp.zeros(distance.shape, jnp.float32)
            for d in offsets:
                block = jnp.where(distance == d, rule[d], block)
            return block

        block = jnp.concatenate(
            [
                placed(ahead, range(-STEPS, STEPS + 1)),
                placed(ahead[:8] + LANES, range(1, STEPS + 1)),
                jnp.zeros((LANES - 16, LANES), jnp.float32),
                placed(ahead[LANES - 8 :] - LANES, range(-STEPS, 0)),
            ],
            axis=0,
        )
        for p, piece in enumerate(halves_of(block)):
            band_ref[2 * t * LANES : 2 * (t + 1) * LANES, p * LANES : (p + 1) * LANES] = piece

    return make


def fill_positions(send_ref, slots_ref):
    owners = send_ref.shape[1]
    count = owners // GROUPS
    rows = slots_ref.shape[0] // 2
    row = lax.broadcasted_iota(jnp.int32, (owners, owners), 0)
    column = lax.broadcasted_iota(jnp.int32, (owners, owners), 1)
    held = jnp.where(row == column, jnp.broadcast_to(send_ref[...], (owners, owners)), 0).astype(jnp.float32)
    held = jnp.broadcast_to(jnp.sum(held, axis=1, keepdims=True), (owners, LANES))
    ends = jnp.dot(
        jnp.where(column <= row, 1.0, 0.0).astype(jnp.bfloat16), held.astype(jnp.bfloat16),
        preferred_element_type=jnp.float32,
    )
    for r in range(rows):
        slot = (lax.broadcasted_iota(jnp.int32, (1, LANES), 1) + r * LANES).astype(jnp.float32)
        passed = ends <= slot
        owner = jnp.sum(jnp.where(passed, 1.0, 0.0), axis=0, keepdims=True).astype(jnp.int32)
        start = jnp.sum(jnp.where(passed, held, 0.0), axis=0, keepdims=True)
        group = lax.shift_right_logical(owner, count.bit_length() - 1)
        slots_ref[r : r + 1, :] = jnp.bitwise_and(owner, count - 1)
        slots_ref[rows + r : rows + r + 1, :] = group * CAP + (slot - start).astype(jnp.int32)


def fill_split(source, edge, split_ref, raw_ref):
    members, fields, cells = source.shape
    height = fields * members
    low = lax.broadcasted_iota(jnp.int32, (members, LANES), 1) < LANES // 2
    for f in range(fields):
        rows = slice(f * members, (f + 1) * members)
        raw_ref[rows, :] = source[:, f, :]
        x = raw_ref[rows, :]
        edge[rows, :] = jnp.where(
            low,
            pltpu.roll(x[:, :LANES], STEPS, 1),
            pltpu.roll(x[:, cells - LANES :], LANES // 2 + 3 * STEPS, 1),
        )
        for p, piece in enumerate(halves_of(x)):
            split_ref[p * height + f * members : p * height + (f + 1) * members, :] = piece


def rule_kernel(
    couple_ref, small_ref, send_ref, source, band_ref, powers_ref, slots_ref, split_ref, edge, raw_ref, *, tiles,
):
    fill_split(source, edge, split_ref, raw_ref)
    fill_powers(couple_ref, powers_ref)
    fill_positions(send_ref, slots_ref)
    make_band = band_maker(small_ref, band_ref, tiles * LANES)
    for t in range(tiles):
        make_band(t)


def forecast_kernel(powers_ref, source, band_ref, *refs, fields, own):
    cells = source.shape[-1]
    members = source.shape[0] // (2 * fields) if own else source.shape[0]
    tiles = cells // LANES
    height = fields * members
    if own:
        split_ref, (state, sums_ref) = source, refs
    else:
        own_state, state, edge, sums_ref, pieces_ref, split_ref, raw_ref = refs
        core = here()[1]

        def put_pieces(side, f, lanes, value):
            for p, piece in enumerate(halves_of(value)):
                at = pl.multiple_of((f * 2 + p) * 2 * members + side * members, 16)
                pieces_ref[pl.ds(at, members), lanes] = piece

        for f in range(fields):
            put_pieces(core, f, slice(0, cells), own_state[f * members : (f + 1) * members, :])
    if not own:
        fill_split(source, edge, split_ref, raw_ref)
    mix = powers_of(powers_ref, fields)
    nearer = lax.broadcasted_iota(jnp.int32, (2 * height, LANES), 1) < LANES // 2
    for t in range(tiles):
        lanes, after, before = (
            slice(n % tiles * LANES, (n % tiles + 1) * LANES) for n in (t, t + 1, t - 1)
        )
        around = jnp.where(nearer, split_ref[:, after], split_ref[:, before])
        product = jnp.dot(
            jnp.concatenate([split_ref[:, lanes], around], axis=1),
            band_ref[2 * t * LANES : 2 * (t + 1) * LANES, :],
            preferred_element_type=jnp.float32,
        )
        moved = (
            product[height:, LANES:] + (product[:height, LANES:] + product[height:, :LANES])
        ) + product[:height, :LANES]
        for f in range(fields):
            value = sum(mix[f][g] * moved[g * members : (g + 1) * members] for g in range(fields))
            state[f * members : (f + 1) * members, lanes] = value
            if not own:
                put_pieces(1 - core, f, lanes, value)
            place = (f * tiles + t) * 8
            sums_ref[place : place + 8, :] = sum(value[8 * i : 8 * i + 8] for i in range(members // 8))


def pieces_of(x):
    high = x.astype(jnp.bfloat16).astype(jnp.float32)
    rest = x - high
    middle = rest.astype(jnp.bfloat16).astype(jnp.float32)
    return high, middle, rest - middle


def sums_kernel(
    powers_ref, small_ref, own_state, own_edge, own_sums, other_state, other_edge, other_sums,
    kept, odd, swapped, even, *refs, owners, units, fields,
):
    carried = refs[: len(units) - 1]
    (
        stay_ref, odd_ref, even_ref, edge_ref, halo_ref, onehot_ref, spread_ref, split_ref,
    ) = refs[len(units) - 1 :]
    states, raw_edges = (own_state, other_state), (own_edge, other_edge)
    block, core = here()
    members = states[0].shape[0] // fields
    cells = states[0].shape[1]
    tiles = cells // LANES
    total = 2 * members
    places = fields * tiles
    has_left = (block > 0).astype(jnp.float32)
    has_right = (block < owners - 1).astype(jnp.float32)
    sub = lax.broadcasted_iota(jnp.int32, (8, LANES), 0)
    lane = lax.broadcasted_iota(jnp.int32, (1, LANES), 1)
    lane8 = lax.broadcasted_iota(jnp.int32, (8, LANES), 1)
    half_lanes = LANES // 2
    low = lane < half_lanes

    strips = incoming(digit_of(block, units[-1]), core, odd, swapped)
    for unit, earlier in reversed(list(zip(units, carried))):
        digit = digit_of(block, unit)
        rows = [earlier[8 * p : 8 * p + 8, :] for p in range(3)]
        picked = []
        for p in range(3):
            from_right = jnp.where(digit != 3, rows[p], strips[p])
            from_left = jnp.where(digit != 0, rows[p], strips[p])
            picked.append(jnp.where(sub < STEPS if p < 2 else lane8 < half_lanes, from_right, from_left))
        strips = picked

    place_ids = lax.broadcasted_iota(jnp.int32, (places, LANES), 0)
    lane_ids = lax.broadcasted_iota(jnp.int32, (LANES, LANES), 0)
    held = kept.shape[0] // 8
    sources = [(kept, 8 * j) for j in range(held)]
    for source, base in ((odd, 16), (swapped, 16), (even, 16)):
        sources += [(source, base + 8 * j) for j in range(held)]
    hits = []
    for n, (source, at) in enumerate(sources):
        local = source[at : at + 1, :].astype(jnp.int32)
        hit = place_ids == lax.shift_right_arithmetic(local, 7)
        hits.append(hit)
        onehot = (lane_ids == jnp.bitwise_and(local, LANES - 1)).astype(jnp.float32)
        lanes = slice(n * LANES, (n + 1) * LANES)
        onehot_ref[:, lanes] = onehot.astype(jnp.bfloat16)
        weight, pull = source[at + 1 : at + 2, :], source[at + 2 : at + 3, :]
        stack = [jnp.where(hit, piece, 0.0) for piece in pieces_of(weight) + pieces_of(pull)]
        spread_ref[:, lanes] = jnp.concatenate(stack, axis=0).astype(jnp.bfloat16)
    placed = lax.dot_general(
        spread_ref[...], onehot_ref[...], (((1,), (1,)), ((), ())), preferred_element_type=jnp.float32
    )
    placed = [placed[p * places : (p + 1) * places] for p in range(6)]
    weight = placed[0] + placed[1] + placed[2]
    pull = placed[3] + placed[4] + placed[5]

    root = jnp.sqrt(weight)
    scale = jnp.where(weight > 0.0, lax.rsqrt(jnp.where(weight > 0.0, weight, 1.0)), 0.0)
    sub16 = lax.broadcasted_iota(jnp.int32, (16, LANES), 0)
    depth = total + 16
    means = {}

    def put(row, lanes, value):
        for p, piece in enumerate(halves_of(value)):
            split_ref[pl.ds(row + p * depth, value.shape[0]), lanes] = piece

    def put_tile(at, sums, halves, into):
        means[at] = jnp.sum(sums, axis=0, keepdims=True) * (1.0 / total)
        lanes = slice(into * LANES, (into + 1) * LANES)
        for half, value in enumerate(halves):
            side = core if half == 0 else 1 - core
            anomaly = (value - means[at]) * root[at : at + 1]
            put(pl.multiple_of(side * members, 16), lanes, anomaly)
        drawn = (pull[at : at + 1] - weight[at : at + 1] * means[at]) * scale[at : at + 1]
        put(total, lanes, jnp.where(sub16 == 0, drawn, 0.0))

    def product_of(first, last):
        lanes = slice(first * LANES, last * LANES)
        anomalies = jnp.concatenate([split_ref[:total, lanes], split_ref[depth : depth + total, lanes]], axis=0)
        return lax.dot_general(
            split_ref[:, lanes], anomalies, (((1,), (1,)), ((), ())), preferred_element_type=jnp.float32
        )

    inner = tiles - 2
    products = []
    for f in range(fields):
        rows = slice(f * members, (f + 1) * members)
        for t in range(1, tiles - 1):
            at = f * tiles + t
            lanes = slice(t * LANES, (t + 1) * LANES)
            sums = own_sums[8 * at : 8 * at + 8, :] + other_sums[8 * at : 8 * at + 8, :]
            put_tile(at, sums, [state[rows, lanes] for state in states], f * inner + t - 1)
        products.append(product_of(f * inner, (f + 1) * inner))

    right_first = half_lanes + 3 * STEPS
    strip_rows = fields * members
    for half in range(2):
        strip = strips[half]
        left = jnp.where(sub < STEPS, pltpu.roll(strip, STEPS, 0) * has_left, 0.0)
        at = right_first % 8
        right = jnp.where(
            (sub >= at) & (sub < at + STEPS), (pltpu.roll(strip, at, 0) if at else strip) * has_right, 0.0
        )
        gap = jnp.zeros((right_first - at - 8, LANES), jnp.float32)
        rest = jnp.zeros((LANES - (right_first - at) - 8, LANES), jnp.float32)
        halo_ref[half * strip_rows : (half + 1) * strip_rows, :] = jnp.transpose(
            jnp.concatenate([left, gap, right, rest], axis=0)
        )
    speed = small_ref[:tiles, :]
    toward_left = speed * small_ref[tiles : 2 * tiles, :]
    toward_right = speed - toward_left
    is_left = lane < STEPS
    is_right = (lane >= right_first) & (lane < right_first + STEPS)
    inside = jnp.where(is_left, has_left, jnp.where(is_right, has_right, 1.0))
    from_outside = (lane8 < STEPS) | ((lane8 >= right_first) & (lane8 < right_first + STEPS))

    def edge_row(rows, row):
        own = jnp.where(
            low, pltpu.roll(rows[:1], STEPS, 1), pltpu.roll(rows[tiles - 1 :], half_lanes + 3 * STEPS, 1)
        )
        left = pltpu.roll(strips[2][row : row + 1], STEPS, 1)
        right = pltpu.roll(strips[2][row : row + 1], right_first, 1)
        return jnp.where(is_left, left, jnp.where(is_right, right, own))

    edge_left = edge_row(toward_left, 3)
    edge_right = edge_row(toward_right, 4)
    from_left = jnp.broadcast_to((edge_left + DIFFUSION) * inside, (8, LANES))
    from_right = jnp.broadcast_to((edge_right + DIFFUSION) * inside, (8, LANES))
    stay = jnp.broadcast_to((1.0 - 2.0 * DIFFUSION - edge_left - edge_right) * inside, (8, LANES))
    mix = powers_of(powers_ref, fields)
    first_sums = [[jnp.zeros((8, LANES), jnp.float32)] * fields for _ in range(2)]
    last_sums = [[jnp.zeros((8, LANES), jnp.float32)] * fields for _ in range(2)]
    for half in range(2):
        state, edge = states[half], raw_edges[half]
        for i in range(members // 8):
            moved = []
            for f in range(fields):
                at = f * members + 8 * i
                x = edge[at : at + 8, :]
                x = jnp.where(from_outside, halo_ref[half * strip_rows + at : half * strip_rows + at + 8, :], x)
                moved.append(transport(x, from_left, stay, from_right))
            for f in range(fields):
                at = f * members + 8 * i
                value = sum(mix[f][g] * moved[g] for g in range(fields))
                first_tile = jnp.where(lane8 < STEPS, pltpu.roll(value, LANES - STEPS, 1), state[at : at + 8, :LANES])
                last_tile = jnp.where(
                    lane8 >= LANES - STEPS,
                    pltpu.roll(value, LANES - right_first, 1),
                    state[at : at + 8, cells - LANES :],
                )
                edge_ref[half * strip_rows + at : half * strip_rows + at + 8, :LANES] = first_tile
                edge_ref[half * strip_rows + at : half * strip_rows + at + 8, LANES:] = last_tile
                first_sums[half][f] = first_sums[half][f] + first_tile
                last_sums[half][f] = last_sums[half][f] + last_tile
    edge_at = fields * inner
    for f in range(fields):
        for n, (t, sums) in enumerate(((0, first_sums), (tiles - 1, last_sums))):
            column = slice(n * LANES, (n + 1) * LANES)
            halves = [
                edge_ref[half * strip_rows + f * members : half * strip_rows + (f + 1) * members, column]
                for half in range(2)
            ]
            put_tile(f * tiles + t, sums[0][f] + sums[1][f], halves, edge_at + 2 * f + n)
    products.append(product_of(edge_at, edge_at + 2 * fields))
    products = sum(products)
    mean = jnp.concatenate([means[at] for at in range(places)], axis=0)
    gram = products[: total + 8] + products[depth : depth + total + 8]
    gram = gram + pltpu.roll(gram, total, 1)
    in_low = lax.broadcasted_iota(jnp.int32, (members, LANES), 1) < total
    folded = jnp.where(in_low, gram[members:total], gram[:members])
    blank = jnp.zeros((stay_ref.shape[0] - members - 1, LANES), jnp.float32)
    for out in (stay_ref, odd_ref, even_ref):
        out[:members, :] = folded
        out[members : members + 1, :] = gram[total : total + 1]
        out[members + 1 :, :] = blank

    found = lax.dot_general(
        jnp.concatenate(pieces_of(mean), axis=0).astype(jnp.bfloat16), onehot_ref[...],
        (((1,), (0,)), ((), ())), preferred_element_type=jnp.float32,
    )
    found = found[:places] + found[places : 2 * places] + found[2 * places :]
    for out, source, partner in ((stay_ref, 0, 0), (odd_ref, 1, 1 + 2 * core), (even_ref, 3, 2)):
        for j in range(held):
            n = source * held + j
            center = jnp.sum(
                jnp.where(hits[n], found[:, n * LANES : (n + 1) * LANES], 0.0), axis=0, keepdims=True
            )
            out[pl.ds(members + 1 + partner * held + j, 1), :] = center


def spread_row(row):
    return jnp.broadcast_to(row, (8, LANES))


def eliminate(rows):
    count = len(rows)
    rows = list(rows)
    sub = lax.broadcasted_iota(jnp.int32, (8, LANES), 0)

    def columns_of(row, b):
        first = 8 * (count + b)
        return [jnp.broadcast_to(row[:, first + k : first + k + 1], (8, LANES)) for k in range(8)]

    upcoming = columns_of(rows[0], 0)
    for b in range(count):
        own = upcoming
        below = {i: columns_of(rows[i], b) for i in range(b + 1, count)}
        if b + 1 < count:
            upcoming = columns_of(rows[b + 1], b + 1)
        for j in range(8):
            scale = lax.rsqrt(spread_row(own[j][j : j + 1, :]))
            upper = spread_row(rows[b][j : j + 1, :]) * scale
            lower = own[j] * scale
            factors = {k: spread_row(own[j][k : k + 1, :]) * scale for k in range(j + 1, 8)}
            for k in range(j + 1, 8):
                own[k] = own[k] - lower * factors[k]
            rows[b] = jnp.where(sub == j, upper, rows[b] - jnp.where(sub > j, lower, 0.0) * upper)
            for i in range(b + 1, count):
                here = below[i][j] * scale
                if i == b + 1:
                    for k in range(8):
                        upcoming[k] = upcoming[k] - here * spread_row(here[k : k + 1, :])
                for k in range(j + 1, 8):
                    below[i][k] = below[i][k] - here * factors[k]
                rows[i] = rows[i] - here * upper
    return rows


def analysis_kernel(
    split_ref, edge_ref, small_ref, slots_ref, kept, odd, swapped, even,
    analysis_ref, innovation_ref, center_ref, pieces_ref, result_ref, departure_ref, sems, *, units, obs_rows, count,
):
    block, core = here()
    members, fields, cells = analysis_ref.shape
    total = 2 * members
    strip_rows = fields * members
    for f in range(fields):
        for half in range(2):
            rows = slice(half * strip_rows + f * members, half * strip_rows + (f + 1) * members)
            side = core if half == 0 else 1 - core
            for p, piece in enumerate(halves_of(edge_ref[rows, :])):
                at = pl.multiple_of((f * 2 + p) * total + side * members, 16)
                pieces_ref[pl.ds(at, members), :] = piece
    head = members + 1
    sums = (kept[:head, :] + even[:head, :]) + (odd[:head, :] + swapped[:head, :])
    returned = kept.shape[0] - head
    center_ref[:returned, :] = kept[head:, :]
    center_ref[returned : 2 * returned, :] = jnp.where(core == 0, odd[head:, :], swapped[head:, :])
    center_ref[2 * returned : 3 * returned, :] = even[head:, :]
    center_ref[3 * returned :, :] = jnp.where(core == 0, swapped[head:, :], odd[head:, :])
    lane = lax.broadcasted_iota(jnp.int32, (8, LANES), 1)
    sub = lax.broadcasted_iota(jnp.int32, (8, LANES), 0)
    shifted = pltpu.roll(sums[:members], total, 1)
    rows = []
    for b in range(total // 8):
        at = 8 * b
        source = sums[at : at + 8] if at < members else shifted[at - members : at - members + 8]
        own = jnp.where(lane == sub + at + total, total - 1.0, 0.0)
        unit = jnp.where(lane == sub + at, 1.0, 0.0)
        rows.append(jnp.where(lane >= total, source + own, unit))
    rows = eliminate(rows)
    cross = sums[members : members + 1]
    inverse = [jnp.where(lane < total, r, 0.0) for r in rows]
    carried = [jnp.sum(r * cross, axis=1, keepdims=True) for r in inverse]
    row_sums = [jnp.sum(r, axis=1, keepdims=True) for r in inverse]
    row_means = [r * (1.0 / total) for r in row_sums]
    weights = jnp.sum(sum(r * c for r, c in zip(inverse, carried)), axis=0, keepdims=True)
    column_mean = jnp.sum(sum(inverse), axis=0, keepdims=True) * (1.0 / total)
    grand = jnp.sum(sum(row_means), axis=0, keepdims=True) * (1.0 / total)
    weights = weights - jnp.sum(sum(r * c for r, c in zip(row_means, carried)), axis=0, keepdims=True)
    root = math.sqrt(total - 1.0)
    add = weights + 1.0 / total - root * (column_mean - grand)
    count_here = members // 8
    mixing = [
        root * jnp.where(core == 0, inverse[b] - row_means[b], inverse[b + count_here] - row_means[b + count_here]) + add
        for b in range(count_here)
    ]
    high, rest = halves_of(jnp.concatenate(mixing, axis=0)[:, :total])
    mixing = jnp.concatenate(
        [jnp.concatenate([high, high], axis=1), jnp.concatenate([rest, rest], axis=1)], axis=0
    )
    copies = []
    width = cells // 2
    for n in range(2):
        lanes = slice(n * width, (n + 1) * width)
        for f in range(fields):
            rows = slice(f * 2 * total, (f + 1) * 2 * total)
            if n == 0:
                states = [pieces_ref[rows, :LANES], split_ref[rows, LANES:width]]
            else:
                states = [split_ref[rows, width : cells - LANES], pieces_ref[rows, LANES:]]
            product = jnp.dot(mixing, jnp.concatenate(states, axis=1), preferred_element_type=jnp.float32)
            result_ref[:, f, lanes] = product[:members] + product[members:]
        copies.append(
            pltpu.make_async_copy(
                result_ref.at[:, :, pl.ds(n * width, width)],
                analysis_ref.at[:, :, pl.ds(n * width, width)],
                sems.at[n],
            )
        )
        copies[-1].start()

    held = count // 4
    lane_group = lane // CAP
    table = []
    for r in range(count):
        merged = jnp.zeros((1, LANES), jnp.float32)
        for group in range(GROUPS):
            owner = group * count + r
            way = [jnp.bitwise_xor(digit_of(block, unit), (owner // unit) % 4) for unit in units]
            row = way[-1] * held
            if len(units) > 2:
                row = row + sum(step * 4**n for n, step in enumerate(way[:-2]))
            size = 4 * held
            for step in reversed(way[1:-1]):
                row = row + step * size
                size = size * 4
            row = row + way[0] * returned
            line = center_ref[pl.ds(row, 1), :]
            moved = pltpu.roll(line, jnp.bitwise_and(group - way[-2], 3) * CAP, 1)
            merged = jnp.where(lane_group[:1] == group, moved, merged)
        table.append(jnp.broadcast_to(merged, (8, LANES)))
    for r in range(obs_rows):
        center = jnp.zeros((8, LANES), jnp.float32)
        lanes = jnp.broadcast_to(slots_ref[obs_rows + r : obs_rows + r + 1, :], (8, LANES))
        for n in range(count):
            found = jnp.take_along_axis(table[n], lanes, axis=1, mode="promise_in_bounds")
            center = jnp.where(slots_ref[r : r + 1, :] == n, found, center)
        center = center[:1]
        at = small_ref.shape[0] - 2 * obs_rows + r
        value, sigma = small_ref[at : at + 1, :], small_ref[at + obs_rows : at + obs_rows + 1, :]
        departure_ref[r : r + 1, :] = (value - center) / sigma
    copies.append(pltpu.make_async_copy(departure_ref, innovation_ref, sems.at[2]))
    copies[-1].start()
    for copy in copies:
        copy.wait()


def shards(
    ensemble, speed, direction, couple, obs_place, obs_field, obs_value, obs_sigma, send_count
):
    members, fields, cells = ensemble.shape
    owners = lax.axis_size("cells")
    total = members * lax.axis_size("members")
    obs = obs_place.shape[0]
    obs_rows = obs // LANES
    tiles = cells // LANES
    places = fields * tiles
    units = stage_units(owners)
    block = lax.axis_index("cells").astype(jnp.int32)
    core = lax.axis_index("members").astype(jnp.int32)
    small = (
        speed.reshape(tiles, LANES), direction.reshape(tiles, LANES),
        *(x.reshape(obs_rows, LANES) for x in (obs_place, obs_field, obs_value, obs_sigma)),
    )
    whole = pl.BlockSpec(memory_space=pltpu.VMEM)
    params = pltpu.CompilerParams(vmem_limit_bytes=VMEM_BYTES)
    real = jnp.float32

    table_rows = 8 * (owners // GROUPS)
    part = table_rows // 4
    other = swap_cores(ensemble, owners)
    rows_of = lambda count: pl.BlockSpec((count, LANES), lambda i: (0, 0))
    small_rows = 2 * tiles + 2 * obs_rows
    strips = pl.pallas_call(
        strips_kernel,
        out_shape=jax.ShapeDtypeStruct((8, LANES), real),
        in_specs=[whole],
        out_specs=whole,
        compiler_params=params,
        name="strips",
    )(ensemble)
    kept, to_odd, to_even, small = pl.pallas_call(
        functools.partial(pack_kernel, rows=obs_rows, cells=cells, fields=fields),
        out_shape=(jax.ShapeDtypeStruct((part, LANES), real),) * 3
        + (jax.ShapeDtypeStruct((small_rows, LANES), real),),
        grid=(1,),
        in_specs=[whole] + [rows_of(x.shape[0]) for x in small],
        out_specs=(whole,) * 4,
        scratch_shapes=[pltpu.VMEM((table_rows, LANES), real)],
        compiler_params=params,
        name="pack",
    )(send_count, *small)
    to_odd, to_even = pl.pallas_call(
        join_kernel,
        out_shape=(jax.ShapeDtypeStruct((16 + part, LANES), real),) * 2,
        in_specs=[whole] * 4,
        out_specs=(whole,) * 2,
        compiler_params=params,
        name="join",
    )(strips, other, to_odd, to_even)

    strip_rows = fields * members
    band = jax.ShapeDtypeStruct((2 * cells, 2 * LANES), jnp.bfloat16)

    powers = jax.ShapeDtypeStruct((fields * fields, LANES), real)
    slots = jax.ShapeDtypeStruct((2 * obs_rows, LANES), jnp.int32)

    pieces = jax.ShapeDtypeStruct((fields * 2 * total, cells), jnp.bfloat16)

    def forecast(operands, extra, own):
        states = jax.ShapeDtypeStruct((strip_rows, cells), real)
        edges = () if own else (jax.ShapeDtypeStruct((strip_rows, LANES), real),)
        outs = (states,) + edges + (jax.ShapeDtypeStruct((places * 8, LANES), real),) + extra
        return pl.pallas_call(
            functools.partial(forecast_kernel, fields=fields, own=own),
            out_shape=outs,
            in_specs=[whole] * len(operands),
            out_specs=(whole,) * len(outs),
            scratch_shapes=[]
            if own
            else [pltpu.VMEM((2 * strip_rows, cells), jnp.bfloat16), pltpu.VMEM((strip_rows, cells), real)],
            compiler_params=params,
            cost_estimate=pl.CostEstimate(
                flops=80 * strip_rows * cells, bytes_accessed=8 * strip_rows * cells, transcendentals=0
            ),
            name="forecast",
        )(*operands)

    split_shape = jax.ShapeDtypeStruct((2 * strip_rows, cells), jnp.bfloat16)
    edge_shape = jax.ShapeDtypeStruct((strip_rows, LANES), real)
    rule, mixed, slots_of, own_split, own_edge = pl.pallas_call(
        functools.partial(rule_kernel, tiles=tiles),
        out_shape=(band, powers, slots, split_shape, edge_shape),
        in_specs=[whole] * 4,
        out_specs=(whole,) * 5,
        scratch_shapes=[pltpu.VMEM((strip_rows, cells), real)],
        compiler_params=params,
        cost_estimate=pl.CostEstimate(
            flops=40 * strip_rows * cells, bytes_accessed=4 * strip_rows * cells, transcendentals=0
        ),
        name="rule",
    )(couple, small, send_count, ensemble)
    own_state, own_sums = forecast((mixed, own_split, rule), (), True)
    own_forecast = (own_state, own_edge, own_sums)
    carried = []
    for n, unit in enumerate(units):
        arrived = exchange(to_odd, to_even, owners, unit)
        if n + 1 < len(units):
            to_odd, to_even, kept = pl.pallas_call(
                functools.partial(regroup_kernel, unit=unit, into_lanes=n + 2 == len(units)),
                out_shape=tuple(jax.ShapeDtypeStruct(x.shape, real) for x in (to_odd, to_even, kept)),
                in_specs=[whole] * 4 + [pl.BlockSpec(memory_space=pl.ANY)],
                out_specs=(whole,) * 3,
                compiler_params=params,
                name="regroup",
            )(kept, *arrived, mixed)
            carried.append(to_odd)
    *other_forecast, split = forecast((mixed, other, rule, own_forecast[0]), (pieces,), False)

    held = kept.shape[0] // 8
    sums_rows = -(-(members + 1 + 4 * held) // 8) * 8
    all_slots = 4 * held * LANES
    sums = jax.ShapeDtypeStruct((sums_rows, LANES), real)
    stay, to_odd, to_even, edges = pl.pallas_call(
        functools.partial(sums_kernel, owners=owners, units=units, fields=fields),
        out_shape=(sums, sums, sums, jax.ShapeDtypeStruct((2 * strip_rows, 2 * LANES), real)),
        in_specs=[whole] * (12 + len(carried)),
        out_specs=(whole,) * 4,
        scratch_shapes=[
            pltpu.VMEM((2 * strip_rows, LANES), real),
            pltpu.VMEM((LANES, all_slots), jnp.bfloat16),
            pltpu.VMEM((6 * places, all_slots), jnp.bfloat16),
            pltpu.VMEM((2 * (total + 16), fields * cells), jnp.bfloat16),
        ],
        compiler_params=params,
        name="sums",
    )(
        mixed, small, *own_forecast, *other_forecast, kept, *arrived, *carried,
    )

    head = members + 1
    used = head + 4 * held
    for n, unit in enumerate(reversed(units)):
        odd, swapped, even = exchange(to_odd, to_even, owners, unit)
        if n + 1 < len(units):
            added = (stay + even) + (odd + swapped)
            if n > 0:
                first = jnp.where(core == 0, odd, swapped)
                third = jnp.where(core == 0, swapped, odd)
                added = jnp.concatenate(
                    [added[:head]] + [x[head:used] for x in (stay, first, even, third)], axis=0
                )
                used = added.shape[0]
            stay = to_odd = to_even = added

    analysis, innovation = pl.pallas_call(
        functools.partial(analysis_kernel, units=units, obs_rows=obs_rows, count=owners // GROUPS),
        out_shape=(
            jax.ShapeDtypeStruct((members, fields, cells), real),
            jax.ShapeDtypeStruct((obs_rows, LANES), real),
        ),
        in_specs=[whole] * 8,
        out_specs=(pl.BlockSpec(memory_space=pl.ANY),) * 2,
        scratch_shapes=[
            pltpu.VMEM((4 * (stay.shape[0] - head), LANES), real),
            pltpu.VMEM((fields * 2 * total, 2 * LANES), jnp.bfloat16),
            pltpu.VMEM((members, fields, cells), real),
            pltpu.VMEM((obs_rows, LANES), real),
            pltpu.SemaphoreType.DMA((3,)),
        ],
        compiler_params=params,
        name="analysis",
    )(
        split, edges, small, slots_of,
        stay, odd, swapped, even,
    )
    return (analysis, innovation.reshape(obs))


def solution(mesh):
    return jax.shard_map(
        shards,
        mesh=mesh,
        in_specs=(
            P("members", None, "cells"),
            P("cells"),
            P("cells"),
            P(),
            P("cells"),
            P("cells"),
            P("cells"),
            P("cells"),
            P("cells", None),
        ),
        out_specs=(P("members", None, "cells"), P("cells")),
        check_vma=False,
    )
```
